512 devices in a mesh: grp: 16 (over x, y_lo), blk: 32 (over y_hi, z, core).
Axes of the slice: x: 4, y: 8 (y_hi: 2, y_lo: 4; y = y_hi * 4 + y_lo), z: 8, core: 2. Of those that a mesh axis runs over, the one named last changes fastest.
Arguments:
- image_emb: bfloat16 [131072, 1152], P(('grp', 'blk')), may hold values from -0.1796875 to 0.1796875
- text_emb: bfloat16 [131072, 1152], P(('grp', 'blk')), may hold values from -0.1796875 to 0.1796875
- image_pair_index: int32 [131072], P(('grp', 'blk')), may hold values from 0 to 1023
- text_ids: int32 [131072], P(('grp', 'blk')), may hold values from 0 to 1023
- exponent_sharpness: float32 [1], replicated, may hold values from 1.5 to 2.5
- additive_offset: float32 [1], replicated, may hold values from -3 to -1
- objective_adjoint: float32 [1], replicated, may hold values from 64 to 256
Outputs:
- grad_image: float32 [131072, 1152], P(('grp', 'blk'))
- grad_text: float32 [131072, 1152], P(('grp', 'blk'))
The draws below stay inside these ranges and needn't reach their ends.
All inputs are finite; a program needn't handle non-finite values.
Results may differ from the reference program's by a relative error of at most 0.0044.
Values may be sent and summed in bfloat16 or wider, within the bound.
A program may use at most 64 MiB of HBM per device.

```python
import math
import jax
import jax.numpy as jnp
from jax import lax

D = 1152
MATCHES_ON_CHIP = 256
SPAN = 4
HOPS = 2
IDS = 1024
ROWS = 131072
N_GRP = 16
N_BLK = 32


def plant(result, key, low, largest):
    extent = result.shape
    index_at = [jax.random.randint(jax.random.fold_in(key, axis), (), 0, extent[axis]) for axis in range(len(extent))]
    result = result.at[tuple(index_at)].set(low)
    longest = extent.index(max(extent))
    index_at[longest] = (index_at[longest] + 1) % extent[longest]
    return result.at[tuple(index_at)].set(largest)


def block_scale(own_key, dims, pieces, least, largest):
    def one(position, blocks):
        draws = jax.random.uniform(jax.random.fold_in(jax.random.fold_in(own_key, 6), position), (blocks,), jnp.float32, least / len(pieces), largest / len(pieces))
        return jnp.repeat(jnp.exp(draws), dims[position] // blocks).reshape((-1,) + (1,) * (len(dims) - position - 1))

    factor_of = one(*pieces[0])
    for cut in pieces[1:]:
        factor_of = factor_of * one(*cut)
    return factor_of


def gaussian(own_key, dims, spread, limit, pieces=(), dtype=jnp.bfloat16):
    drawn = spread * jax.random.normal(own_key, dims, jnp.float32)
    if pieces:
        drawn = drawn * block_scale(own_key, dims, pieces, -0.22, 0.18)
    return jnp.clip(drawn, -limit, limit).astype(dtype)


def setup_inputs(seed: int = 0) -> dict:
    splits = jax.random.split(jax.random.key(seed), 8)
    image_emb = gaussian(splits[0], (ROWS, D), 0.03, 0.1796875, ((0, 512),))
    text_emb = gaussian(splits[1], (ROWS, D), 0.03, 0.1796875, ((0, 512),))
    image_pair_index = plant(jax.random.randint(splits[2], (ROWS,), 0, IDS), jax.random.fold_in(splits[2], 1), 0, IDS - 1).astype(jnp.int32)
    text_ids = plant(jax.random.randint(splits[3], (ROWS,), 0, IDS), jax.random.fold_in(splits[3], 1), 0, IDS - 1).astype(jnp.int32)
    exponent_sharpness = jnp.clip(jax.random.uniform(splits[4], (1,), jnp.float32, 1.5, 2.5), 1.5, 2.5)
    additive_offset = jnp.clip(jax.random.uniform(splits[5], (1,), jnp.float32, -3.0, -1.0), -3.0, -1.0)
    objective_adjoint = jnp.clip(jnp.exp(jax.random.uniform(splits[6], (1,), jnp.float32, math.log(64.0), math.log(256.0))), 64.0, 256.0)
    return dict(image_emb=image_emb, text_emb=text_emb, image_pair_index=image_pair_index, text_ids=text_ids, exponent_sharpness=exponent_sharpness, additive_offset=additive_offset, objective_adjoint=objective_adjoint)


EPSILON = 1e-06

def normalize(rows):
    wide = rows.astype(jnp.float32)
    inverse = lax.rsqrt(lax.optimization_barrier(jnp.sum(wide * wide, axis=-1, keepdims=True)) + EPSILON)
    unit = wide * inverse
    rounded = lax.optimization_barrier(unit.astype(jnp.bfloat16)).astype(jnp.float32)
    return (inverse, unit, rounded)

def finish(inverse, unit, grad_unit):
    return inverse * (grad_unit - unit * lax.optimization_barrier(jnp.sum(unit * grad_unit, axis=-1, keepdims=True)))

def reference(image_emb, text_emb, image_pair_index, text_ids, exponent_sharpness, additive_offset, objective_adjoint):
    groups = N_GRP
    blocks = N_BLK
    shape = (groups, blocks, MATCHES_ON_CHIP, D)
    inv_image, unit_image, normalized_image = normalize(image_emb.reshape(shape))
    inv_text, unit_text, text_hat = normalize(text_emb.reshape(shape))
    img_label = image_pair_index.reshape(groups, blocks, MATCHES_ON_CHIP)
    txt_label = text_ids.reshape(groups, blocks, MATCHES_ON_CHIP)
    sharpness_factor = jnp.exp(exponent_sharpness[0])
    weighting_factor = -(objective_adjoint[0] * sharpness_factor / MATCHES_ON_CHIP)
    hi = lax.Precision.HIGHEST
    d_image = jnp.zeros(shape, jnp.float32)
    d_text = jnp.zeros(shape, jnp.float32)
    for hop_index in range(HOPS):
        for cycle_index in range(SPAN):
            offset = (SPAN - 1) * hop_index + cycle_index
            incoming_visitor = jnp.roll(text_hat, (hop_index, offset), axis=(0, 1))
            visual_label = jnp.roll(txt_label, (hop_index, offset), axis=(0, 1))
            embedding_inner_grid = jnp.einsum('gkid,gkjd->gkij', normalized_image, incoming_visitor, precision=hi)
            match_score = sharpness_factor * embedding_inner_grid + additive_offset[0]
            sign = jnp.where(img_label[..., :, None] == visual_label[..., None, :], 1.0, -1.0).astype(jnp.float32)
            coef = weighting_factor * sign * jax.nn.sigmoid(-sign * match_score)
            coef = lax.optimization_barrier(coef.astype(jnp.bfloat16)).astype(jnp.float32)
            d_image = d_image + jnp.einsum('gkij,gkjd->gkid', coef, incoming_visitor, precision=hi)
            term = jnp.einsum('gkij,gkid->gkjd', coef, normalized_image, precision=hi)
            d_text = d_text + jnp.roll(term, (-hop_index, -offset), axis=(0, 1))
    grad_image = finish(inv_image, unit_image, d_image).reshape(ROWS, D)
    grad_text = finish(inv_text, unit_text, d_text).reshape(ROWS, D)
    return (grad_image, grad_text)
```

```python
import functools

import jax
import jax.numpy as jnp
from jax import lax
from jax.experimental import pallas as pl
from jax.experimental.pallas import tpu as pltpu
from jax.sharding import PartitionSpec as P

MESH = pl.DeviceIdType.MESH
EPSILON = 1e-06

SPAN = 4
SLOTS = 8
RUN = 16
CHUNKS = 4
LATE = 4


def kernel(
    n_grp,
    n_blk,
    image_hbm,
    text_hbm,
    image_ids,
    text_ids,
    sharpness,
    offset,
    adjoint,
    grad_image,
    grad_text,
    raw,
    buf,
    ids,
    own_ids,
    inverse,
    total,
    load_sem,
    send_sem,
    id_send_sem,
    wrap_sem,
    wrap_id_sem,
    recv_sem,
    id_recv_sem,
):
    rows = buf.shape[2]
    piece = rows // CHUNKS
    g = lax.axis_index("grp")
    k = lax.axis_index("blk")
    j = lax.rem(k, RUN)

    loads = [
        pltpu.make_async_copy(text_hbm, raw.at[0], load_sem.at[0]),
        pltpu.make_async_copy(image_hbm, raw.at[1], load_sem.at[1]),
    ]
    for load in loads:
        load.start()

    def device(dg, dk):
        return (lax.rem(g + dg + n_grp, n_grp), lax.rem(k + dk + n_blk, n_blk))

    barrier = pltpu.get_barrier_semaphore()

    def greet(target):
        pl.semaphore_signal(barrier, inc=1, device_id=target, device_id_type=MESH)

    for target in (device(0, 1), device(0, -1), device(1, 0), device(-1, 0)):
        greet(target)

    @pl.when(j == 0)
    def _():
        for back in range(2, 7):
            greet(device(0 if back < 4 else -1, -back))

    @pl.when(j == RUN - 1)
    def _():
        for ahead in range(2, 7):
            greet(device(0 if ahead < 4 else 1, ahead))

    def wrap_distance(stream):
        to_edge = RUN - j if stream == 0 else j + 1
        return to_edge, (to_edge >= 2) & (to_edge <= 6)

    for stream in range(2):
        loads[stream].wait()
        for c in range(CHUNKS):
            part = pl.ds(c * piece, piece)
            wide = raw[stream, part, :].astype(jnp.float32)
            inv = lax.rsqrt(jnp.sum(wide * wide, axis=-1, keepdims=True) + EPSILON)
            inverse[stream, part, :] = jnp.broadcast_to(inv, (piece, 128))
            buf[stream, 0, part, :] = (wide * inv).astype(jnp.bfloat16)
    ids[0, 0] = text_ids[...].astype(jnp.float32)
    ids[1, 0] = image_ids[...].astype(jnp.float32)

    far_sends = sum(wrap_distance(stream)[1].astype(jnp.int32) for stream in range(2))
    pl.semaphore_wait(barrier, 4 + far_sends)

    def route(stream, s):
        step = 1 - 2 * stream
        hop = s == SPAN - 1
        zero = jnp.int32(0)
        target = device(jnp.where(hop, step, zero), jnp.where(hop, zero, step))
        edge = j == jnp.where(stream == 0, RUN - 1, 0)
        goes = (s < SLOTS - 1) & (jnp.logical_not(edge) | (s == 0) | hop)
        return target, goes

    def block_copy(stream, s, c, target):
        part = pl.ds(c * piece, piece)
        return pltpu.make_async_remote_copy(
            src_ref=buf.at[stream, s, part],
            dst_ref=buf.at[stream, s + 1, part],
            send_sem=send_sem.at[stream, s],
            recv_sem=recv_sem.at[stream, s + 1, c],
            device_id=target,
            device_id_type=MESH,
        )

    def id_copy(stream, s, target):
        return pltpu.make_async_remote_copy(
            src_ref=ids.at[stream, s],
            dst_ref=ids.at[stream, s + 1],
            send_sem=id_send_sem.at[stream, s],
            recv_sem=id_recv_sem.at[stream, s + 1],
            device_id=target,
            device_id_type=MESH,
        )

    def forward(stream, s, c):
        target, goes = route(stream, s)

        @pl.when(goes)
        def _():
            if c is None:
                id_copy(stream, s, target).start()
            else:
                block_copy(stream, s, c, target).start()

    def receive(stream, s, c):
        target, _ = route(stream, s)
        if c is None:
            id_copy(stream, s - 1, target).wait_recv()
        else:
            block_copy(stream, s - 1, c, target).wait_recv()

    def wrap_copies(stream):
        to_edge, far = wrap_distance(stream)
        same = to_edge < SPAN
        slot = jnp.where(same, to_edge, to_edge + 1)
        step = 1 - 2 * stream
        target = device(jnp.where(same, 0, step), step * to_edge)
        copies = [
            pltpu.make_async_remote_copy(
                src_ref=ids.at[stream, 0],
                dst_ref=ids.at[stream, slot],
                send_sem=wrap_id_sem.at[stream],
                recv_sem=id_recv_sem.at[stream, slot],
                device_id=target,
                device_id_type=MESH,
            )
        ]
        for c in range(CHUNKS):
            part = pl.ds(c * piece, piece)
            copies.append(
                pltpu.make_async_remote_copy(
                    src_ref=buf.at[stream, 0, part],
                    dst_ref=buf.at[stream, slot, part],
                    send_sem=wrap_sem.at[stream],
                    recv_sem=recv_sem.at[stream, slot, c],
                    device_id=target,
                    device_id_type=MESH,
                )
            )
        whole = pltpu.make_async_remote_copy(
            src_ref=buf.at[stream, 0],
            dst_ref=buf.at[stream, slot],
            send_sem=wrap_sem.at[stream],
            recv_sem=recv_sem.at[stream, slot, 0],
            device_id=target,
            device_id_type=MESH,
        )
        return far, copies, whole

    for c in (None, *range(CHUNKS)):
        for stream in range(2):
            forward(stream, 0, c)
    for stream in range(2):
        far, copies, _ = wrap_copies(stream)

        @pl.when(far)
        def _():
            for copy in copies:
                copy.start()

    scale = jnp.exp(jnp.full((1, 128), sharpness[0], jnp.float32))[:, :1]
    shift = offset[0]
    weight = -(adjoint[0] * scale / rows)

    row = lax.broadcasted_iota(jnp.int32, (128, 128), 0)
    lane = lax.broadcasted_iota(jnp.int32, (128, 128), 1)
    for stream in range(2):
        for half in range(rows // 128):
            line = jnp.broadcast_to(ids[stream, 0, half : half + 1, :], (128, 128))
            column = jnp.sum(jnp.where(row == lane, line, 0.0), axis=-1, keepdims=True)
            own_ids[stream, pl.ds(half * 128, 128), :] = jnp.broadcast_to(column, (128, 128))

    def compute(stream, s, first=False):
        mine = 1 - stream
        visitor = buf[stream, s]
        grid = lax.dot_general(
            buf[mine, 0], visitor, (((1,), (1,)), ((), ())), preferred_element_type=jnp.float32
        )
        logit = scale * grid + shift
        column = own_ids[mine, :, :]
        parts = []
        for half in range(rows // 128):
            line = ids[stream, s, half : half + 1, :]
            match = column == jnp.broadcast_to(line, (rows, 128))
            here = logit[:, half * 128 : (half + 1) * 128]
            signed = jnp.where(match, here, -here)
            parts.append(jnp.where(match, weight, -weight) * (1.0 / (1.0 + jnp.exp(signed))))
        coef = jnp.concatenate(parts, axis=1).astype(jnp.bfloat16)
        term = jnp.dot(coef, visitor, preferred_element_type=jnp.float32)
        if first:
            total[mine] = term
        else:
            total[mine] += term

    for stream in range(2):
        compute(stream, 0, first=True)

    low = j < RUN // 2
    lead = jnp.where(low, 1, 0)
    lag = 1 - lead
    near = jnp.where(low, j, RUN - 1 - j)

    def late(s):
        return near < jnp.where(s < SPAN, s, s - 1)

    def step(t, carry):
        in_time = t < SLOTS
        lag_now = in_time & jnp.logical_not(late(t))
        old = t - LATE
        lag_old = (old >= 1) & late(old)

        for c in (None, *range(CHUNKS)):

            @pl.when(in_time)
            def _():
                receive(lead, t, c)
                forward(lead, t, c)

            @pl.when(lag_now)
            def _():
                receive(lag, t, c)
                forward(lag, t, c)

        @pl.when(in_time)
        def _():
            compute(lead, t)

        @pl.when(lag_now)
        def _():
            compute(lag, t)

        @pl.when(lag_old)
        def _():
            for c in (None, *range(CHUNKS)):
                receive(lag, old, c)
                forward(lag, old, c)
            compute(lag, old)

        return carry

    lax.fori_loop(1, SLOTS + LATE, step, 0)

    for stream, out in ((1, grad_image), (0, grad_text)):
        for c in range(CHUNKS):
            part = pl.ds(c * piece, piece)
            inv = inverse[stream, part, :][:, :1]
            unit = raw[stream, part, :].astype(jnp.float32) * inv
            grad = total[stream, part, :]
            along = jnp.sum(unit * grad, axis=-1, keepdims=True)
            out[part, :] = inv * (grad - unit * along)

    for stream in range(2):
        for s in range(SLOTS - 1):
            target, goes = route(stream, s)

            @pl.when(goes)
            def _():
                id_copy(stream, s, target).wait_send()
                pltpu.make_async_remote_copy(
                    src_ref=buf.at[stream, s],
                    dst_ref=buf.at[stream, s + 1],
                    send_sem=send_sem.at[stream, s],
                    recv_sem=recv_sem.at[stream, s + 1, 0],
                    device_id=target,
                    device_id_type=MESH,
                ).wait_send()

        far, copies, whole = wrap_copies(stream)

        @pl.when(far)
        def _():
            copies[0].wait_send()
            whole.wait_send()


def body(n_grp, n_blk, image_emb, text_emb, image_pair_index, text_ids, sharpness, offset, adjoint):
    rows, width = image_emb.shape
    vmem = pl.BlockSpec(memory_space=pltpu.VMEM)
    smem = pl.BlockSpec(memory_space=pltpu.SMEM)
    hbm = pl.BlockSpec(memory_space=pl.ANY)
    flops = 4 * SLOTS * 2 * rows * rows * width
    return pl.pallas_call(
        functools.partial(kernel, n_grp, n_blk),
        out_shape=(
            jax.ShapeDtypeStruct((rows, width), jnp.float32),
            jax.ShapeDtypeStruct((rows, width), jnp.float32),
        ),
        in_specs=[hbm, hbm, vmem, vmem, smem, smem, smem],
        out_specs=(vmem, vmem),
        scratch_shapes=[
            pltpu.VMEM((2, rows, width), jnp.bfloat16),
            pltpu.VMEM((2, SLOTS, rows, width), jnp.bfloat16),
            pltpu.VMEM((2, SLOTS, rows // 128, 128), jnp.float32),
            pltpu.VMEM((2, rows, 128), jnp.float32),
            pltpu.VMEM((2, rows, 128), jnp.float32),
            pltpu.VMEM((2, rows, width), jnp.float32),
            pltpu.SemaphoreType.DMA((2,)),
            pltpu.SemaphoreType.DMA((2, SLOTS)),
            pltpu.SemaphoreType.DMA((2, SLOTS)),
            pltpu.SemaphoreType.DMA((2,)),
            pltpu.SemaphoreType.DMA((2,)),
            pltpu.SemaphoreType.DMA((2, SLOTS, CHUNKS)),
            pltpu.SemaphoreType.DMA((2, SLOTS)),
        ],
        compiler_params=pltpu.CompilerParams(
            collective_id=0, has_side_effects=True, vmem_limit_bytes=40 * 1024 * 1024
        ),
        cost_estimate=pl.CostEstimate(
            flops=flops, bytes_accessed=12 * rows * width, transcendentals=2 * SLOTS * rows * rows
        ),
    )(
        image_emb,
        text_emb,
        image_pair_index.reshape(rows // 128, 128),
        text_ids.reshape(rows // 128, 128),
        sharpness,
        offset,
        adjoint,
    )


def solution(mesh):
    both = ("grp", "blk")
    return jax.shard_map(
        functools.partial(body, mesh.shape["grp"], mesh.shape["blk"]),
        mesh=mesh,
        in_specs=(P(both, None), P(both, None), P(both), P(both), P(), P(), P()),
        out_specs=(P(both, None), P(both, None)),
        check_vma=False,
    )
```

```python
import functools

import jax
import jax.numpy as jnp
from jax import lax
from jax.experimental import pallas as pl
from jax.experimental.pallas import tpu as pltpu
from jax.sharding import PartitionSpec as P

MESH = pl.DeviceIdType.MESH
EPSILON = 1e-06

SPAN = 4
SLOTS = 8
RUN = 16
WAVES = 4
DETOUR = 5


ORDER = (
    (
        10381668, 2261260, 16777260, 150994944, 3491608, 62167621, 184549376, 2793870, 83886126, 218103808,
        4020058, 129938119, 251658240, 33554448, 8219678, 12942865, 72074873, 100663296, 183979163, 201326645,
        134475411, 15728051, 234881079, 268435456,
    ),
    (
        1859908, 19958308, 6408805, 50332489, 87599782, 6679271, 121816011, 150994944, 33554452, 184550509,
        218106778, 251661300, 16080658, 5201819, 167972856, 7841209, 100663345, 67108864, 8335094, 201329911,
        234881024, 268435479, 134217728, 0,
    ),
    (
        10381668, 1475076, 150997769, 196514438, 11059911, 16777262, 218103808, 251775979, 50331661, 83947128,
        13694842, 117440571, 7963952, 183702901, 33555481, 209675709, 234979250, 281915383, 67108881,
        100663314, 134219475, 0, 0, 0,
    ),
    (
        1859908, 19958308, 53779045, 95052682, 117441483, 164809447, 184552813, 218107310, 251886639, 6549372,
        182713436, 201330265, 37832562, 234882746, 268508915, 5105362, 67108885, 100663318, 134219735, 0, 0,
        0, 0, 0,
    ),
    (
        10381668, 162562344, 196383081, 12100010, 218103856, 254573547, 16777228, 50334797, 83887032,
        117440527, 13610169, 172183355, 16588733, 201544860, 241394909, 268519351, 33554432, 73754581,
        100664983, 134217755, 0, 0, 0, 0,
    ),
    (
        1593636, 10902023, 16933640, 60609130, 95478443, 150994944, 129450955, 184549376, 218106805,
        251661743, 14909308, 168008766, 15725882, 201329749, 239543318, 268645527, 33653980, 67229337,
        100665243, 134217759, 0, 0, 0, 0,
    ),
    (
        10381668, 162693636, 196514373, 11207302, 218103854, 3347143, 16780267, 266398861, 50331663, 83889779,
        117440512, 15418448, 167772220, 201579858, 15723923, 234884568, 268435519, 7161497, 40990101,
        67108893, 100663326, 134217759, 0, 0,
    ),
    (
        1859908, 3181092, 16779877, 61498185, 10281616, 83886123, 11596497, 117440564, 150994962, 184552813,
        218103854, 251659503, 14386480, 13196409, 14658774, 7720663, 33654750, 167773820, 67110589, 201326654,
        100667355, 234881024, 134217728, 268435456,
    ),
    (
        10115336, 1347879, 151038760, 187619910, 3318256, 16777262, 218103857, 55769805, 251658240, 83952974,
        117440527, 4672662, 13471063, 5057945, 15842778, 182714301, 33558108, 201330333, 67112670, 234881024,
        100663327, 268435456, 134217728, 0,
    ),
    (
        1859908, 19040524, 10900493, 50331657, 4630926, 83886090, 4897231, 117440523, 150994988, 184549421,
        218203374, 251658287, 7013657, 13219185, 33554460, 67200883, 100665239, 134219768, 15683257,
        183729589, 201326653, 234881086, 268435519, 0,
    ),
    (
        10381668, 1475076, 150997769, 196387241, 230207978, 29180715, 251658240, 50333005, 83887502,
        117441999, 7964508, 33554448, 13739993, 67181915, 113585206, 134298807, 168021555, 201580217,
        234885051, 268435519, 0, 0, 0, 0,
    ),
    (
        1859908, 19958308, 53779045, 3713702, 83886096, 3980007, 117440556, 150994989, 184738904, 218103855,
        251658265, 5093010, 33555740, 8252445, 72822577, 100757363, 134221719, 167775796, 216494069,
        234884791, 268435515, 0, 0, 0,
    ),
    (
        10381668, 162693636, 196514373, 230335110, 254573547, 16778508, 50333005, 83887502, 117440527,
        7698192, 15960030, 33555985, 67110521, 7013565, 100663354, 147277019, 167772160, 16465650, 201326645,
        234881078, 268439543, 0, 0, 0,
    ),
    (
        1859908, 3181092, 16779877, 53913993, 3713767, 83886124, 150994944, 117505803, 184549421, 218106776,
        264230553, 13743124, 4677560, 33555804, 81524601, 167970194, 100663326, 5076983, 134217786, 201326641,
        234881074, 268439283, 0, 0,
    ),
    (
        10381668, 162693636, 10977861, 184553261, 230335110, 11506375, 251662255, 16777228, 167775536,
        50331661, 83947185, 117441492, 15686812, 6379421, 49612787, 4679065, 201326618, 234881024, 6289106,
        67108883, 100663351, 134217728, 268435456, 0,
    ),
    (
        1859908, 151177764, 16777992, 14851365, 184552316, 50332489, 218294950, 83886986, 15383911, 251661309,
        117441483, 167772208, 16584126, 4683313, 201328249, 234884252, 33558228, 72689309, 268438750,
        105756063, 134217751, 0, 0, 0,
    ),
)


def kernel(
    n_grp,
    n_blk,
    image_hbm,
    text_hbm,
    image_ids,
    text_ids,
    sharpness,
    offset,
    adjoint,
    grad_image,
    grad_text,
    raw,
    hat,
    buf,
    ids,
    own_ids,
    inverse,
    total,
    load_sem,
    send_sem,
    id_send_sem,
    wrap_sem,
    wrap_id_sem,
    detour_sem,
    recv_sem,
    id_recv_sem,
):
    rows = hat.shape[1]
    piece = rows // WAVES
    g = lax.axis_index("grp")
    k = lax.axis_index("blk")
    j = lax.rem(k, RUN)

    loads = [
        pltpu.make_async_copy(text_hbm, raw.at[0], load_sem.at[0]),
        pltpu.make_async_copy(image_hbm, raw.at[1], load_sem.at[1]),
    ]
    for load in loads:
        load.start()

    def device(dg, dk):
        return (lax.rem(g + dg + n_grp, n_grp), lax.rem(k + dk + n_blk, n_blk))

    next_grp = [device(step, 0)[0] for step in (1, -1)]
    next_blk = [device(0, step)[1] for step in (1, -1)]

    barrier = pltpu.get_barrier_semaphore()

    def greet(target):
        pl.semaphore_signal(barrier, inc=1, device_id=target, device_id_type=MESH)

    for target in (device(0, 1), device(0, -1), device(1, 0), device(-1, 0)):
        greet(target)

    even = lax.rem(j, 2) == 0

    @pl.when(even & (j >= 2))
    def _():
        greet(device(0, -2))

    @pl.when(jnp.logical_not(even) & (j <= RUN - 3))
    def _():
        greet(device(0, 2))

    @pl.when(j == 0)
    def _():
        for back in range(2, 7):
            greet(device(0 if back < 4 else -1, -back))
        greet(device(-1, -2))

    @pl.when(j == RUN - 1)
    def _():
        for ahead in range(2, 7):
            greet(device(0 if ahead < 4 else 1, ahead))
        greet(device(1, 2))

    def wrap_distance(stream):
        to_edge = RUN - j if stream == 0 else j + 1
        return to_edge, (to_edge >= 2) & (to_edge <= 6)

    words = []
    for i in range(len(ORDER[0])):
        word = jnp.int32(ORDER[0][i])
        for place in range(1, RUN):
            if ORDER[place][i] != ORDER[place - 1][i]:
                word = jnp.where(j >= place, ORDER[place][i], word)
        words.append(word)

    for stream, own in ((0, text_ids), (1, image_ids)):
        loads[stream].wait()
        for c in range(WAVES):
            part = pl.ds(c * piece, piece)
            wide = raw[stream, part, :].astype(jnp.float32)
            inv = lax.rsqrt(jnp.sum(wide * wide, axis=-1, keepdims=True) + EPSILON)
            inverse[stream, part, :] = jnp.broadcast_to(inv, (piece, 128))
            unit = (wide * inv).astype(jnp.bfloat16)
            hat[stream, part, :] = unit
            buf[stream, c, pl.ds(0, piece), :] = unit
            at = c * piece
            line = own[at // 128 : at // 128 + 1, :].astype(jnp.float32)
            line = line[:, at % 128 : at % 128 + piece]
            ids[stream, 0, c] = jnp.concatenate([line] * (128 // piece), axis=1)

    far_sends = sum(wrap_distance(stream)[1].astype(jnp.int32) for stream in range(2))
    for stream in range(2):
        far_sends += (wrap_distance(stream)[0] == 2).astype(jnp.int32)
    skips = jnp.where(even, j != RUN - 2, j != 1).astype(jnp.int32)
    pl.semaphore_wait(barrier, 4 + skips + far_sends)

    def pick(stream, pair):
        return pair[stream] if isinstance(stream, int) else jnp.where(stream == 0, pair[0], pair[1])

    def route(stream, s, reach):
        place = pick(stream, (j, RUN - 1 - j))
        entry = lax.rem(place, 2) == 0
        fresh = (s == 0) | (s == SPAN)
        if reach == 2:
            goes = entry & (place != RUN - 2) & (fresh | (s == 1) | (s == SPAN + 1))
            return (g, pick(stream, [device(0, step)[1] for step in (2, -2)])), goes
        hop = s == SPAN - 1
        target = (
            jnp.where(hop, pick(stream, next_grp), g),
            jnp.where(hop, k, pick(stream, next_blk)),
        )
        goes = jnp.where(place == RUN - 1, s == 0, entry | fresh)
        return target, (s < SLOTS - 1) & (hop | goes)

    def chunk(stream, s, c):
        at = s * piece
        if not isinstance(at, int):
            at = pl.multiple_of(at, piece)
        return buf.at[stream, c, pl.ds(at, piece)]

    def remote(src, dst, send, recv, target):
        return pltpu.make_async_remote_copy(
            src_ref=src,
            dst_ref=dst,
            send_sem=send,
            recv_sem=recv,
            device_id=target,
            device_id_type=MESH,
        )

    def block_copy(stream, s, c, reach, target):
        return remote(
            chunk(stream, s, c),
            chunk(stream, s + reach, c),
            send_sem.at[reach - 1, stream, s],
            recv_sem.at[stream, s + reach, c],
            target,
        )

    def id_copy(stream, s, reach, target):
        return remote(
            ids.at[stream, s],
            ids.at[stream, s + reach],
            id_send_sem.at[reach - 1, stream, s],
            id_recv_sem.at[stream, s + reach],
            target,
        )

    def forward(stream, s, c):
        for reach in (2, 1):
            target, goes = route(stream, s, reach)

            @pl.when(goes)
            def _():
                @pl.when(c == 0)
                def _():
                    id_copy(stream, s, reach, target).start()

                block_copy(stream, s, c, reach, target).start()

    def receive(stream, s, c):
        target = (g, pick(stream, next_blk))

        @pl.when(c == 0)
        def _():
            id_copy(stream, s - 1, 1, target).wait_recv()

        block_copy(stream, s - 1, c, 1, target).wait_recv()

    def wrap_route(stream):
        to_edge, far = wrap_distance(stream)
        same = to_edge < SPAN
        slot = jnp.where(same, to_edge, to_edge + 1)
        step = 1 - 2 * stream
        return far, slot, device(jnp.where(same, 0, step), step * to_edge)

    def wrap_id_copy(stream):
        _, slot, target = wrap_route(stream)
        return remote(
            ids.at[stream, 0],
            ids.at[stream, slot],
            wrap_id_sem.at[stream],
            id_recv_sem.at[stream, slot],
            target,
        )

    def wrap(stream, c):
        far, slot, target = wrap_route(stream)

        if c == 0:

            @pl.when(far)
            def _():
                wrap_id_copy(stream).start()

        if c % 2:
            far = far & (wrap_distance(stream)[0] != DETOUR)

        @pl.when(far)
        def _():
            remote(
                chunk(stream, 0, c),
                chunk(stream, slot, c),
                wrap_sem.at[stream],
                recv_sem.at[stream, slot, c],
                target,
            ).start()

    def detour_copy(stream, c):
        step = pick(stream, (1, -1))
        return remote(
            chunk(stream, SPAN - 1, c),
            chunk(stream, DETOUR + 1, c),
            detour_sem.at[stream],
            recv_sem.at[stream, DETOUR + 1, c],
            device(step, 2 * step),
        )

    def detour(stream, s, c):
        @pl.when((s == SPAN - 1) & (j == pick(stream, (RUN - 2, 1))) & (lax.rem(c, 2) == 1))
        def _():
            detour_copy(stream, c).start()

    for c in range(WAVES):
        for stream in range(2):
            forward(stream, 0, c)
        for stream in range(2):
            wrap(stream, c)

    row = lax.broadcasted_iota(jnp.int32, (128, 128), 0)
    lane = lax.broadcasted_iota(jnp.int32, (128, 128), 1)
    for stream, own in ((0, text_ids), (1, image_ids)):
        for half in range(rows // 128):
            line = jnp.broadcast_to(own[half : half + 1, :].astype(jnp.float32), (128, 128))
            column = jnp.sum(jnp.where(row == lane, line, 0.0), axis=-1, keepdims=True)
            own_ids[stream, pl.ds(half * 128, 128), :] = jnp.broadcast_to(column, (128, 128))
        total[stream] = jnp.zeros(total.shape[1:], jnp.float32)

    scale = jnp.exp(jnp.full((1, 128), sharpness[0], jnp.float32))[:, :1]
    shift = offset[0]
    weight = -(adjoint[0] * scale / rows)
    group = SPAN * piece
    turn = lax.broadcasted_iota(jnp.int32, (1, 128), 1) // piece

    def compute(stream, c, half):
        mine = 1 - stream
        visitors = buf[stream, c, pl.ds(pl.multiple_of(half * group, group), group), :]
        grid = lax.dot_general(
            hat[mine], visitors, (((1,), (1,)), ((), ())), preferred_element_type=jnp.float32
        )
        logit = scale * grid + shift
        column = own_ids[mine, :, :]
        parts = []
        for at in range(0, group, 128):
            s = half * SPAN + at // piece
            line = ids[stream, s, c]
            for other in range(1, 128 // piece):
                line = jnp.where(turn == other, ids[stream, s + other, c], line)
            match = column == jnp.broadcast_to(line, (rows, 128))
            here = logit[:, at : at + 128]
            signed = jnp.where(match, here, -here)
            parts.append(jnp.where(match, weight, -weight) * (1.0 / (1.0 + jnp.exp(signed))))
        coef = jnp.concatenate(parts, axis=1).astype(jnp.bfloat16)
        total[mine] += jnp.dot(coef, visitors, preferred_element_type=jnp.float32)

    def step(i, carry):
        word = words[0]
        for other in range(1, len(words)):
            word = jnp.where(i == other, words[other], word)

        for _ in range(4):
            entry = lax.rem(word, 64)
            word = lax.div(word, 64)
            stream = lax.div(entry, 32)
            s = lax.rem(lax.div(entry, 4), 8)
            c = lax.rem(entry, 4)

            @pl.when(entry > 0)
            def _():
                receive(stream, s, c)
                forward(stream, s, c)
                detour(stream, s, c)

        @pl.when(word > 0)
        def _():
            product = word - 1
            compute(lax.div(product, 8), lax.div(lax.rem(product, 8), 2), lax.rem(product, 2))

        return carry

    lax.fori_loop(0, len(words), step, 0)

    for stream, out in ((1, grad_image), (0, grad_text)):
        for c in range(WAVES):
            part = pl.ds(c * piece, piece)
            inv = inverse[stream, part, :][:, :1]
            unit = raw[stream, part, :].astype(jnp.float32) * inv
            grad = total[stream, part, :]
            along = jnp.sum(unit * grad, axis=-1, keepdims=True)
            out[part, :] = inv * (grad - unit * along)

    for stream in range(2):
        for s in range(SLOTS - 1):
            for reach in (2, 1):
                target, goes = route(stream, s, reach)

                @pl.when(goes)
                def _():
                    id_copy(stream, s, reach, target).wait_send()
                    remote(
                        hat.at[stream],
                        hat.at[stream],
                        send_sem.at[reach - 1, stream, s],
                        recv_sem.at[stream, s + 1, 0],
                        target,
                    ).wait_send()

        far, slot, target = wrap_route(stream)
        detoured = wrap_distance(stream)[0] == DETOUR

        @pl.when(far)
        def _():
            wrap_id_copy(stream).wait_send()

        for cond, amount in ((jnp.logical_not(detoured), rows), (detoured, rows // 2)):

            @pl.when(far & cond)
            def _():
                part = hat.at[stream, pl.ds(0, amount)]
                remote(
                    part, part, wrap_sem.at[stream], recv_sem.at[stream, slot, 0], target
                ).wait_send()

        @pl.when(j == (RUN - 2, 1)[stream])
        def _():
            part = hat.at[stream, pl.ds(0, rows // 2)]
            remote(
                part, part, detour_sem.at[stream], recv_sem.at[stream, slot, 0], target
            ).wait_send()


def body(n_grp, n_blk, image_emb, text_emb, image_pair_index, text_ids, sharpness, offset, adjoint):
    rows, width = image_emb.shape
    vmem = pl.BlockSpec(memory_space=pltpu.VMEM)
    smem = pl.BlockSpec(memory_space=pltpu.SMEM)
    hbm = pl.BlockSpec(memory_space=pltpu.HBM)
    flops = 4 * SLOTS * 2 * rows * rows * width
    return pl.pallas_call(
        functools.partial(kernel, n_grp, n_blk),
        out_shape=(
            jax.ShapeDtypeStruct((rows, width), jnp.float32),
            jax.ShapeDtypeStruct((rows, width), jnp.float32),
        ),
        in_specs=[hbm, hbm, vmem, vmem, smem, smem, smem],
        out_specs=(vmem, vmem),
        scratch_shapes=[
            pltpu.VMEM((2, rows, width), jnp.bfloat16),
            pltpu.VMEM((2, rows, width), jnp.bfloat16),
            pltpu.VMEM((2, WAVES, SLOTS * rows // WAVES, width), jnp.bfloat16),
            pltpu.VMEM((2, SLOTS, WAVES, 1, 128), jnp.float32),
            pltpu.VMEM((2, rows, 128), jnp.float32),
            pltpu.VMEM((2, rows, 128), jnp.float32),
            pltpu.VMEM((2, rows, width), jnp.float32),
            pltpu.SemaphoreType.DMA((2,)),
            pltpu.SemaphoreType.DMA((2, 2, SLOTS)),
            pltpu.SemaphoreType.DMA((2, 2, SLOTS)),
            pltpu.SemaphoreType.DMA((2,)),
            pltpu.SemaphoreType.DMA((2,)),
            pltpu.SemaphoreType.DMA((2,)),
            pltpu.SemaphoreType.DMA((2, SLOTS, WAVES)),
            pltpu.SemaphoreType.DMA((2, SLOTS)),
        ],
        compiler_params=pltpu.CompilerParams(
            collective_id=0, has_side_effects=True, vmem_limit_bytes=60 * 1024 * 1024
        ),
        cost_estimate=pl.CostEstimate(
            flops=flops, bytes_accessed=12 * rows * width, transcendentals=2 * SLOTS * rows * rows
        ),
    )(
        image_emb,
        text_emb,
        image_pair_index.reshape(rows // 128, 128),
        text_ids.reshape(rows // 128, 128),
        sharpness,
        offset,
        adjoint,
    )


def solution(mesh):
    both = ("grp", "blk")
    return jax.shard_map(
        functools.partial(body, mesh.shape["grp"], mesh.shape["blk"]),
        mesh=mesh,
        in_specs=(P(both, None), P(both, None), P(both), P(both), P(), P(), P()),
        out_specs=(P(both, None), P(both, None)),
        check_vma=False,
    )
```

```python
import functools

import jax
import jax.numpy as jnp
from jax import lax
from jax.experimental import pallas as pl
from jax.experimental.pallas import tpu as pltpu
from jax.sharding import PartitionSpec as P

MESH = pl.DeviceIdType.MESH
EPSILON = 1e-06

SPAN = 4
SLOTS = 8
LINE = 4
PATIENT = (7, 2)
RUN = 16
WAVES = 4
DETOURS = (
)


ORDER = (
    (
        10639617, 150997798, 184736233, 230598190, 251658283, 2115340, 16777241, 1543181, 3791945, 50331700,
        4259418, 83927474, 167776058, 33555729, 15592819, 124605127, 67112381, 201328598, 234881086,
        268697047, 100663314, 134217747, 0, 0,
    ),
    (
        10115329, 10910504, 150994989, 184549376, 218277422, 251837404, 7684889, 7017840, 6153656, 8240313,
        13583245, 15684602, 16777732, 167772540, 50331657, 204017478, 33554432, 83886087, 117440523, 67363958,
        234881024, 100663314, 134444287, 268435456,
    ),
    (
        1859908, 9865473, 11430569, 151177692, 184549421, 221368878, 16777216, 251661300, 50385520, 14282549,
        167775764, 83946570, 16090487, 201326649, 6619890, 33685391, 117440570, 234881024, 7339226, 67108881,
        268435515, 100664722, 134218967, 0,
    ),
    (
        1859908, 9865473, 11430569, 151177692, 196560413, 14002073, 218103854, 12710939, 251661302, 2346481,
        167776120, 16777228, 204969033, 50331648, 33613066, 83886130, 132710283, 234881024, 67110226,
        114126591, 268435456, 134219219, 0, 0,
    ),
    (
        2380292, 6, 162695425, 10005349, 184719815, 218276590, 251837487, 20131377, 14106228, 50332538,
        183729910, 83944472, 201326653, 235136793, 268436479, 117441821, 33554432, 72742801, 106509970,
        134219227, 0, 0, 0, 0,
    ),
    (
        2380292, 162695425, 11952549, 186552999, 11207406, 218103857, 251865839, 7720184, 14020212, 8351376,
        183729876, 201330513, 16854924, 234881024, 50331661, 268514687, 83886094, 33554456, 117440527,
        67110486, 100663322, 134219227, 0, 0,
    ),
    (
        1859908, 9476616, 41, 26518273, 50334349, 84042635, 117503019, 151176295, 184737042, 232197011,
        251661423, 14626614, 182709501, 201326649, 235119900, 268558079, 33554456, 67110485, 107575190,
        134219487, 0, 0, 0, 0,
    ),
    (
        1859908, 2568, 16925441, 50387529, 11076261, 83886094, 128776587, 151177681, 196427026, 218103854,
        264183152, 5491894, 6504311, 167772216, 201330617, 234884757, 268678591, 33670617, 67110746,
        100663326, 134219487, 0, 0, 0,
    ),
    (
        1206628, 11555367, 150997513, 6, 1878849, 184552489, 27839371, 218103808, 63353711, 251658260,
        84094478, 117441493, 4292182, 4697395, 183745973, 201577655, 234885011, 268435519, 33556248, 67110745,
        100787930, 134217759, 0, 0,
    ),
    (
        10381668, 516, 11571521, 151038470, 12751341, 184549387, 218106794, 16978708, 50525035, 251658240,
        83886997, 5831864, 117440528, 13844055, 14228858, 183602898, 201579987, 33558428, 234881024,
        268435519, 74823321, 100663326, 134217759, 0,
    ),
    (
        1859908, 9476616, 41, 16777985, 50483853, 83887018, 11336075, 117440528, 151176295, 196445364,
        230268243, 264437146, 13092564, 14888789, 167772215, 201584243, 235122646, 268439255, 33554460,
        67108893, 100663326, 134217759, 0, 0,
    ),
    (
        1859908, 8, 16941825, 50387209, 4346537, 83888782, 121443046, 4819687, 150998316, 184653037,
        218107246, 12430356, 251860726, 5758140, 167775799, 16487859, 201326620, 33558167, 234881024,
        268439295, 67108893, 100663326, 134217759, 0,
    ),
    (
        1206628, 11555367, 162955657, 10779658, 184552331, 16777228, 62825329, 218103808, 84093646, 251658260,
        117444111, 13485077, 7816633, 13964794, 6516446, 33558303, 167772178, 201432951, 67108883, 234881086,
        100663322, 268435519, 134217755, 0,
    ),
    (
        9980260, 11555367, 150997513, 12767878, 184552007, 218276590, 29816076, 251658283, 50334861, 89883541,
        117440527, 13868240, 14013916, 14257978, 167774097, 33554432, 14495455, 67112793, 201328275,
        100663358, 234881024, 134217755, 268435519, 0,
    ),
    (
        1859908, 16828936, 61135113, 11077962, 83886094, 127472587, 151177707, 196447506, 224849235, 12543280,
        251661402, 7310834, 7576789, 33554454, 67110778, 100789975, 134217759, 167772220, 201326653,
        234881086, 268435519, 0, 0, 0,
    ),
    (
        1859908, 16828936, 53908068, 2794533, 83886094, 4518630, 117440555, 151176743, 184737042, 225109209,
        251853877, 7282068, 7568568, 33789299, 67229114, 100906903, 134217759, 167772220, 201326653,
        234881086, 268435519, 0, 0, 0,
    ),
    (
        10381668, 1491460, 150997513, 2649133, 184549417, 3084782, 218106858, 28101780, 251658240, 50332501,
        83944883, 117441524, 6247452, 33555997, 4842614, 67237495, 100664979, 134217755, 167775804, 201330301,
        234884798, 268439295, 0, 0,
    ),
    (
        10381668, 161516292, 12767813, 184549417, 229157766, 12522183, 251658283, 16778004, 50386290,
        97469334, 117503440, 7675228, 39921590, 73742327, 100663322, 134217755, 167775804, 201330553,
        234885050, 268439547, 0, 0, 0, 0,
    ),
    (
        1859908, 26264104, 60084841, 4252330, 83886118, 10285803, 117440556, 150994944, 184650577, 218105006,
        251661273, 12954643, 7453844, 33555827, 67110742, 100665239, 134217759, 183737656, 16215733,
        201326651, 234885047, 268435519, 0, 0,
    ),
    (
        1859908, 3180840, 16777257, 53779109, 11314214, 83888590, 151176267, 117440527, 184550573, 218106776,
        251658287, 6895216, 13219121, 40987861, 67110743, 100663326, 134219772, 167775544, 201563517,
        235122110, 268680703, 0, 0, 0,
    ),
    (
        10381668, 1346308, 150994984, 195322477, 3072647, 218103850, 16954159, 251658240, 50332500, 83886094,
        117441871, 7698198, 6682142, 33621722, 71814196, 100865205, 167772216, 148582227, 201326649,
        250342899, 268439547, 0, 0, 0,
    ),
    (
        10381668, 1491460, 150994984, 10773101, 184549386, 229159406, 16778031, 251658283, 50332500, 83887438,
        117441935, 7960412, 15833048, 16221914, 167775536, 14150777, 201326650, 235105471, 268664059,
        33554448, 67108881, 100663314, 134217747, 0,
    ),
    (
        1859908, 3293736, 16777257, 50387273, 11428522, 83886987, 117440527, 151176231, 184549421, 218103854,
        251661272, 7186001, 8251228, 15926482, 33554452, 67198072, 167772212, 100667222, 201546937, 134217751,
        251358899, 268697335, 0, 0,
    ),
    (
        1859908, 20070952, 11162217, 50331661, 87734666, 129135563, 150994944, 184549421, 218103854,
        251661272, 7452313, 15157112, 14023710, 15690874, 4682802, 168019123, 33555731, 67108885, 201326653,
        100663318, 134217751, 234881086, 268435519, 0,
    ),
    (
        10381668, 151161604, 184717869, 218278789, 253426377, 5288394, 16777228, 50332501, 83886094,
        117440527, 8251228, 4689680, 16065972, 167772208, 33653975, 201546873, 6778046, 67108922, 234881024,
        100773363, 134221787, 268435515, 0, 0,
    ),
    (
        10381668, 150997548, 195330349, 218106542, 251661039, 2646597, 16827079, 50331661, 83886094,
        117505328, 7822428, 8334750, 5492211, 167772216, 5837845, 5055997, 201328185, 33554432, 67110526,
        234881082, 100667354, 268435515, 134217755, 0,
    ),
    (
        1859908, 10783016, 16829093, 11432550, 50331661, 150995628, 83952572, 184552267, 218103854, 117440527,
        251852349, 4973657, 180440376, 7050453, 201530710, 7579099, 33778879, 234881024, 67110771, 100667102,
        134221279, 268435456, 0, 0,
    ),
    (
        1859908, 9869608, 16826922, 15891174, 50332489, 83886986, 154975037, 117440512, 184552493, 218106990,
        251915439, 4686899, 167772212, 6812824, 6905428, 215312083, 33670650, 234881078, 67112669, 268435511,
        100663326, 134217759, 0, 0,
    ),
    (
        10381668, 10506756, 11049592, 2801222, 3124999, 167988244, 16777228, 50388821, 201528373, 83887502,
        117623951, 158408438, 6366685, 33557374, 234881049, 184549395, 67108894, 112932535, 218216447,
        268435456, 134217728, 251658287, 0, 0,
    ),
    (
        10381668, 10915448, 11043132, 15381061, 151175814, 19968509, 50331661, 83887028, 167772208, 117440527,
        184617854, 5578452, 214290421, 6411666, 33557934, 218103827, 234881074, 67110809, 251886579,
        268435479, 100664991, 134217755, 0, 0,
    ),
    (
        1859908, 16828680, 9945716, 50388326, 87808458, 14222072, 117638097, 167772222, 5215762, 201326641,
        13272345, 5764791, 150994988, 234883706, 184642395, 33557724, 79341021, 218103867, 268435456,
        100663326, 251661039, 134217759, 0, 0,
    ),
    (
        1859908, 9658164, 10214949, 16777992, 53779879, 98886312, 117502718, 167775248, 150994988, 11009681,
        214257106, 5584443, 184551021, 218106542, 234881074, 41088662, 251869911, 268435456, 67108893,
        100665243, 134217759, 0, 0, 0,
    ),
    (
        10115329, 151177767, 184552297, 218106794, 2146607, 16777259, 251658245, 50385289, 2035210, 6493451,
        83945268, 13462677, 117503609, 6911861, 7302814, 168021727, 33555511, 201326653, 67112849, 234881024,
        100663314, 268435519, 134217747, 0,
    ),
    (
        10115329, 151177767, 184552045, 218106542, 5435908, 251658283, 1412208, 14718741, 7704982, 20017842,
        48712912, 50455386, 67108881, 83887246, 100663296, 121418951, 15580853, 134217759, 167775676,
        201326653, 234881086, 268439543, 0, 0,
    ),
    (
        1859908, 9865473, 11446697, 151177672, 16777228, 184605513, 50334986, 83886094, 117502704, 218221464,
        13063760, 251852634, 13233563, 182681361, 216520691, 33555604, 234884798, 67112917, 268435515,
        100664534, 134217751, 0, 0, 0,
    ),
    (
        1859908, 10914049, 11430565, 16826919, 150997784, 2463540, 50331661, 184551085, 7276362, 83887029,
        5855124, 218103854, 117503435, 33623473, 251658287, 13180727, 67108920, 167772191, 201404029,
        100663358, 234881082, 149766131, 268435456, 0,
    ),
    (
        2380292, 6, 11700481, 10934602, 150997383, 184549415, 218278795, 254983152, 16777265, 50388530,
        87792947, 131661493, 5471964, 167776029, 201577502, 234885023, 268436863, 33653905, 67212502,
        100663322, 134219479, 0, 0, 0,
    ),
    (
        20996, 11682369, 150997541, 11823590, 184552010, 12255943, 218103850, 251837425, 16778034, 13843996,
        50332509, 15423417, 83886094, 6516447, 167772220, 201578137, 117695479, 234881051, 268521424,
        33554432, 67110225, 100742546, 134217751, 0,
    ),
    (
        1859908, 2509320, 152233, 16777985, 50331661, 86829482, 117440527, 151177707, 184552749, 218323888,
        266007601, 14664818, 5233874, 168005528, 201326649, 234884756, 268439547, 40985945, 67229146,
        100663326, 134219739, 0, 0, 0,
    ),
    (
        1859908, 150024, 27562753, 50334029, 84059018, 3979664, 117440555, 150997799, 184621940, 218323888,
        251861970, 14664950, 168005490, 201564060, 242984819, 268439295, 33654047, 67110485, 100771286,
        134217755, 0, 0, 0, 0,
    ),
    (
        10381668, 2380292, 151022124, 2019969, 184550121, 27986828, 218103821, 50332591, 83886123, 251661391,
        117440512, 13606072, 13978938, 183729910, 201330517, 234881086, 268439510, 39912924, 67213137,
        7185618, 100663326, 134217759, 0, 0,
    ),
    (
        10381668, 2380292, 161508097, 10779466, 184550128, 218106794, 16777228, 50525012, 251718763, 83886080,
        117440527, 5741752, 14134516, 183745942, 201577975, 234881086, 268435519, 40993872, 74814674,
        100787930, 134217759, 0, 0, 0,
    ),
    (
        1859908, 9476616, 16945921, 50483853, 83888782, 117502694, 151177707, 184552308, 218106805, 251658287,
        13093942, 14519485, 167775795, 201561150, 234882682, 268439295, 4830298, 33556244, 67229011,
        100787670, 134217759, 0, 0, 0,
    ),
    (
        1859908, 2568, 16777985, 50385508, 87708329, 3979690, 117440528, 162630123, 184552308, 218295633,
        258407856, 14626609, 167776120, 217816282, 234884754, 268681179, 40981779, 67229142, 100663326,
        134217759, 0, 0, 0, 0,
    ),
    (
        9980260, 11555367, 150997513, 2019974, 197323339, 16779916, 218103857, 50334669, 251659179, 83886080,
        117440527, 15011378, 15420625, 183723189, 5232443, 201326647, 234881086, 268695380, 5895518, 33554456,
        67110487, 100663322, 134217755, 0,
    ),
    (
        9980260, 11555367, 150997513, 12767878, 184552007, 27839371, 218104689, 50331695, 251658283, 83944754,
        117440527, 13436728, 15418745, 15848565, 167772214, 14668987, 201326611, 234885022, 268563903,
        33555991, 67108889, 100663322, 134217755, 0,
    ),
    (
        1859908, 16828936, 61133412, 2689701, 83886094, 3978342, 117440555, 150997799, 184737042, 218295635,
        264203284, 14888021, 13463159, 6534650, 167772220, 49661593, 201326592, 67110747, 234881086,
        100663326, 268435519, 134217759, 0, 0,
    ),
    (
        1859908, 16828936, 61133412, 2794533, 83886094, 3978342, 117440555, 151176359, 189631348, 218103854,
        257100789, 13212790, 13458936, 15300025, 167776059, 201330522, 234999707, 33554432, 268435519,
        67108893, 100663326, 134217759, 0, 0,
    ),
    (
        10381668, 161516292, 12767813, 184740422, 218106506, 12368967, 251658283, 16862348, 50332501,
        84096398, 117505296, 13993047, 5057945, 15840951, 33554460, 167772216, 201330301, 67108893, 100665278,
        234881082, 134221791, 268435515, 0, 0,
    ),
    (
        10381668, 161516292, 12767813, 184549417, 229157766, 12368967, 251658283, 16829588, 50332501,
        83946710, 121467956, 39917365, 15848630, 67108889, 168002807, 216383322, 100665278, 234881082,
        134461439, 268435456, 0, 0, 0, 0,
    ),
    (
        1859908, 3180840, 16777257, 53779109, 3712038, 83886123, 11580519, 150994959, 117440557, 184549394,
        218103854, 251661272, 7013971, 5618772, 33556274, 67108893, 108623283, 134219768, 15425140, 183729910,
        201326653, 234881086, 268435519, 0,
    ),
    (
        1859908, 3180840, 16777257, 53779109, 11314214, 83944167, 150996076, 184549421, 117440527, 218179118,
        251658287, 6895216, 13219121, 33672725, 7695667, 67108921, 167776023, 100666718, 134217759, 201330554,
        251363062, 268435519, 0, 0,
    ),
    (
        10381668, 1491460, 150994984, 2648905, 184549417, 229159406, 16956364, 251658240, 50332500, 83886997,
        117441494, 7698192, 39921553, 73744159, 100861620, 134217755, 16457085, 14630070, 167776248,
        201326649, 234881082, 268435515, 0, 0,
    ),
    (
        10381668, 1491460, 150994984, 2648905, 184549417, 229159406, 16956364, 251658240, 50332500, 83887438,
        117531600, 13829980, 7959676, 33555986, 168004977, 73742333, 114007450, 201326654, 134217755,
        235122163, 268439295, 0, 0, 0,
    ),
    (
        1859908, 20070952, 11162217, 50331661, 87624074, 3979755, 117443345, 150994944, 184549421, 218103854,
        251733551, 5350617, 41125211, 74808342, 100663326, 134221407, 13577905, 183721716, 201580022,
        234881086, 268435519, 0, 0, 0,
    ),
    (
        1859908, 20070952, 11162217, 50331661, 87624074, 121420267, 150994988, 184552273, 218105006,
        251661272, 12666451, 12934682, 6002420, 33554460, 15424663, 67108893, 100663326, 134348211, 168021499,
        201326653, 234881086, 268435519, 0, 0,
    ),
    (
        10381668, 1491460, 150994984, 196514185, 218294922, 263123655, 16777228, 50332500, 83886997,
        117441494, 7698228, 4582736, 38374844, 67212511, 100663322, 134220827, 13311485, 167772216, 201564083,
        234885114, 268435515, 0, 0, 0,
    ),
    (
        10381668, 10666500, 150994949, 184717933, 218276270, 251837386, 20005575, 3497012, 50331701, 87778737,
        4553872, 117440527, 4836599, 33554456, 73742237, 100664991, 134219516, 167775805, 201330302,
        234884799, 268435515, 0, 0, 0,
    ),
    (
        1859908, 20072968, 53909833, 3713450, 83886123, 117502695, 150994988, 184552316, 218106776, 251852413,
        4304816, 16587867, 5713428, 33646354, 67228887, 100666974, 134219763, 167772212, 201330042, 234884854,
        268435511, 0, 0, 0,
    ),
    (
        1859908, 3293736, 16777257, 53913929, 2783974, 150994988, 83886094, 184552316, 121824203, 218103808,
        12572208, 251658257, 6808753, 5322418, 7167987, 33556246, 67340119, 100663326, 134217759, 167775545,
        201330042, 234884539, 268435511, 0,
    ),
    (
        10381668, 2380292, 14723590, 11055593, 16778041, 50332523, 150997818, 83887036, 184737083, 218106813,
        117503294, 5622837, 167772176, 4715933, 214247319, 251788278, 33555987, 67112089, 234881024,
        100873911, 268435483, 134217728, 0, 0,
    ),
    (
        10381668, 1475076, 11178616, 2798009, 151243578, 16233159, 184549421, 16778004, 218105198, 50331661,
        251874302, 88401296, 121632210, 180475667, 33773086, 67110873, 201326641, 100665014, 134220955,
        234881024, 268439027, 0, 0, 0,
    ),
    (
        1859908, 16777992, 50479945, 9744180, 83886094, 16210315, 117440527, 16476711, 150994988, 12025848,
        167772208, 184549417, 233499321, 201329744, 6796376, 5612692, 256846575, 234881024, 13464987,
        268435484, 33554432, 67108893, 100663326, 134217759,
    ),
    (
        1859908, 16777992, 9739556, 50332540, 16153958, 83946890, 151177784, 14603006, 117441551, 184720313,
        4979665, 218106520, 251661050, 167853081, 5748372, 214267606, 33554460, 234881074, 67108893,
        100666590, 268435456, 134217759, 0, 0,
    ),
    (
        10115329, 151177767, 184552297, 218106542, 2289932, 16777229, 251658283, 52749573, 1674352, 46777359,
        86724117, 13488601, 6250070, 117487514, 14284538, 67110011, 167775740, 201326653, 100663314,
        234881086, 268436735, 134217728, 0, 0,
    ),
    (
        10115329, 150997800, 184720231, 229163310, 16970253, 251658283, 52752718, 83930630, 117486855,
        13720688, 5885080, 48715344, 67109981, 7959706, 100663354, 8337147, 167772220, 134217747, 201330550,
        234881086, 268439039, 0, 0, 0,
    ),
    (
        1859908, 9865473, 11430569, 28363208, 150994944, 50386441, 5456540, 184549421, 83946521, 12107101,
        218105521, 33554448, 13301659, 251659254, 117440512, 182679548, 71800179, 201326653, 4812730,
        234881083, 100663296, 268436735, 134217751, 0,
    ),
    (
        1859908, 10914049, 11430565, 16828872, 150997769, 50334989, 83886986, 117503499, 7443504, 184549421,
        7033969, 33554452, 218180509, 67110262, 251658287, 107968406, 167902780, 15195283, 201326615,
        134217728, 234884798, 268648191, 0, 0,
    ),
    (
        2380292, 10633601, 150994988, 10005349, 184552039, 229302983, 13024240, 251658252, 16777216, 53972210,
        15060240, 6349941, 83886134, 15693690, 117687250, 167772190, 33556436, 201326653, 234881086,
        268439507, 67110233, 100664730, 134219479, 0,
    ),
    (
        2380292, 162695425, 10250661, 184720202, 12772039, 218103850, 16970545, 251661042, 50388531, 97840756,
        117441488, 5465914, 4701661, 167772220, 201450877, 33554456, 234885010, 67368534, 268435456,
        100663322, 141391071, 0, 0, 0,
    ),
    (
        1859908, 2509320, 41, 16777985, 50334029, 84059018, 121696998, 151177707, 184552273, 218295348,
        13063316, 251661298, 13485430, 5848572, 167776120, 201330302, 33558168, 234881024, 268439295,
        67213143, 100664990, 134219739, 0, 0,
    ),
    (
        1859908, 150024, 16777985, 50500425, 94954149, 121418790, 162601451, 184736820, 230366546, 264187284,
        6540787, 167772216, 201561469, 250189054, 33554460, 268694971, 67110746, 100663326, 134346455, 0, 0,
        0, 0, 0,
    ),
    (
        10381668, 2380292, 44, 151159169, 2915146, 184549417, 29551244, 218103821, 50331648, 251661291,
        83944753, 117673103, 13866320, 6503802, 15801750, 167772219, 201578103, 234881086, 268435519, 5076626,
        33554460, 67110747, 100663326, 134217759,
    ),
    (
        10381668, 516, 11571521, 151159430, 11965127, 184549424, 16779916, 218103854, 50334797, 255523540,
        83886080, 117441522, 13700629, 15424761, 168021398, 217560631, 234885009, 268435519, 33554460,
        73258578, 100665242, 134346451, 0, 0,
    ),
    (
        1859908, 9476616, 16777985, 50331661, 3035817, 84060558, 117441551, 151177959, 184735284, 12774737,
        218105428, 251661302, 16199473, 174706168, 33554432, 5582771, 201326649, 67348351, 234881024,
        268435515, 100787603, 134346203, 0, 0,
    ),
    (
        1859908, 8, 16777985, 59822696, 87726410, 11166416, 117440527, 151177707, 198366296, 224877614,
        251861972, 16199478, 167849498, 15199731, 201326620, 33554432, 234884799, 268435515, 74802389,
        100665243, 134219735, 0, 0, 0,
    ),
    (
        9980260, 11555367, 150997513, 195482246, 12104176, 218103850, 16777228, 50535373, 89336526, 251658240,
        117444111, 15013648, 40086835, 14013589, 167997243, 217544595, 234972798, 67108864, 268435519,
        100664983, 134219487, 0, 0, 0,
    ),
    (
        9980260, 11555367, 150997513, 2019974, 197180329, 218103850, 16777228, 257080431, 50331661, 83889294,
        117441528, 4429148, 15415156, 33556021, 15953617, 167772178, 206560734, 234885014, 268435519,
        67108889, 100664983, 134219487, 0, 0,
    ),
    (
        1859908, 16828936, 61133412, 3713360, 83886122, 3978342, 117440555, 164809170, 184628781, 218189166,
        265903088, 14536497, 39530009, 167772160, 201563389, 251379351, 67110557, 100665243, 134217759,
        268435519, 0, 0, 0, 0,
    ),
    (
        1859908, 16828936, 61133412, 2795856, 83886094, 4518630, 117440555, 150997799, 196560402, 218106805,
        14351379, 251860249, 7572663, 33554453, 15297785, 74954391, 100665243, 167772220, 201326653,
        134221727, 234881024, 268435519, 0, 0,
    ),
    (
        10381668, 161516292, 10932805, 184549424, 229157766, 12893127, 251658283, 16778004, 63755634,
        83944888, 15037492, 117440527, 40064785, 6919350, 67348307, 100787959, 134217759, 167776059,
        201326653, 234881086, 268435519, 0, 0, 0,
    ),
    (
        10381668, 161516292, 10932805, 184549808, 218276526, 3079239, 251661012, 16778034, 50541397, 83886998,
        117441524, 13989648, 33654609, 67212470, 7185655, 100663326, 134219768, 183746233, 201326653,
        234881086, 268435519, 0, 0, 0,
    ),
    (
        1859908, 3180840, 16777257, 53779109, 3712038, 83886123, 162575463, 117440527, 184549421, 218293778,
        251763700, 14001392, 7163004, 33672341, 13462973, 67108893, 100665239, 134217759, 182681598,
        201326649, 234881082, 268435515, 0, 0,
    ),
    (
        1859908, 3180840, 16777257, 53779109, 11338406, 83886094, 151175911, 117625935, 184549376, 218106776,
        251661266, 5090329, 13219121, 33765141, 67110742, 100665239, 134217759, 14146876, 14679486, 167772216,
        201326649, 234881082, 268435515, 0,
    ),
    (
        10381668, 1491460, 150994984, 2648905, 184549417, 229159406, 5295088, 16777259, 251658240, 50331661,
        83944817, 121466384, 7808785, 7962194, 33555987, 67110495, 100663322, 134217755, 13614906, 167775549,
        201326645, 234884542, 268439039, 0,
    ),
    (
        10381668, 1491460, 150994984, 2648905, 184549417, 229159406, 16780236, 50334413, 251658260, 83886094,
        117507029, 4576668, 39921118, 67213267, 100663322, 134217755, 15146544, 15679154, 167775548,
        201330549, 234885046, 268439543, 0, 0,
    ),
    (
        1859908, 20070952, 11162217, 50331661, 87624074, 2955755, 117440527, 150994988, 184552274, 218106776,
        258426095, 5723796, 40990422, 67108893, 100663326, 134221215, 15191544, 167772208, 15675057,
        201330547, 234881086, 268435519, 0, 0,
    ),
    (
        1859908, 20070952, 11162217, 50331661, 4254090, 83886123, 129135563, 150994944, 184552273, 218103854,
        251852306, 6894873, 40986325, 67110743, 100663326, 134217759, 14642548, 168021048, 15412849,
        201572211, 234881086, 268435519, 0, 0,
    ),
    (
        10381668, 1491460, 150994984, 195324745, 218276526, 11471815, 251658251, 16778004, 50386289, 83886998,
        117503440, 4925201, 7818451, 33554456, 81108510, 167772220, 100663322, 134219487, 16482166, 201330303,
        234881082, 268435515, 0, 0,
    ),
    (
        10381668, 161516292, 195482181, 229157766, 264155847, 16777228, 50332941, 83887438, 117440527,
        39913238, 4838487, 67213232, 7023699, 100663327, 134219507, 168005428, 216493941, 235122615,
        268439295, 0, 0, 0, 0, 0,
    ),
    (
        1859908, 20070952, 11162217, 50331661, 3712038, 84048593, 151243531, 117441679, 184552280, 218106813,
        251851993, 5502654, 12674395, 46517527, 167772216, 67108893, 100663326, 134348402, 215465651,
        234881078, 268435511, 0, 0, 0,
    ),
    (
        1859908, 10783016, 16777228, 53779109, 10281638, 83886123, 117621707, 150995004, 184549421, 218172312,
        264050301, 5091218, 33670463, 74802523, 100665239, 134220831, 167775544, 215428721, 235105971,
        268439035, 0, 0, 0, 0,
    ),
    (
        10381668, 2380292, 1743416, 11315897, 15532538, 16237265, 12660628, 16781260, 150994988, 167772212,
        50332501, 184552278, 83886094, 121468149, 218105646, 12445558, 251658264, 33781745, 201326592,
        67108889, 100663322, 134220955, 234881024, 268435507,
    ),
    (
        10381668, 14844420, 1741381, 2069162, 32033483, 50578299, 16772948, 150994988, 83887438, 117441488,
        7538065, 184549421, 167987031, 218294162, 33555987, 12539487, 67108913, 251658240, 201326592,
        100663322, 134219510, 234881074, 268439027, 0,
    ),
    (
        1859908, 16777992, 9503348, 50331661, 13967141, 4969126, 83888590, 14499766, 14939403, 117504789,
        12035641, 150997563, 167775254, 184552025, 201329774, 218106522, 234881074, 263042543, 268435507,
        33554460, 67108893, 100663326, 134217759, 0,
    ),
    (
        1859908, 20138248, 10002213, 50335053, 94167741, 133755638, 16584247, 6526060, 12041874, 150997523,
        10831470, 184551061, 167775279, 218103850, 264680859, 201326592, 33556247, 67108893, 234881074,
        100663326, 134221023, 268435456, 0, 0,
    ),
    (
        10115329, 10910504, 150994989, 184549376, 218277422, 3475212, 38868591, 251661021, 67108885, 1142042,
        7175518, 16777759, 1543222, 50334793, 100666962, 2847154, 83887034, 134217747, 121420999, 167776059,
        201326653, 234881086, 268435519, 0,
    ),
    (
        10115329, 150997800, 196778855, 224414348, 16811823, 258388877, 7816197, 33752335, 50331657, 6843509,
        84009650, 1908147, 67108885, 117551864, 5895351, 100663353, 134456535, 167775996, 201326653,
        234881086, 268435519, 0, 0, 0,
    ),
    (
        1859908, 9865473, 7498409, 10343723, 163759637, 33555481, 2299802, 184552283, 16778015, 218295602,
        62709065, 251658240, 15953110, 83956618, 67108919, 182702807, 117441679, 100663296, 201326649,
        134221715, 234881082, 268439547, 0, 0,
    ),
    (
        1859908, 10914049, 11430565, 27051784, 150994988, 5282845, 184552557, 50332504, 33620638, 218107054,
        83889422, 2989269, 251661301, 117442511, 67110289, 14927542, 167869915, 100663314, 134456569,
        201326653, 234885051, 268435519, 0, 0,
    ),
    (
        2380292, 6, 11700481, 150994954, 2021989, 184549414, 229303015, 251661039, 12698648, 8095577,
        33555761, 16778316, 13446303, 50331661, 5090932, 83887029, 67110266, 117503734, 100666838, 134217751,
        167772220, 201330555, 234881086, 268435519,
    ),
    (
        2380292, 10668289, 150994981, 11958662, 184717959, 218278795, 16778031, 251658283, 53941296, 4663064,
        84118734, 33554452, 6630772, 117440527, 14540217, 67196122, 8220318, 100665084, 167772160, 134221655,
        201326592, 234885051, 268435519, 0,
    ),
    (
        1859908, 2509320, 16828993, 50334029, 88140426, 117504395, 11696849, 150994962, 184549421, 218106780,
        13751508, 251658287, 39935868, 12677118, 6155381, 67214518, 115453151, 167772160, 134452983,
        201326592, 234881082, 268435515, 0, 0,
    ),
    (
        1859908, 2568, 26252033, 50332521, 11076261, 93918091, 117440527, 162605547, 184549421, 218103854,
        251658287, 7587028, 12797309, 40050686, 13462898, 6679965, 67108887, 167772216, 100793946, 201326592,
        134217755, 234884791, 268435515, 0,
    ),
    (
        10381668, 2380292, 161508097, 10793418, 184549421, 218106794, 16777228, 50525453, 251658283, 83886094,
        130085909, 15439288, 6276184, 7446269, 33554481, 5242770, 13483162, 167774068, 67108864, 201326645,
        100666782, 234881024, 134221279, 268435456,
    ),
    (
        10381668, 20996, 10525441, 150994950, 186553005, 218278795, 16971020, 50509133, 251658240, 83886094,
        121463864, 15306352, 15539991, 6758226, 13189118, 33554460, 167775514, 201447157, 67108915, 234881078,
        100663326, 268435511, 134217759, 0,
    ),
    (
        1859908, 2568, 26264129, 50331661, 3840330, 83888784, 117502694, 6363627, 150994988, 184552749,
        218293529, 264086709, 14933814, 33556245, 15197403, 7843831, 67108923, 100787670, 134217759,
        167772208, 201326641, 234881074, 268435507, 0,
    ),
    (
        1859908, 8, 16828929, 10801764, 50331664, 11069770, 83886097, 128776587, 151176359, 198286168,
        218103854, 258559343, 7565075, 33554488, 14507867, 15298489, 67352447, 167775255, 100663326,
        201326641, 234883058, 134217728, 268435507, 0,
    ),
    (
        9980260, 11555367, 150997513, 195482246, 12772039, 218104618, 16777216, 11326767, 50331697, 251658240,
        83889294, 117670927, 15058005, 33768989, 6005918, 14400883, 67356243, 167772160, 217413623, 234881086,
        268435519, 100663322, 134217755, 0,
    ),
    (
        9980260, 11555367, 151159177, 10777261, 184738544, 218106516, 22485964, 251658283, 50331661, 14771122,
        83887056, 117440512, 7838940, 33653876, 7961978, 8371602, 167773436, 67110519, 201326653, 100663322,
        234881086, 268435519, 134217755, 0,
    ),
    (
        1859908, 16828936, 61133412, 3713360, 83886122, 3978342, 117440555, 151176359, 184737048, 218106771,
        12424501, 251659632, 46518070, 6909815, 167775794, 7812606, 67108921, 201326655, 234881082, 268439259,
        100663326, 134217759, 0, 0,
    ),
    (
        1859908, 16828936, 10803465, 50331664, 87730506, 4088907, 117440555, 162690578, 184737049, 218106771,
        5442906, 251658287, 5753974, 33782940, 173790968, 216366334, 67108893, 234885114, 100667102,
        268435456, 134217759, 0, 0, 0,
    ),
    (
        10381668, 161516292, 195482181, 2820998, 218103850, 13038279, 251661012, 22514828, 56311373, 83886094,
        15418832, 117440527, 6510353, 33674427, 67358105, 167772160, 108754579, 201326653, 234885019,
        134217759, 268435519, 0, 0, 0,
    ),
    (
        10381668, 1346308, 151179880, 184552006, 2026506, 218106507, 263015535, 16777228, 50388117, 87766456,
        121586745, 4572666, 6368605, 33554462, 167772220, 72334745, 100793818, 201326653, 134217755,
        234881086, 268435519, 0, 0, 0,
    ),
    (
        1859908, 3180840, 16777257, 53779109, 3713424, 83886123, 11580519, 150994959, 117440512, 12011026,
        184549429, 218106777, 251765999, 7163312, 13196785, 33646392, 67110771, 168019449, 100663326,
        201457530, 134217728, 234885051, 268435519, 0,
    ),
    (
        1859908, 20070952, 53891689, 3712042, 83886118, 3044459, 117443343, 150994944, 184734872, 218293876,
        12518645, 251658266, 7324982, 168002929, 5996402, 33558428, 82171379, 201328575, 100663354, 234881024,
        268437499, 134217728, 0, 0,
    ),
    (
        10381668, 1491460, 150994984, 2648905, 184740905, 218149354, 11324401, 16777236, 251658240, 50331661,
        83944818, 121582992, 7677713, 5106967, 33656373, 73885689, 100892314, 134217755, 167776059, 201326653,
        234881086, 268435519, 0, 0,
    ),
    (
        10381668, 1346308, 150994984, 195322477, 12771975, 218299019, 28132145, 251658240, 50332530, 83952533,
        130874902, 4673116, 4838906, 39972597, 73790710, 100665015, 134217755, 167772220, 201326653,
        234881086, 268435519, 0, 0, 0,
    ),
    (
        1859908, 20070952, 11162217, 50331661, 87624074, 3044459, 117440527, 150994988, 184552274, 218106776,
        251659503, 12690713, 12938517, 13204827, 33554460, 67231155, 100663326, 134219767, 15707768,
        167772220, 201326653, 234881086, 268435519, 0,
    ),
    (
        1859908, 3293736, 16777257, 50387273, 10003498, 83944171, 117601359, 150994988, 184552274, 218106776,
        258426095, 12692820, 14507126, 40987803, 67230935, 100665272, 134217759, 183746233, 201326653,
        234881086, 268435519, 0, 0, 0,
    ),
    (
        10381668, 151161604, 184720200, 229153669, 251834799, 12628426, 16829524, 54580594, 87627187,
        117515223, 7683356, 33554456, 67110494, 100665013, 134331807, 168005431, 201330301, 234884798,
        268439295, 0, 0, 0, 0, 0,
    ),
    (
        10381668, 161513772, 184552045, 229302853, 2821062, 251658283, 13152753, 20005939, 55104849, 87770515,
        117441495, 39966517, 73889718, 100894682, 134217755, 167772220, 201330553, 235122686, 268435515, 0, 0,
        0, 0, 0,
    ),
    (
        1859908, 10783016, 16829093, 11311504, 50332497, 4902695, 150994954, 83887037, 184549421, 134021003,
        218293779, 251659887, 12670612, 40990107, 67110769, 100665266, 134219763, 167775544, 201330041,
        234884538, 268439035, 0, 0, 0,
    ),
    (
        1859908, 2267432, 16778021, 4233642, 50334413, 162574119, 83886094, 11842685, 184549391, 117440512,
        218106814, 12420370, 251745535, 6227353, 13220954, 33556275, 67110772, 100663326, 134217759,
        167772216, 201330293, 235106042, 268435511, 0,
    ),
    (
        10381668, 10715652, 15706745, 2607749, 2649963, 150994988, 3142142, 16778004, 50332501, 83944470,
        129299921, 184549376, 5101330, 33554456, 67110809, 218103854, 100791984, 167772212, 134220891,
        251661679, 201326592, 234884530, 268438775, 0,
    ),
    (
        10381668, 10522116, 1550969, 11516553, 16035590, 16544830, 3228369, 16780332, 150994944, 50332501,
        83944598, 184612333, 117440512, 167890200, 33554451, 67230809, 218105518, 213773659, 100663296,
        251658271, 134217782, 234881074, 268438775, 0,
    ),
    (
        1859908, 20073736, 16146229, 4423606, 2619793, 15105554, 50331661, 3714728, 83886139, 150995692,
        117440527, 5086040, 195380910, 5879151, 218221207, 33554432, 67108893, 167772208, 100842590,
        201326592, 251658271, 134217778, 234881024, 268435507,
    ),
    (
        1859908, 20070964, 16145788, 14457270, 50495373, 14987256, 83886094, 4699194, 5579476, 117441516,
        150994984, 10851859, 184735130, 167775259, 33554460, 225880983, 67108864, 213773041, 100663296,
        251658240, 134220959, 234881024, 268435507, 0,
    ),
)


def kernel(
    n_grp,
    n_blk,
    image_hbm,
    text_hbm,
    image_ids,
    text_ids,
    sharpness,
    offset,
    adjoint,
    grad_image,
    grad_text,
    raw,
    hat,
    buf,
    ids,
    own_ids,
    inverse,
    total,
    load_sem,
    send_sem,
    id_send_sem,
    wrap_sem,
    wrap_id_sem,
    detour_sem,
    ready_sem,
    recv_sem,
    id_recv_sem,
):
    rows = hat.shape[1]
    piece = rows // WAVES
    g = lax.axis_index("grp")
    k = lax.axis_index("blk")
    j = lax.rem(k, RUN)

    loads = [
        pltpu.make_async_copy(text_hbm, raw.at[0], load_sem.at[0]),
        pltpu.make_async_copy(image_hbm, raw.at[1], load_sem.at[1]),
    ]
    for load in loads:
        load.start()

    def device(dg, dk):
        return (lax.rem(g + dg + n_grp, n_grp), lax.rem(k + dk + n_blk, n_blk))

    next_grp = [device(step, 0)[0] for step in (1, -1)]
    next_blk = [device(0, step)[1] for step in (1, -1)]

    barrier = pltpu.get_barrier_semaphore()

    def greet(target):
        pl.semaphore_signal(barrier, inc=1, device_id=target, device_id_type=MESH)

    for target in (device(0, -1), device(1, 0), device(-1, 0)):
        greet(target)

    @pl.when(j != RUN - 1)
    def _():
        greet(device(0, 1))

    even = lax.rem(j, 2) == 0

    @pl.when(even & (j >= 2))
    def _():
        greet(device(0, -2))

    @pl.when(jnp.logical_not(even) & (j <= RUN - 3))
    def _():
        greet(device(0, 2))

    def wrap_target(stream, owner, sender):
        step = 1 - 2 * stream
        return (0 if owner < SPAN else step, step * sender)

    def wrap_links(stream):
        links = [(distance, distance) for distance in range(1, SLOTS - 1)]
        links += [(owner, sender) for which, owner, sender, _, _ in DETOURS if which == stream]
        return sorted({(wrap_target(stream, *link), link[1]) for link in links})

    def others(stream):
        return [link for link in wrap_links(stream) if link[0] != (0, 1 - 2 * stream)]

    @pl.when(j == 0)
    def _():
        for (dg, dk), _ in others(0):
            greet(device(-dg, -dk))

    far_sends = sum([(RUN - j == sender).astype(jnp.int32) for _, sender in others(0)])
    far_sends += jnp.where(j == RUN - 1, len(others(1)), 0) - jnp.where(j == 0, 1, 0)
    ready_count = sum([(j + 1 == sender).astype(jnp.int32) for _, sender in wrap_links(1)])
    for (dg, dk), sender in others(1):

        @pl.when(j + 1 == sender)
        def _():
            greet(device(dg, dk))

    def wrap_distance(stream):
        to_edge = RUN - j if stream == 0 else j + 1
        return to_edge, (to_edge >= 2) & (to_edge <= 6)

    skips = jnp.where(even, j != RUN - 2, j != 1).astype(jnp.int32)
    barrier_count = 4 + skips + far_sends

    @pl.when(j == RUN - 1)
    def _():
        pl.semaphore_wait(barrier, barrier_count)
        for (dg, dk), _ in wrap_links(1):
            pl.semaphore_signal(
                ready_sem, inc=1, device_id=device(-dg, -dk), device_id_type=MESH
            )

    for stream, own in ((0, text_ids), (1, image_ids)):
        loads[stream].wait()
        for c in range(WAVES):
            part = pl.ds(c * piece, piece)
            wide = raw[stream, part, :].astype(jnp.float32)
            inv = lax.rsqrt(jnp.sum(wide * wide, axis=-1, keepdims=True) + EPSILON)
            inverse[stream, part, :] = jnp.broadcast_to(inv, (piece, 128))
            unit = (wide * inv).astype(jnp.bfloat16)
            hat[stream, part, :] = unit
            buf[stream, c, pl.ds(0, piece), :] = unit
            at = c * piece
            line = own[at // 128 : at // 128 + 1, :].astype(jnp.float32)
            line = line[:, at % 128 : at % 128 + piece]
            ids[stream, 0, c] = jnp.concatenate([line] * (128 // piece), axis=1)

    @pl.when(j != RUN - 1)
    def _():
        pl.semaphore_wait(barrier, barrier_count)

    def pick(stream, pair):
        return pair[stream] if isinstance(stream, int) else jnp.where(stream == 0, pair[0], pair[1])

    def route(stream, s, reach):
        place = pick(stream, (j, RUN - 1 - j))
        entry = lax.rem(place, 2) == 0
        fresh = (s == 0) | (s == SPAN)
        if reach == 2:
            goes = entry & (place != RUN - 2) & (fresh | (s == 1) | (s == SPAN + 1))
            return (g, pick(stream, [device(0, step)[1] for step in (2, -2)])), goes
        hop = s == SPAN - 1
        target = (
            jnp.where(hop, pick(stream, next_grp), g),
            jnp.where(hop, k, pick(stream, next_blk)),
        )
        goes = jnp.where(place == RUN - 1, s == 0, entry | fresh)
        return target, (s < SLOTS - 1) & (hop | goes)

    def chunk(stream, s, c):
        at = s * piece
        if not isinstance(at, int):
            at = pl.multiple_of(at, piece)
        return buf.at[stream, c, pl.ds(at, piece)]

    def remote(src, dst, send, recv, target):
        return pltpu.make_async_remote_copy(
            src_ref=src,
            dst_ref=dst,
            send_sem=send,
            recv_sem=recv,
            device_id=target,
            device_id_type=MESH,
        )

    def block_copy(stream, s, c, reach, target):
        return remote(
            chunk(stream, s, c),
            chunk(stream, s + reach, c),
            send_sem.at[reach - 1, stream, s],
            recv_sem.at[stream, s + reach, c],
            target,
        )

    def id_copy(stream, s, reach, target):
        return remote(
            ids.at[stream, s],
            ids.at[stream, s + reach],
            id_send_sem.at[reach - 1, stream, s],
            id_recv_sem.at[stream, s + reach],
            target,
        )

    def forward(stream, s, c):
        for reach in (2, 1):
            target, goes = route(stream, s, reach)

            @pl.when(goes)
            def _():
                @pl.when(c == 0)
                def _():
                    id_copy(stream, s, reach, target).start()

                block_copy(stream, s, c, reach, target).start()

    def receive(stream, s, c):
        target = (g, pick(stream, next_blk))

        @pl.when(c == 0)
        def _():
            id_copy(stream, s - 1, 1, target).wait_recv()

        block_copy(stream, s - 1, c, 1, target).wait_recv()

    def wrap_route(stream):
        to_edge, far = wrap_distance(stream)
        same = to_edge < SPAN
        slot = jnp.where(same, to_edge, to_edge + 1)
        step = 1 - 2 * stream
        return far, slot, device(jnp.where(same, 0, step), step * to_edge)

    def wrap_id_copy(stream):
        _, slot, target = wrap_route(stream)
        return remote(
            ids.at[stream, 0],
            ids.at[stream, slot],
            wrap_id_sem.at[stream],
            id_recv_sem.at[stream, slot],
            target,
        )

    def wrap(stream, c, far):
        _, slot, target = wrap_route(stream)

        @pl.when(far)
        def _():
            remote(
                chunk(stream, 0, c),
                chunk(stream, slot, c),
                wrap_sem.at[stream],
                recv_sem.at[stream, slot, c],
                target,
            ).start()

    def wrap_early(stream):
        to_edge, far = wrap_distance(stream)

        @pl.when(far)
        def _():
            wrap_id_copy(stream).start()

        for c in range(WAVES):
            now = far & (to_edge < PATIENT[stream])
            for which, owner, _, _, waves in DETOURS:
                if which == stream and c in waves:
                    now = now & (to_edge != owner)
            wrap(stream, c, now)

    def wrap_late(other, s, c):
        for stream in range(2):
            to_edge, far = wrap_distance(stream)
            now = far & (to_edge >= PATIENT[stream]) & (other == 1 - stream) & (s == SPAN - 1)
            for which, owner, _, _, waves in DETOURS:
                if which == stream:
                    kept = functools.reduce(jnp.logical_and, [c != wave for wave in waves])
                    now = now & ((to_edge != owner) | kept)
            wrap(stream, c, now)

    def detour_copy(n, c):
        stream, owner, sender, s, _ = DETOURS[n]
        slot = owner if owner < SPAN else owner + 1
        return remote(
            chunk(stream, s, c),
            chunk(stream, slot, c),
            detour_sem.at[n],
            recv_sem.at[stream, slot, c],
            device(*wrap_target(stream, owner, sender)),
        )

    def detour(stream, s, c):
        for n, (which, _, sender, slot, waves) in enumerate(DETOURS):
            place = RUN - sender if which == 0 else sender - 1
            now = functools.reduce(jnp.logical_or, [c == wave for wave in waves])

            @pl.when((stream == which) & (s == slot) & (j == place) & now)
            def _():
                detour_copy(n, c).start()

    for c in range(WAVES):
        forward(0, 0, c)

        @pl.when(j != 0)
        def _():
            forward(1, 0, c)

    wrap_early(0)

    def cross():
        pl.semaphore_wait(ready_sem, ready_count)
        for c in range(WAVES):

            @pl.when(j == 0)
            def _():
                forward(1, 0, c)

        wrap_early(1)

    row = lax.broadcasted_iota(jnp.int32, (128, 128), 0)
    lane = lax.broadcasted_iota(jnp.int32, (128, 128), 1)
    for stream, own in ((0, text_ids), (1, image_ids)):
        for half in range(rows // 128):
            line = jnp.broadcast_to(own[half : half + 1, :].astype(jnp.float32), (128, 128))
            column = jnp.sum(jnp.where(row == lane, line, 0.0), axis=-1, keepdims=True)
            own_ids[stream, pl.ds(half * 128, 128), :] = jnp.broadcast_to(column, (128, 128))
        total[stream] = jnp.zeros(total.shape[1:], jnp.float32)

    scale = jnp.exp(jnp.full((1, 128), sharpness[0], jnp.float32))[:, :1]
    shift = offset[0]
    weight = -(adjoint[0] * scale / rows)
    group = SPAN * piece
    turn = lax.broadcasted_iota(jnp.int32, (1, 128), 1) // piece

    def compute(stream, c, half):
        mine = 1 - stream
        visitors = buf[stream, c, pl.ds(pl.multiple_of(half * group, group), group), :]
        grid = lax.dot_general(
            hat[mine], visitors, (((1,), (1,)), ((), ())), preferred_element_type=jnp.float32
        )
        logit = scale * grid + shift
        column = own_ids[mine, :, :]
        parts = []
        for at in range(0, group, 128):
            s = half * SPAN + at // piece
            line = ids[stream, s, c]
            for other in range(1, 128 // piece):
                line = jnp.where(turn == other, ids[stream, s + other, c], line)
            match = column == jnp.broadcast_to(line, (rows, 128))
            here = logit[:, at : at + 128]
            signed = jnp.where(match, here, -here)
            parts.append(jnp.where(match, weight, -weight) * (1.0 / (1.0 + jnp.exp(signed))))
        coef = jnp.concatenate(parts, axis=1).astype(jnp.bfloat16)
        total[mine] += jnp.dot(coef, visitors, preferred_element_type=jnp.float32)

    words = []
    line = lax.rem(g, LINE)
    turn_at = 2 * j + lax.div(k, RUN)
    for i in range(len(ORDER[0])):
        word = jnp.int32(0)
        for row in reversed(range(LINE)):
            entries = [ORDER[row * 2 * RUN + place][i] for place in range(2 * RUN)]
            entry = jnp.int32(entries[0])
            for place in range(1, 2 * RUN):
                if entries[place] != entries[place - 1]:
                    entry = jnp.where(turn_at >= place, entries[place], entry)
            word = entry if row == LINE - 1 else jnp.where(line == row, entry, word)
        words.append(word)

    def step(i, carry):
        word = words[0]
        for other in range(1, len(words)):
            word = jnp.where(i == other, words[other], word)

        @pl.when(lax.rem(word, 64) == 1)
        def _():
            cross()

        for _ in range(4):
            entry = lax.rem(word, 64)
            word = lax.div(word, 64)
            stream = lax.div(entry, 32)
            s = lax.rem(lax.div(entry, 4), 8)
            c = lax.rem(entry, 4)

            @pl.when(entry > 1)
            def _():
                receive(stream, s, c)
                forward(stream, s, c)
                wrap_late(stream, s, c)
                detour(stream, s, c)

        @pl.when(word > 0)
        def _():
            product = word - 1
            compute(lax.div(product, 8), lax.div(lax.rem(product, 8), 2), lax.rem(product, 2))

        return carry

    lax.fori_loop(0, len(words), step, 0)

    for stream, out in ((1, grad_image), (0, grad_text)):
        for c in range(WAVES):
            part = pl.ds(c * piece, piece)
            inv = inverse[stream, part, :][:, :1]
            unit = raw[stream, part, :].astype(jnp.float32) * inv
            grad = total[stream, part, :]
            along = jnp.sum(unit * grad, axis=-1, keepdims=True)
            out[part, :] = inv * (grad - unit * along)

    for stream in range(2):
        for s in range(SLOTS - 1):
            for reach in (2, 1):
                target, goes = route(stream, s, reach)

                @pl.when(goes)
                def _():
                    id_copy(stream, s, reach, target).wait_send()
                    remote(
                        hat.at[stream],
                        hat.at[stream],
                        send_sem.at[reach - 1, stream, s],
                        recv_sem.at[stream, s + 1, 0],
                        target,
                    ).wait_send()

        far, slot, target = wrap_route(stream)

        @pl.when(far)
        def _():
            wrap_id_copy(stream).wait_send()

        for distance in range(2, SLOTS - 1):
            away = [len(d[4]) for d in DETOURS if d[0] == stream and d[1] == distance]
            amount = rows - piece * sum(away)
            if amount:

                @pl.when(wrap_distance(stream)[0] == distance)
                def _():
                    part = hat.at[stream, pl.ds(0, amount)]
                    remote(
                        part, part, wrap_sem.at[stream], recv_sem.at[stream, slot, 0], target
                    ).wait_send()

    for n, (stream, _, sender, _, waves) in enumerate(DETOURS):

        @pl.when(j == (RUN - sender if stream == 0 else sender - 1))
        def _():
            part = hat.at[stream, pl.ds(0, piece * len(waves))]
            target = device(0, 1 - 2 * stream)
            remote(
                part, part, detour_sem.at[n], recv_sem.at[stream, 1, 0], target
            ).wait_send()


def body(n_grp, n_blk, image_emb, text_emb, image_pair_index, text_ids, sharpness, offset, adjoint):
    rows, width = image_emb.shape
    vmem = pl.BlockSpec(memory_space=pltpu.VMEM)
    smem = pl.BlockSpec(memory_space=pltpu.SMEM)
    hbm = pl.BlockSpec(memory_space=pltpu.HBM)
    flops = 4 * SLOTS * 2 * rows * rows * width
    return pl.pallas_call(
        functools.partial(kernel, n_grp, n_blk),
        out_shape=(
            jax.ShapeDtypeStruct((rows, width), jnp.float32),
            jax.ShapeDtypeStruct((rows, width), jnp.float32),
        ),
        in_specs=[hbm, hbm, vmem, vmem, smem, smem, smem],
        out_specs=(vmem, vmem),
        scratch_shapes=[
            pltpu.VMEM((2, rows, width), jnp.bfloat16),
            pltpu.VMEM((2, rows, width), jnp.bfloat16),
            pltpu.VMEM((2, WAVES, SLOTS * rows // WAVES, width), jnp.bfloat16),
            pltpu.VMEM((2, SLOTS, WAVES, 1, 128), jnp.float32),
            pltpu.VMEM((2, rows, 128), jnp.float32),
            pltpu.VMEM((2, rows, 128), jnp.float32),
            pltpu.VMEM((2, rows, width), jnp.float32),
            pltpu.SemaphoreType.DMA((2,)),
            pltpu.SemaphoreType.DMA((2, 2, SLOTS)),
            pltpu.SemaphoreType.DMA((2, 2, SLOTS)),
            pltpu.SemaphoreType.DMA((2,)),
            pltpu.SemaphoreType.DMA((2,)),
            pltpu.SemaphoreType.DMA((max(1, len(DETOURS)),)),
            pltpu.SemaphoreType.REGULAR,
            pltpu.SemaphoreType.DMA((2, SLOTS, WAVES)),
            pltpu.SemaphoreType.DMA((2, SLOTS)),
        ],
        compiler_params=pltpu.CompilerParams(
            collective_id=0, has_side_effects=True, vmem_limit_bytes=60 * 1024 * 1024
        ),
        cost_estimate=pl.CostEstimate(
            flops=flops, bytes_accessed=12 * rows * width, transcendentals=2 * SLOTS * rows * rows
        ),
    )(
        image_emb,
        text_emb,
        image_pair_index.reshape(rows // 128, 128),
        text_ids.reshape(rows // 128, 128),
        sharpness,
        offset,
        adjoint,
    )


def solution(mesh):
    both = ("grp", "blk")
    return jax.shard_map(
        functools.partial(body, mesh.shape["grp"], mesh.shape["blk"]),
        mesh=mesh,
        in_specs=(P(both, None), P(both, None), P(both), P(both), P(), P(), P()),
        out_specs=(P(both, None), P(both, None)),
        check_vma=False,
    )
```

```python
import functools

import jax
import jax.numpy as jnp
from jax import lax
from jax.experimental import pallas as pl
from jax.experimental.pallas import tpu as pltpu
from jax.sharding import PartitionSpec as P

MESH = pl.DeviceIdType.MESH
EPSILON = 1e-06

SPAN = 4
SLOTS = 8
LINE = 4
PATIENT = (7, 2)
RUN = 16
WAVES = 4
DETOURS = (
)


ORDER = (
    (
        10639617, 10394406, 11111341, 150994991, 184549376, 218219307, 251761156, 16777216, 1543181, 3791945,
        50331700, 4259418, 15245746, 13452412, 2078645, 16102731, 16381366, 83889623, 167772223, 33554432,
        117440512, 67108864, 201326610, 234881024, 268435456, 100663315, 134217728,
    ),
    (
        10115329, 10910504, 150994989, 184722990, 218106844, 5293675, 251661341, 14789717, 15038358, 3536626,
        15416590, 1293647, 16777224, 167809404, 53022534, 201548487, 33554432, 83890065, 117440512, 67108882,
        235107583, 100663296, 134217728, 268435456, 0, 0, 0,
    ),
    (
        1859908, 9865473, 11430569, 151177692, 184549421, 221368878, 16777216, 2558964, 251907405, 50331678,
        168002870, 14478410, 84137493, 4242617, 8381401, 16725690, 201569371, 33554432, 117440512, 234881024,
        67108864, 268435456, 100664722, 134218967, 0, 0, 0,
    ),
    (
        1859908, 9865473, 11430569, 151177692, 12011037, 184551321, 7269722, 14354384, 218103855, 251658240,
        2346481, 167825272, 16777216, 204969033, 13165834, 65601419, 15725906, 33557718, 83887571, 117440512,
        234881024, 67108864, 100663296, 268435456, 134217728, 0, 0,
    ),
    (
        2380292, 6, 11700481, 10005349, 12229063, 151190155, 184552176, 218103857, 251658240, 13683896,
        16780537, 64544437, 6540795, 168022928, 84141849, 201326592, 240243711, 268435456, 117442449,
        33554432, 67110239, 106509970, 134219227, 0, 0, 0, 0,
    ),
    (
        2380292, 11700481, 11952549, 150995623, 3072489, 184549424, 218299498, 251661483, 7720184, 14020212,
        8351376, 15957716, 167772177, 201326653, 16854924, 234881024, 5070797, 50331662, 268436440, 83886080,
        33554432, 117440512, 67110486, 100663322, 134219227, 0, 0,
    ),
    (
        1859908, 9476616, 41, 9741057, 16779917, 11428747, 50332624, 84067431, 122608914, 151215150,
        184552559, 218312502, 251662199, 168005555, 216614713, 234881024, 268558079, 33554456, 67110485,
        107575190, 134219487, 0, 0, 0, 0, 0, 0,
    ),
    (
        1859908, 2568, 2507521, 2773865, 2943632, 4633574, 16780071, 50331666, 83886080, 117626100, 150994944,
        184549422, 218107248, 251661297, 5491894, 6504311, 167772216, 201330617, 234884757, 268678591,
        33670617, 67110746, 100663326, 134219487, 0, 0, 0,
    ),
    (
        1206628, 11555367, 27145, 1878849, 150998057, 195611531, 13022063, 16777236, 5713422, 6264207,
        218107088, 50405044, 251658293, 83886134, 4947771, 117441789, 167772160, 201326654, 234881087,
        268435456, 33556248, 67110745, 100787930, 134217759, 0, 0, 0,
    ),
    (
        10381668, 516, 11571521, 162834950, 187632199, 3230634, 230480625, 13337493, 16844175, 64175703,
        251731322, 83886080, 6534326, 117440572, 168025555, 201330588, 33554432, 234881087, 268435456,
        74823321, 100663326, 134217759, 0, 0, 0, 0, 0,
    ),
    (
        1859908, 9476616, 41, 2675457, 16777253, 60339114, 10291919, 4934417, 83888984, 129604947, 12778906,
        13092564, 14888789, 150998263, 184553401, 6270934, 218103867, 251658240, 167772160, 201326592,
        234881024, 268435456, 33554460, 67108893, 100663326, 134217759, 0,
    ),
    (
        1859908, 8, 16941825, 10803465, 3737930, 4503978, 50331663, 4819687, 83889452, 117544173, 12668270,
        7302106, 150998833, 14507890, 184549432, 16487859, 218342876, 251662079, 167772160, 201326592,
        33554432, 234881024, 268435456, 67108893, 100663326, 134217759, 0,
    ),
    (
        1206628, 11555367, 11960713, 10779658, 150997899, 11066444, 184549423, 22227662, 4283919, 6003932,
        6268788, 50457937, 8228283, 16217276, 218359001, 84000730, 251658240, 117440512, 33554432, 167772160,
        201326592, 67108864, 234881024, 100663296, 268435456, 134217728, 0,
    ),
    (
        9980260, 11555367, 2648585, 150994989, 12227056, 184549387, 12403498, 13163249, 218103829, 16870926,
        15152143, 251754292, 50572637, 4679228, 83886110, 14495455, 6897497, 117440574, 167776219, 33554432,
        67108864, 201326592, 100663296, 234881024, 134217728, 268435456, 0,
    ),
    (
        1859908, 2411016, 16946020, 61409610, 4518606, 83888870, 117517095, 151180852, 6745427, 12543280,
        184552538, 218103808, 7310834, 251658261, 5885555, 49117050, 67108864, 100663326, 134217759,
        167772220, 201326653, 234881086, 268435519, 0, 0, 0, 0,
    ),
    (
        1859908, 9488904, 16833097, 2794533, 3979662, 50494161, 13708056, 83965549, 12801710, 13067567,
        117648923, 150994944, 5715767, 184549433, 218103808, 6149562, 251662046, 33554432, 67108895,
        100663296, 134217728, 167772220, 201326653, 234881086, 268435519, 0, 0,
    ),
    (
        10381668, 1491460, 163764745, 12227206, 11058247, 184549423, 229428372, 16778069, 251717043, 50332660,
        90133532, 122119709, 6780062, 33554463, 67110547, 100663323, 134217728, 167775804, 201584253,
        234881082, 268439295, 0, 0, 0, 0, 0, 0,
    ),
    (
        10381668, 10521348, 163762757, 2810281, 12890602, 3230447, 184604018, 218103808, 265241494, 16840144,
        7675228, 6367158, 56965111, 83886106, 117440539, 33554432, 67108864, 100663296, 134217728, 167775804,
        201330553, 234885050, 268439547, 0, 0, 0, 0,
    ),
    (
        1859908, 9486888, 26530409, 4252330, 3980006, 50334503, 83987281, 129864878, 163949587, 184549376,
        218217620, 251658240, 33643740, 67110742, 100665239, 134217759, 15965496, 167772213, 217046458,
        234885047, 268435519, 0, 0, 0, 0, 0, 0,
    ),
    (
        1859908, 3180840, 16777257, 3447461, 11314214, 4504014, 4903916, 50334616, 88972335, 7162970,
        150996338, 117440512, 184549427, 218105622, 251658240, 33556311, 67239710, 100663296, 134470968,
        182185589, 201326650, 234881087, 268439287, 0, 0, 0, 0,
    ),
    (
        10381668, 1346308, 151034728, 184552006, 3072647, 218106858, 16779980, 251659092, 50331662, 83887439,
        117442326, 6416215, 7186015, 33554448, 71814196, 115545269, 167772160, 148582227, 16481529, 201326650,
        234881024, 268439547, 0, 0, 0, 0, 0,
    ),
    (
        10381668, 1491460, 150994984, 10773101, 2915210, 184549418, 5419823, 218103821, 16777216, 251659598,
        50331648, 83887503, 117440540, 6415837, 7063135, 12836379, 167772212, 14150777, 201326650, 235105471,
        268664059, 33554448, 67108881, 100663314, 134217747, 0, 0,
    ),
    (
        1859908, 3293736, 16777257, 61397321, 3062154, 4355022, 83886124, 12422061, 117440529, 150994944,
        184549401, 218103834, 251658240, 7984923, 12661919, 33785148, 67323249, 181116758, 15414773,
        100667318, 201330423, 134217728, 234881024, 268435519, 0, 0, 0,
    ),
    (
        1859908, 3293736, 16777257, 3582281, 50334090, 3978155, 83888935, 129862573, 150994969, 184549376,
        218103834, 251658240, 7833371, 12709492, 13086047, 4402934, 4928631, 167772220, 33555731, 67108885,
        201328061, 100663296, 134221719, 234881087, 268435456, 0, 0,
    ),
    (
        10381668, 151161604, 1479213, 184549422, 12497514, 218103814, 251658240, 5288394, 16777228, 50332501,
        83886094, 117440527, 8251228, 4689680, 16065972, 6370800, 16473209, 183082418, 33664499, 201326592,
        67108864, 234885083, 100663296, 134217787, 268435456, 0, 0,
    ),
    (
        10381668, 150997548, 195330349, 11467438, 218104389, 251658240, 2912902, 16777228, 13829005, 50331663,
        91708508, 125775262, 5492211, 167772216, 5837845, 5055997, 201328185, 33556094, 15726266, 67108891,
        234881024, 100663296, 268435456, 134217728, 0, 0, 0,
    ),
    (
        1859908, 10783016, 10013349, 16777225, 11590375, 50335498, 162837518, 83886080, 191091694, 218103855,
        117440537, 251658240, 14757777, 5702964, 167882323, 7282006, 16633495, 201330098, 33554432, 234882931,
        67108864, 100667102, 134221279, 268435456, 0, 0, 0,
    ),
    (
        1859908, 9869608, 10011178, 16779755, 50385532, 84136842, 151057132, 117440512, 184552493, 218106990,
        251915439, 4686899, 167772212, 6812824, 6905428, 215312083, 33670650, 14661494, 234881054, 67108864,
        268435487, 100663296, 134217728, 0, 0, 0, 0,
    ),
    (
        10381668, 10506756, 11049592, 2801222, 3124999, 167988244, 16777228, 13950805, 50334800, 201328014,
        14339215, 84001915, 117440512, 6366685, 5086078, 13479390, 158203886, 33554432, 234881071, 184549376,
        67108864, 100663296, 218103808, 268435456, 134217728, 251658240, 0,
    ),
    (
        10381668, 10915448, 11043132, 15381061, 151175814, 3191293, 12643597, 16777231, 50331648, 89197438,
        13980795, 167772223, 117440540, 7693489, 5204888, 184549426, 12531609, 208270839, 33554459, 218103808,
        234881024, 67108864, 251658240, 268435456, 100663296, 134217728, 0,
    ),
    (
        1859908, 30460168, 10116873, 50332533, 87808458, 14222072, 16450513, 117442066, 167772160, 208082169,
        14625300, 11624410, 11909754, 7812886, 15657623, 150994974, 235010799, 184549376, 33554432, 67108864,
        218103808, 268435456, 100663296, 251658240, 134217728, 0, 0,
    ),
    (
        1859908, 9658164, 10214949, 16777992, 3448231, 15000232, 50331710, 83887051, 117440512, 167775248,
        16753772, 150994985, 12930514, 5584443, 201328237, 184549376, 5974702, 6147034, 218107115, 234881053,
        33554432, 251660187, 268435487, 67108864, 100663296, 134217728, 0,
    ),
    (
        10115329, 10930727, 151186093, 184549679, 218103808, 18264588, 251658240, 2675081, 50363448, 6493451,
        83945268, 13462677, 13956729, 117440541, 15328919, 15595254, 167775740, 33558352, 201326592, 67112849,
        234881024, 100667346, 268435475, 134217728, 0, 0, 0,
    ),
    (
        10115329, 11979303, 150994985, 184549422, 230457642, 251661012, 1412208, 14718741, 7704982, 3240626,
        31935696, 33554432, 4580186, 50332814, 71087303, 83886080, 100667061, 117440512, 134348507, 167775676,
        201326653, 235142654, 268435456, 0, 0, 0, 0,
    ),
    (
        1859908, 9865473, 11446697, 3328456, 150994953, 16777216, 198222701, 50331648, 83934222, 7529999,
        117440528, 218103808, 7019865, 14269405, 267459742, 8338999, 167772221, 201326649, 49013908,
        234881024, 67354581, 268436694, 100663296, 134217751, 0, 0, 0,
    ),
    (
        1859908, 10914049, 11430565, 16826919, 150997784, 2463540, 50331661, 184551085, 7276362, 83887029,
        5855124, 4027118, 230493617, 13180727, 15194104, 117444498, 5242106, 33554491, 251658240, 67108864,
        167772160, 201326592, 100663296, 234881024, 134217728, 268435456, 0,
    ),
    (
        2380292, 6, 11700481, 10934602, 154040711, 184552110, 218103808, 3324912, 251658289, 13426226,
        16780916, 50335054, 83886080, 117662714, 5471964, 4321053, 168028157, 201327999, 234881041, 268435456,
        33555986, 67212502, 100663322, 134219479, 0, 0, 0,
    ),
    (
        20996, 11682369, 10381861, 10791750, 12255943, 150994986, 184552433, 218156203, 251658240, 16989724,
        50386804, 15423417, 83886094, 6516447, 167772220, 215996057, 121749391, 234882367, 268435456,
        33555793, 67108882, 100664534, 134217751, 0, 0, 0, 0,
    ),
    (
        1859908, 2509320, 152233, 11064065, 20755366, 50334187, 83886124, 117440512, 150994944, 184552749,
        218323888, 266007601, 14664818, 5233874, 168005528, 201326649, 234884756, 268439547, 40985945,
        67229146, 100663326, 134219739, 0, 0, 0, 0, 0,
    ),
    (
        1859908, 150024, 10785537, 16779597, 50331648, 4367242, 95220454, 117440551, 155639084, 184549376,
        223042480, 251882607, 13336339, 167775805, 13606812, 217968285, 234964987, 268435480, 33554432,
        67110485, 100771286, 134217755, 0, 0, 0, 0, 0,
    ),
    (
        10381668, 2380292, 27180, 2019969, 150995689, 11209612, 11332557, 184552527, 16780472, 218103865,
        50331648, 84102835, 251658240, 117665108, 173526523, 217935805, 234882524, 268435456, 33555984,
        67213137, 7185618, 100663326, 134217759, 0, 0, 0, 0,
    ),
    (
        10381668, 2380292, 10513153, 10779466, 150995696, 184601514, 11465556, 218104753, 16777231, 50334904,
        251658240, 13583737, 83889530, 117440534, 168021750, 201577975, 234881086, 268435519, 7439440,
        33658066, 67108893, 100787930, 134217759, 0, 0, 0, 0,
    ),
    (
        1859908, 9476616, 3576577, 16779594, 3041934, 50331663, 83888619, 117443884, 150998381, 184549422,
        234032559, 251866993, 14892504, 15438910, 168017881, 201327706, 234881024, 268435456, 7423131,
        33554451, 67110741, 100787670, 134217759, 0, 0, 0, 0,
    ),
    (
        1859908, 2568, 2507521, 9742925, 3041934, 27177999, 62343960, 96660817, 12950518, 117440572,
        150994944, 16223730, 184549402, 4976243, 218363642, 251659515, 167772160, 201326592, 234881024,
        268435456, 33670484, 67229142, 100663326, 134217759, 0, 0, 0,
    ),
    (
        9980260, 11555367, 150997513, 2019974, 197323339, 3611276, 3992303, 16780850, 218107472, 65752273,
        251658293, 83886080, 15715730, 131940188, 184407358, 201326592, 234881024, 268435456, 5895518,
        33554456, 67110487, 100663322, 134217755, 0, 0, 0, 0,
    ),
    (
        9980260, 11555367, 150997513, 12767878, 196655687, 3611276, 5450479, 16777230, 218107407, 50541596,
        15418745, 15848565, 16068342, 251782391, 83886142, 117440512, 167900607, 201326592, 234881024,
        268435479, 33554456, 67108889, 100663322, 134217755, 0, 0, 0,
    ),
    (
        1859908, 26266120, 50500425, 2689701, 83888526, 11334353, 131148583, 12276973, 12545044, 150998101,
        184549376, 218103808, 251887154, 15414713, 183602903, 49661593, 201326592, 67110747, 234881086,
        100663326, 268437503, 134217728, 0, 0, 0, 0, 0,
    ),
    (
        1859908, 26266120, 50500425, 2794533, 2955662, 4881103, 83886124, 122522484, 12778862, 151199124,
        14650521, 184549397, 218107507, 251658240, 15705558, 167772220, 201330522, 234999707, 33554495,
        268435456, 67108893, 100663326, 134217759, 0, 0, 0, 0,
    ),
    (
        10381668, 161516292, 12767813, 2812486, 184549418, 12368967, 223552299, 251659093, 16777216, 4404622,
        50426868, 6772241, 83887286, 117440512, 7187923, 33785660, 167772221, 201328505, 67108864, 100902846,
        234881024, 134221791, 268435515, 0, 0, 0, 0,
    ),
    (
        10381668, 161516292, 12767813, 184738217, 218135178, 11465457, 251710612, 16778069, 13692118,
        13956560, 50332764, 7679384, 5207676, 91215544, 117440512, 33554489, 67108926, 167775902, 201326592,
        100907007, 234881024, 134217728, 268435456, 0, 0, 0, 0,
    ),
    (
        1859908, 3180840, 16777257, 3447461, 3712038, 2955755, 4903916, 50525742, 83886080, 7013971,
        151108692, 7720085, 117441971, 184549399, 218107422, 251661599, 33554432, 67108921, 100663296,
        134217728, 15691445, 167776055, 201326653, 234881086, 268435519, 0, 0,
    ),
    (
        1859908, 3180840, 16777257, 3447461, 50332710, 3046090, 11868942, 88705935, 150994991, 6895216,
        13219121, 13487637, 184550836, 15826525, 15334750, 117444029, 218361339, 251658303, 33554432,
        67108864, 167772160, 100663296, 134217728, 201326592, 234881024, 268435456, 0,
    ),
    (
        10381668, 1491460, 150994984, 2648905, 184552361, 218276551, 16956364, 3756884, 259064790, 50403159,
        83886110, 117442066, 33558303, 7030355, 67110640, 100663296, 134221181, 13332401, 184520179,
        201326649, 234884858, 268435456, 0, 0, 0, 0, 0,
    ),
    (
        10381668, 1491460, 150994984, 2648905, 184552361, 218276551, 5422028, 16777229, 251658240, 3999054,
        50331670, 13829980, 83887228, 117442455, 14095890, 5111672, 33554457, 13344154, 14628606, 167776250,
        67108923, 100663296, 201326592, 134217728, 234881024, 268435456, 0,
    ),
    (
        1859908, 3293736, 16777257, 3582281, 50334090, 10400656, 95491019, 117443501, 151070255, 184550617,
        218105114, 251658240, 7570779, 33557526, 67110743, 100663326, 134422111, 13843642, 168021371,
        201580022, 234881086, 268435519, 0, 0, 0, 0, 0,
    ),
    (
        1859908, 3293736, 16777257, 3582281, 3737994, 3979755, 50517100, 96306350, 12666451, 117444122,
        150994944, 184549376, 7294037, 218219961, 251658240, 15424663, 33554461, 8350942, 67108923, 100663351,
        134217728, 167772220, 201326653, 234881086, 268435519, 0, 0,
    ),
    (
        10381668, 1491460, 150994984, 196514185, 2026122, 218103819, 251710191, 16777236, 50333005, 83886094,
        117654486, 4314588, 15800245, 33629750, 67212511, 100663322, 134220827, 13311485, 167772216,
        201564083, 234885114, 268435515, 0, 0, 0, 0, 0,
    ),
    (
        10381668, 10666500, 150994949, 196776557, 218106502, 251837386, 3228359, 16866356, 56302925, 97059766,
        14480471, 6367027, 117520285, 33554432, 15837145, 67108891, 100663296, 134217728, 167775805,
        201330302, 234884799, 268435515, 0, 0, 0, 0, 0,
    ),
    (
        1859908, 20072968, 3578185, 50375082, 3046094, 83888911, 117541756, 163422062, 184659888, 218103808,
        251658240, 4658896, 13337919, 39437461, 67228887, 8339038, 100663348, 134217728, 167772160, 201330042,
        234884854, 268435511, 0, 0, 0, 0, 0,
    ),
    (
        1859908, 3293736, 16777257, 3582281, 50331686, 11577835, 3071758, 12651407, 155647832, 83886080,
        191358129, 117440512, 218103858, 251659482, 5766356, 33670555, 67340119, 100663326, 134217759,
        167775545, 201330042, 234884539, 268435511, 0, 0, 0, 0,
    ),
    (
        10381668, 2380292, 14723590, 11055593, 16778041, 50332523, 150997818, 97760188, 184553325, 218107822,
        117441492, 5622837, 167772176, 4715933, 12920727, 5110774, 201533016, 258946743, 33554432, 67108864,
        234881024, 100663296, 268435456, 134217728, 0, 0, 0,
    ),
    (
        10381668, 1475076, 11178616, 2798009, 153078586, 196599499, 16778004, 16307566, 5836079, 218104910,
        4191698, 63035155, 251876894, 83886080, 14358489, 117440538, 167775387, 33558003, 67108864, 201326592,
        100663296, 134217728, 234881024, 268435456, 0, 0, 0,
    ),
    (
        1859908, 16777992, 13779785, 50332348, 83887013, 16210315, 117440527, 16476711, 150998572, 180542975,
        184553065, 218344362, 201428048, 5349073, 12408466, 251739307, 234882459, 268553431, 33554461,
        67110878, 100663296, 134217728, 0, 0, 0, 0, 0,
    ),
    (
        1859908, 16777992, 9739556, 64381820, 14200679, 83886094, 151177784, 14603006, 117441551, 4627385,
        184549423, 229213375, 12688122, 251658259, 167772160, 5748372, 214267606, 33676444, 234884318,
        67108895, 100663296, 268435456, 134217728, 0, 0, 0, 0,
    ),
    (
        10115329, 10930727, 151169965, 184549376, 218296588, 16954184, 251658245, 62952340, 3958321, 33761040,
        2838037, 13488601, 83886102, 6913401, 117441246, 14284538, 67110011, 167775740, 201327805, 100663358,
        234882303, 268435456, 134217728, 0, 0, 0, 0,
    ),
    (
        10115329, 11959080, 150994985, 184549422, 218276612, 16970253, 251679659, 50332239, 83930630,
        117486855, 13720688, 5885080, 15160912, 33555549, 7959706, 67108922, 100663296, 8337147, 167773436,
        134221686, 201326592, 234881086, 268439039, 0, 0, 0, 0,
    ),
    (
        1859908, 9865473, 11430569, 28363208, 150994944, 50386441, 5456540, 184549421, 7662617, 13034229,
        83887130, 13301659, 218104822, 33554432, 251885564, 117440512, 15031544, 167776081, 67108922,
        216868286, 234882303, 100663319, 268435456, 134217728, 0, 0, 0,
    ),
    (
        1859908, 10914049, 11430565, 16828872, 150997769, 50334989, 83886986, 117503499, 7443504, 184549421,
        7033969, 38463316, 218105206, 14542255, 67112731, 13187064, 251756157, 100663296, 167772160, 15728318,
        201326643, 134217728, 234881024, 268435456, 0, 0, 0,
    ),
    (
        2380292, 10633601, 2808172, 151165414, 195748551, 218103808, 13024240, 251658252, 16777266, 4251187,
        50331700, 4677212, 99313166, 4963805, 117567247, 168024020, 33555710, 201326655, 234881024, 268435456,
        67110233, 100664730, 134219479, 0, 0, 0, 0,
    ),
    (
        2380292, 11700481, 10250661, 151165770, 12772039, 184549418, 218103808, 13300529, 16777259, 251658240,
        64020019, 84104121, 117441488, 5465914, 4701661, 167772220, 207742333, 6647698, 38663871, 234882775,
        67108864, 268435456, 100663296, 134217728, 0, 0, 0,
    ),
    (
        1859908, 2509320, 41, 26530561, 60466058, 83952587, 117440555, 150997799, 184765265, 4803504,
        218106997, 5729266, 266325212, 183993747, 201330302, 33558168, 234979071, 268435456, 67110493,
        100664990, 134219739, 0, 0, 0, 0, 0, 0,
    ),
    (
        1859908, 150024, 16777985, 60199753, 10134410, 83948240, 117440555, 151176295, 184736820, 230366546,
        12529044, 6540787, 251658296, 168007037, 15308030, 16608988, 201451354, 234881047, 33554459,
        268435487, 67108864, 100663296, 134217728, 0, 0, 0, 0,
    ),
    (
        10381668, 2380292, 44, 151159169, 2915146, 184549417, 12774028, 16777229, 5446635, 218103822,
        50564239, 251659600, 83889465, 117440512, 6503802, 15801750, 167772219, 201578103, 234881086,
        268435519, 5076626, 33554460, 67110747, 100663326, 134217759, 0, 0,
    ),
    (
        10381668, 516, 11571521, 151159430, 11965127, 184549424, 3598988, 16777265, 3865300, 232870898,
        63937808, 265907893, 99454460, 117440573, 167772160, 201330577, 234882879, 268435456, 33554432,
        73258578, 100743066, 134219739, 0, 0, 0, 0, 0,
    ),
    (
        1859908, 9476616, 27579137, 50334026, 11166603, 83887119, 117443303, 162893100, 12774737, 184550996,
        234036214, 251658240, 14651250, 167773852, 5582771, 33554489, 201566079, 67108923, 234881024,
        268435456, 100787603, 134346203, 0, 0, 0, 0, 0,
    ),
    (
        1859908, 8, 16941825, 50479945, 3840330, 11166416, 83886095, 117443051, 151066156, 184552749,
        224877614, 14359508, 251911356, 13446682, 175349687, 201326592, 33558207, 234882427, 268435475,
        67110742, 100665243, 134219735, 0, 0, 0, 0, 0,
    ),
    (
        9980260, 11555367, 150997513, 10932870, 12104176, 184550186, 218307533, 5450446, 24186383, 13844049,
        4806202, 15973725, 14542070, 50331709, 83886080, 251750014, 117440575, 33554432, 167772160, 201326592,
        234881024, 67108864, 268435456, 100664983, 134219487, 0, 0,
    ),
    (
        9980260, 11555367, 150997513, 2019974, 12630953, 13038378, 184603947, 222268558, 4429148, 15415156,
        32314933, 7941942, 5848951, 251658302, 50331711, 83886080, 117440537, 33554432, 167772160, 201326592,
        234881047, 268435456, 67108864, 100663322, 134219487, 0, 0,
    ),
    (
        1859908, 26266120, 4363081, 50331685, 10134410, 95220433, 117443026, 6479148, 150994963, 12668270,
        184771951, 218103857, 6780732, 251751608, 33791229, 167775895, 201326592, 241819579, 67108864,
        100665243, 134217759, 268435519, 0, 0, 0, 0, 0,
    ),
    (
        1859908, 26266120, 50500425, 2795856, 83888526, 11342795, 117440551, 13730988, 150994989, 12663733,
        5348783, 184549425, 218103863, 257281586, 33647865, 15574522, 67108893, 100665243, 167772220,
        201326653, 134221727, 234881024, 268435519, 0, 0, 0, 0,
    ),
    (
        10381668, 161516292, 10932805, 2810288, 184549418, 12893127, 231261483, 14889813, 4408214, 251723351,
        23287569, 50435254, 15324378, 83886135, 117440512, 33554459, 67108864, 100663326, 134467295,
        167772160, 201326653, 234881086, 268435519, 0, 0, 0, 0,
    ),
    (
        10381668, 161516292, 10932805, 2810288, 184549418, 221183047, 251661012, 3494706, 16777267, 50332566,
        7406580, 7675223, 6630808, 83993847, 117440512, 33556379, 67108864, 100663296, 134219768, 183746233,
        201326653, 234881086, 268435519, 0, 0, 0, 0,
    ),
    (
        1859908, 3180840, 16777257, 3447461, 50332710, 10400650, 4113105, 83886125, 151184914, 130128884,
        15947411, 184661297, 16108693, 225916342, 251660183, 33554432, 67108895, 100663296, 134217728,
        182681598, 201326649, 234881082, 268435515, 0, 0, 0, 0,
    ),
    (
        1859908, 3180840, 16777257, 3447461, 50331686, 3847178, 4113127, 83888977, 163392408, 5090329,
        130659633, 5977877, 184549405, 218103831, 251658270, 33554432, 67108895, 100663296, 134217728,
        14146876, 14679486, 167772216, 201326649, 234881082, 268435515, 0, 0,
    ),
    (
        10381668, 1491460, 150994984, 2648905, 184552361, 230859463, 28132143, 3759181, 255684112, 7808785,
        58293842, 84014611, 117440537, 33554458, 67108891, 100663296, 134217786, 16203516, 167772212,
        201326645, 234884542, 268439039, 0, 0, 0, 0, 0,
    ),
    (
        10381668, 1491460, 150994984, 2648905, 184552361, 218276551, 16780236, 50416333, 251658254, 83952597,
        117441948, 6153309, 33555986, 67213267, 100663322, 134217755, 15146544, 15679154, 167775548,
        201330549, 251625398, 268435456, 0, 0, 0, 0, 0,
    ),
    (
        1859908, 3293736, 16777257, 3582281, 50399626, 4618958, 4899787, 84076077, 117440512, 157762799,
        190273172, 218103830, 251658267, 33556247, 67108893, 100663326, 134221215, 15191544, 167772208,
        15675057, 201330547, 234881086, 268435519, 0, 0, 0, 0,
    ),
    (
        1859908, 3293736, 16777257, 3582281, 50334090, 84063246, 11695051, 4909905, 117443544, 150994944,
        191444249, 218103808, 251658240, 40986325, 67110743, 100663326, 134217759, 14642548, 13093944,
        167772217, 16203442, 201326651, 234881086, 268435519, 0, 0, 0,
    ),
    (
        10381668, 1491460, 150994984, 10775369, 184722094, 11471815, 218103819, 251658260, 16866380, 50331661,
        83886998, 4519376, 117517468, 7818451, 33554456, 13999646, 74315452, 167772214, 100666877, 134217728,
        201564158, 234881082, 268435515, 0, 0, 0, 0,
    ),
    (
        10381668, 161516292, 10932805, 184593286, 11317738, 218103855, 251658252, 16778509, 50331648,
        83887438, 117556623, 33555984, 4838487, 5085104, 67108913, 100791986, 134219507, 168005428, 15167349,
        201326647, 234884798, 268439295, 0, 0, 0, 0, 0,
    ),
    (
        1859908, 3293736, 16777257, 3582281, 50373670, 94286926, 4180747, 150994962, 12311384, 117440537,
        191622099, 218103808, 251658303, 5854932, 7554544, 33558065, 167772189, 8363166, 67108915, 100663296,
        134217786, 201330043, 234881078, 268435511, 0, 0, 0,
    ),
    (
        1859908, 10783016, 16777228, 3447461, 50331686, 95318922, 133350347, 150994989, 16059288, 4912217,
        16594622, 184551188, 218103808, 251659611, 33554432, 67204950, 100663326, 134220831, 167775544,
        14102129, 201326643, 234884538, 268439035, 0, 0, 0, 0,
    ),
    (
        10381668, 2380292, 1743416, 11315897, 15532538, 16237265, 12660628, 13815756, 11887445, 6110542,
        16777231, 158820142, 12946398, 167775711, 50333337, 184552603, 83886080, 117440512, 218103808,
        251658291, 33554432, 201326592, 67108864, 100663296, 134217728, 234881024, 268435456,
    ),
    (
        10381668, 14844420, 1741381, 2069162, 32033483, 55821179, 11796413, 150996302, 83886080, 123278288,
        6215472, 7941405, 184549422, 167773715, 12539487, 218103857, 33554432, 80330138, 251658240, 201330163,
        100663296, 134217728, 234881024, 268435456, 0, 0, 0,
    ),
    (
        1859908, 16777992, 9503348, 4704589, 50375093, 10282173, 83967926, 16597751, 4113784, 117440569,
        15654552, 151193000, 167772160, 13036121, 184549402, 6225066, 201326619, 218103808, 234884331,
        251658268, 268435456, 33556381, 67108895, 100663296, 134217728, 0, 0,
    ),
    (
        1859908, 20138248, 10002213, 2874701, 50334158, 100201206, 117440512, 16584247, 6526060, 12041874,
        150997523, 10831470, 197326485, 11364074, 167772209, 231331607, 251658270, 201329887, 33554432,
        67108864, 234881024, 100663296, 134217728, 268435456, 0, 0, 0,
    ),
    (
        10115329, 10910504, 162106285, 184549376, 218105612, 6746960, 33555729, 251747037, 1142042, 67108894,
        8238581, 16777224, 1543222, 50334793, 100666962, 2847154, 1913786, 99414771, 134217788, 117440573,
        167772160, 201326654, 234881024, 268435519, 0, 0, 0,
    ),
    (
        10115329, 11959080, 150997929, 184549376, 224414348, 20219695, 251763406, 7816197, 2557199, 33557621,
        50538118, 14366602, 14766545, 4945611, 84120991, 67347671, 117444348, 100663357, 134217728, 167772222,
        201326592, 234881024, 268435519, 0, 0, 0, 0,
    ),
    (
        1859908, 9865473, 7498409, 10343723, 12764693, 150995993, 35854234, 3275611, 184552754, 16777216,
        218103854, 62709065, 267611350, 14488458, 14930647, 83887247, 82568441, 167772160, 117440571,
        100663296, 201326655, 134217728, 234881024, 268435456, 0, 0, 0,
    ),
    (
        1859908, 10914049, 11430565, 27051784, 150994988, 5282845, 188058733, 50331648, 12124830, 33554482,
        218107150, 2989269, 8190965, 90924433, 14532156, 251892887, 117440512, 67362451, 167772160, 100667323,
        134217728, 201326592, 234881024, 268435519, 0, 0, 0,
    ),
    (
        2380292, 6, 11700481, 11966794, 3045767, 150994990, 184549376, 218103850, 251661039, 12698648,
        8095577, 38061361, 16780447, 13688018, 50331705, 87774426, 7300474, 67108879, 117444054, 100663296,
        150454039, 167772222, 201326655, 234881024, 268435456, 0, 0,
    ),
    (
        2380292, 10668289, 10379685, 150994989, 3052167, 184549422, 218106858, 16779980, 251658240, 3609648,
        50331672, 3742876, 97603123, 4035765, 33676729, 123025079, 67112606, 107988950, 167772160, 134221655,
        201326592, 234885051, 268435519, 0, 0, 0, 0,
    ),
    (
        1859908, 2509320, 3459649, 3842725, 4088528, 16779985, 50331687, 83887276, 117440512, 150994944,
        184549421, 223169436, 251854109, 39935868, 12677118, 6155381, 8232118, 67108915, 7306778, 100663353,
        167772218, 134217787, 201326592, 234881024, 268435456, 0, 0,
    ),
    (
        1859908, 2568, 9474817, 2773865, 16779920, 50331648, 10032011, 83888847, 117440512, 151176359,
        184549421, 218103854, 267466031, 13721436, 13107120, 33554456, 13462898, 6679965, 67108887, 167772216,
        100793946, 201326592, 134458843, 234881083, 268435456, 0, 0,
    ),
    (
        10381668, 2380292, 161508097, 10793418, 184549421, 218155946, 28243213, 3999054, 65367600, 251658240,
        83957306, 117442044, 7446269, 33809585, 13214975, 175590619, 67108917, 201330078, 100663296,
        234884575, 134217728, 268435456, 0, 0, 0, 0, 0,
    ),
    (
        10381668, 20996, 10525441, 150994950, 186553005, 218278795, 16971020, 50509133, 5836302, 251661327,
        83886137, 117538456, 4961404, 16358525, 41100543, 167775514, 214816501, 67108864, 234882998,
        100663351, 268435487, 134217728, 0, 0, 0, 0, 0,
    ),
    (
        1859908, 2568, 9486913, 16777229, 50501962, 10134542, 83887051, 6363627, 117440556, 150998317,
        198632729, 218298002, 251662134, 40984125, 15197403, 7843831, 67110331, 100665239, 134220831,
        167772209, 201326592, 234881074, 268435507, 0, 0, 0, 0,
    ),
    (
        1859908, 8, 9488897, 16777225, 2689613, 50331685, 2955918, 84063206, 123913383, 151209581, 184549422,
        6901103, 218328851, 251658240, 49659420, 16489941, 7863958, 67108923, 167898135, 100663345, 201326592,
        234883058, 134217728, 268435507, 0, 0, 0,
    ),
    (
        9980260, 11555367, 150997513, 195482246, 12772039, 218104618, 11326767, 16777265, 50331648, 4258958,
        7411064, 265389945, 6005918, 83889523, 6634939, 117440572, 49641463, 67108864, 167772222, 201328319,
        234881024, 268435456, 100663323, 134217728, 0, 0, 0,
    ),
    (
        9980260, 11555367, 11960713, 12751306, 150997899, 12372628, 3585393, 14771122, 184550352, 7838940,
        218103860, 14132753, 14231447, 22005755, 251659895, 50587325, 83886080, 117440575, 33554459,
        167772160, 67108864, 201326592, 100663296, 234881024, 268435456, 134217728, 0,
    ),
    (
        1859908, 26266120, 4363081, 50331685, 10134410, 83886097, 10400715, 13732626, 14083309, 12777044,
        117440533, 163958582, 6909815, 184553010, 7812606, 7319545, 218103867, 251658240, 33554432, 167772160,
        67108894, 201326592, 234881024, 268435487, 100663296, 134217728, 0,
    ),
    (
        1859908, 2411016, 21140324, 3844426, 4088907, 10323115, 50331692, 5168409, 12801710, 13069268,
        13223292, 16105015, 84098966, 15326807, 117440575, 150998750, 184549376, 218103808, 251658240,
        33554432, 167772191, 201326592, 67108864, 234881024, 100663296, 268435456, 134217728,
    ),
    (
        10381668, 161516292, 10932805, 2820998, 184549418, 13038279, 218106580, 257395852, 5979725, 13726734,
        7410682, 4961845, 15951453, 8091283, 16779005, 50331710, 83890143, 117440512, 33554432, 67108864,
        167772160, 100663296, 201326592, 234881024, 134217728, 268435456, 0,
    ),
    (
        10381668, 1346308, 151179880, 12626502, 11055598, 184549423, 221426993, 266394773, 16837846, 4146233,
        4572666, 6368605, 14262046, 50332923, 16121306, 83890075, 117440575, 33554432, 167772160, 67108864,
        100663296, 201326592, 134217728, 234881024, 268435456, 0, 0,
    ),
    (
        1859908, 3180840, 16777257, 3447461, 50334096, 10400650, 87999185, 12011026, 151185013, 12690671,
        12956982, 14886263, 117441948, 6264691, 184549436, 226483870, 251662267, 33554495, 67108864,
        167772160, 100663296, 201326592, 134217728, 234881024, 268435456, 0, 0,
    ),
    (
        1859908, 3293736, 16777257, 11065673, 10019472, 50331691, 3979729, 83886124, 117440512, 164811928,
        184552345, 12518645, 218107290, 264617748, 16199189, 16369079, 15062515, 168011711, 33556475,
        67108864, 201326592, 100663296, 234881024, 268435456, 134217728, 0, 0,
    ),
    (
        10381668, 1491460, 150994984, 2648905, 184740905, 12890602, 223523631, 3759245, 20919696, 251660049,
        64059218, 14898398, 83886104, 124217337, 7306906, 33554491, 67108864, 100663296, 134217728, 167772220,
        201326653, 234881086, 268435519, 0, 0, 0, 0,
    ),
    (
        10381668, 1346308, 151034728, 184552006, 12771975, 13040267, 218281228, 3756914, 16777232, 13434390,
        4673116, 4838906, 6418165, 6681846, 251659959, 50335515, 83886080, 117440512, 33554493, 67108864,
        100663358, 134217791, 167772160, 201326592, 234881024, 268435456, 0,
    ),
    (
        1859908, 3293736, 16777257, 3582281, 50399626, 10296014, 4899787, 83886125, 117443480, 151098607,
        184551060, 218105200, 258938292, 41100789, 67231155, 100666846, 134217759, 15707768, 167772220,
        201326653, 234881086, 268435519, 0, 0, 0, 0, 0,
    ),
    (
        1859908, 3293736, 16777257, 11065673, 61760144, 4518795, 83888935, 129600338, 150994944, 6767855,
        12692820, 184549430, 218330481, 251751579, 33764828, 67108893, 100665272, 134217759, 183746233,
        201326653, 234881086, 268435519, 0, 0, 0, 0, 0,
    ),
    (
        10381668, 151161604, 1481544, 184722030, 218280367, 251658250, 5440199, 5710641, 5977101, 16778129,
        7414743, 50451700, 83886080, 117440536, 7034462, 33668511, 67108919, 100663296, 134217728, 167775804,
        201330301, 235142846, 268435515, 0, 0, 0, 0,
    ),
    (
        10381668, 161513772, 2382445, 184552110, 2821062, 218103851, 251658240, 13152753, 20005939, 55104849,
        87770515, 117441495, 6412085, 33554486, 67214814, 100894682, 134217755, 167772220, 201330553,
        235122686, 268435515, 0, 0, 0, 0, 0, 0,
    ),
    (
        1859908, 10783016, 4246181, 4633190, 11782605, 3920530, 16777261, 50335627, 150998991, 84076051,
        184549376, 117440512, 218103808, 251659887, 12670612, 7435675, 33554481, 13495453, 67108895,
        100663296, 134217728, 167775544, 201330041, 235126202, 268435511, 0, 0,
    ),
    (
        1859908, 2267432, 16778021, 4233642, 50334413, 11579175, 150994958, 11842685, 83886095, 5319614,
        184549400, 117440512, 5586927, 224331161, 251658266, 13575921, 33554460, 67110772, 100663326,
        134217759, 167772216, 201330293, 235106042, 268435511, 0, 0, 0,
    ),
    (
        10381668, 10715652, 15706745, 2607749, 2649963, 16547756, 150994955, 16778004, 50332501, 83944470,
        129299921, 184551186, 33653981, 67299225, 13760176, 232193115, 100663296, 167772160, 134221234,
        251658240, 201329911, 234881024, 268435456, 0, 0, 0, 0,
    ),
    (
        10381668, 10522116, 1550969, 11516553, 16035590, 16544830, 3228369, 16780332, 150995797, 50331648,
        83944598, 184612333, 5098776, 12180569, 117440538, 180219227, 33557919, 67108914, 218107127,
        201326592, 100663296, 251658240, 134217728, 234881024, 268435456, 0, 0,
    ),
    (
        1859908, 20073736, 16146229, 4423606, 2619793, 15105554, 2861581, 50335438, 83948268, 150994968,
        117440512, 12138093, 197039386, 6121173, 218105642, 33557533, 67288158, 167775391, 100663347,
        201326592, 251658240, 134217728, 234881024, 268435456, 0, 0, 0,
    ),
    (
        1859908, 3293748, 16780668, 10186597, 16309705, 50331687, 14987256, 99421838, 4764945, 10550037,
        117442067, 150994944, 5876313, 184549421, 167775259, 11199964, 33554461, 230550257, 67108864,
        201329823, 100663296, 251658240, 134217779, 234881024, 268435456, 0, 0,
    ),
)


def kernel(
    n_grp,
    n_blk,
    image_hbm,
    text_hbm,
    image_ids,
    text_ids,
    sharpness,
    offset,
    adjoint,
    grad_image,
    grad_text,
    raw,
    hat,
    buf,
    ids,
    own_ids,
    inverse,
    total,
    load_sem,
    send_sem,
    id_send_sem,
    wrap_sem,
    wrap_id_sem,
    detour_sem,
    ready_sem,
    recv_sem,
    id_recv_sem,
):
    rows = hat.shape[1]
    piece = rows // WAVES
    g = lax.axis_index("grp")
    k = lax.axis_index("blk")
    j = lax.rem(k, RUN)

    loads = [
        pltpu.make_async_copy(text_hbm, raw.at[0], load_sem.at[0]),
        pltpu.make_async_copy(image_hbm, raw.at[1], load_sem.at[1]),
    ]
    for load in loads:
        load.start()

    def device(dg, dk):
        return (lax.rem(g + dg + n_grp, n_grp), lax.rem(k + dk + n_blk, n_blk))

    next_grp = [device(step, 0)[0] for step in (1, -1)]
    next_blk = [device(0, step)[1] for step in (1, -1)]

    barrier = pltpu.get_barrier_semaphore()

    def greet(target):
        pl.semaphore_signal(barrier, inc=1, device_id=target, device_id_type=MESH)

    for target in (device(0, -1), device(1, 0), device(-1, 0)):
        greet(target)

    @pl.when(j != RUN - 1)
    def _():
        greet(device(0, 1))

    even = lax.rem(j, 2) == 0

    @pl.when(even & (j >= 2))
    def _():
        greet(device(0, -2))

    @pl.when(jnp.logical_not(even) & (j <= RUN - 3))
    def _():
        greet(device(0, 2))

    def wrap_target(stream, owner, sender):
        step = 1 - 2 * stream
        return (0 if owner < SPAN else step, step * sender)

    def wrap_links(stream):
        links = [(distance, distance) for distance in range(1, SLOTS - 1)]
        links += [(owner, sender) for which, owner, sender, _, _ in DETOURS if which == stream]
        return sorted({(wrap_target(stream, *link), link[1]) for link in links})

    def others(stream):
        return [link for link in wrap_links(stream) if link[0] != (0, 1 - 2 * stream)]

    @pl.when(j == 0)
    def _():
        for (dg, dk), _ in others(0):
            greet(device(-dg, -dk))

    far_sends = sum([(RUN - j == sender).astype(jnp.int32) for _, sender in others(0)])
    far_sends += jnp.where(j == RUN - 1, len(others(1)), 0) - jnp.where(j == 0, 1, 0)
    ready_count = sum([(j + 1 == sender).astype(jnp.int32) for _, sender in wrap_links(1)])
    for (dg, dk), sender in others(1):

        @pl.when(j + 1 == sender)
        def _():
            greet(device(dg, dk))

    def wrap_distance(stream):
        to_edge = RUN - j if stream == 0 else j + 1
        return to_edge, (to_edge >= 2) & (to_edge <= 6)

    skips = jnp.where(even, j != RUN - 2, j != 1).astype(jnp.int32)
    barrier_count = 4 + skips + far_sends

    @pl.when(j == RUN - 1)
    def _():
        pl.semaphore_wait(barrier, barrier_count)
        for (dg, dk), _ in wrap_links(1):
            pl.semaphore_signal(
                ready_sem, inc=1, device_id=device(-dg, -dk), device_id_type=MESH
            )

    for stream, own in ((0, text_ids), (1, image_ids)):
        loads[stream].wait()
        for c in range(WAVES):
            part = pl.ds(c * piece, piece)
            wide = raw[stream, part, :].astype(jnp.float32)
            inv = lax.rsqrt(jnp.sum(wide * wide, axis=-1, keepdims=True) + EPSILON)
            inverse[stream, part, :] = jnp.broadcast_to(inv, (piece, 128))
            unit = (wide * inv).astype(jnp.bfloat16)
            hat[stream, part, :] = unit
            buf[stream, c, pl.ds(0, piece), :] = unit
            at = c * piece
            line = own[at // 128 : at // 128 + 1, :].astype(jnp.float32)
            line = line[:, at % 128 : at % 128 + piece]
            ids[stream, 0, c] = jnp.concatenate([line] * (128 // piece), axis=1)

    @pl.when(j != RUN - 1)
    def _():
        pl.semaphore_wait(barrier, barrier_count)

    def pick(stream, pair):
        return pair[stream] if isinstance(stream, int) else jnp.where(stream == 0, pair[0], pair[1])

    def route(stream, s, reach):
        place = pick(stream, (j, RUN - 1 - j))
        entry = lax.rem(place, 2) == 0
        fresh = (s == 0) | (s == SPAN)
        if reach == 2:
            goes = entry & (place != RUN - 2) & (fresh | (s == 1) | (s == SPAN + 1))
            return (g, pick(stream, [device(0, step)[1] for step in (2, -2)])), goes
        hop = s == SPAN - 1
        target = (
            jnp.where(hop, pick(stream, next_grp), g),
            jnp.where(hop, k, pick(stream, next_blk)),
        )
        goes = jnp.where(place == RUN - 1, s == 0, entry | fresh)
        return target, (s < SLOTS - 1) & (hop | goes)

    def chunk(stream, s, c):
        at = s * piece
        if not isinstance(at, int):
            at = pl.multiple_of(at, piece)
        return buf.at[stream, c, pl.ds(at, piece)]

    def remote(src, dst, send, recv, target):
        return pltpu.make_async_remote_copy(
            src_ref=src,
            dst_ref=dst,
            send_sem=send,
            recv_sem=recv,
            device_id=target,
            device_id_type=MESH,
        )

    def block_copy(stream, s, c, reach, target):
        return remote(
            chunk(stream, s, c),
            chunk(stream, s + reach, c),
            send_sem.at[reach - 1, stream, s],
            recv_sem.at[stream, s + reach, c],
            target,
        )

    def id_copy(stream, s, reach, target):
        return remote(
            ids.at[stream, s],
            ids.at[stream, s + reach],
            id_send_sem.at[reach - 1, stream, s],
            id_recv_sem.at[stream, s + reach],
            target,
        )

    def forward(stream, s, c):
        for reach in (2, 1):
            target, goes = route(stream, s, reach)

            @pl.when(goes)
            def _():
                @pl.when(c == 0)
                def _():
                    id_copy(stream, s, reach, target).start()

                block_copy(stream, s, c, reach, target).start()

    def receive(stream, s, c):
        target = (g, pick(stream, next_blk))

        @pl.when(c == 0)
        def _():
            id_copy(stream, s - 1, 1, target).wait_recv()

        block_copy(stream, s - 1, c, 1, target).wait_recv()

    def wrap_route(stream):
        to_edge, far = wrap_distance(stream)
        same = to_edge < SPAN
        slot = jnp.where(same, to_edge, to_edge + 1)
        step = 1 - 2 * stream
        return far, slot, device(jnp.where(same, 0, step), step * to_edge)

    def wrap_id_copy(stream):
        _, slot, target = wrap_route(stream)
        return remote(
            ids.at[stream, 0],
            ids.at[stream, slot],
            wrap_id_sem.at[stream],
            id_recv_sem.at[stream, slot],
            target,
        )

    def wrap(stream, c, far):
        _, slot, target = wrap_route(stream)

        @pl.when(far)
        def _():
            remote(
                chunk(stream, 0, c),
                chunk(stream, slot, c),
                wrap_sem.at[stream],
                recv_sem.at[stream, slot, c],
                target,
            ).start()

    def wrap_early(stream):
        to_edge, far = wrap_distance(stream)

        @pl.when(far)
        def _():
            wrap_id_copy(stream).start()

        for c in range(WAVES):
            now = far & (to_edge < PATIENT[stream])
            for which, owner, _, _, waves in DETOURS:
                if which == stream and c in waves:
                    now = now & (to_edge != owner)
            wrap(stream, c, now)

    def wrap_late(other, s, c):
        for stream in range(2):
            to_edge, far = wrap_distance(stream)
            now = far & (to_edge >= PATIENT[stream]) & (other == 1 - stream) & (s == SPAN - 1)
            for which, owner, _, _, waves in DETOURS:
                if which == stream:
                    kept = functools.reduce(jnp.logical_and, [c != wave for wave in waves])
                    now = now & ((to_edge != owner) | kept)
            wrap(stream, c, now)

    def detour_copy(n, c):
        stream, owner, sender, s, _ = DETOURS[n]
        slot = owner if owner < SPAN else owner + 1
        return remote(
            chunk(stream, s, c),
            chunk(stream, slot, c),
            detour_sem.at[n],
            recv_sem.at[stream, slot, c],
            device(*wrap_target(stream, owner, sender)),
        )

    def detour(stream, s, c):
        for n, (which, _, sender, slot, waves) in enumerate(DETOURS):
            place = RUN - sender if which == 0 else sender - 1
            now = functools.reduce(jnp.logical_or, [c == wave for wave in waves])

            @pl.when((stream == which) & (s == slot) & (j == place) & now)
            def _():
                detour_copy(n, c).start()

    for c in range(WAVES):
        forward(0, 0, c)

        @pl.when(j != 0)
        def _():
            forward(1, 0, c)

    wrap_early(0)

    def cross():
        pl.semaphore_wait(ready_sem, ready_count)
        for c in range(WAVES):

            @pl.when(j == 0)
            def _():
                forward(1, 0, c)

        wrap_early(1)

    row = lax.broadcasted_iota(jnp.int32, (128, 128), 0)
    lane = lax.broadcasted_iota(jnp.int32, (128, 128), 1)
    for stream, own in ((0, text_ids), (1, image_ids)):
        for half in range(rows // 128):
            line = jnp.broadcast_to(own[half : half + 1, :].astype(jnp.float32), (128, 128))
            column = jnp.sum(jnp.where(row == lane, line, 0.0), axis=-1, keepdims=True)
            own_ids[stream, pl.ds(half * 128, 128), :] = jnp.broadcast_to(column, (128, 128))
        total[stream] = jnp.zeros(total.shape[1:], jnp.float32)

    scale = jnp.exp(jnp.full((1, 128), sharpness[0], jnp.float32))[:, :1]
    shift = offset[0]
    weight = -(adjoint[0] * scale / rows)
    group = SPAN * piece
    turn = lax.broadcasted_iota(jnp.int32, (1, 128), 1) // piece

    def compute(stream, c, half):
        mine = 1 - stream
        visitors = buf[stream, c, pl.ds(pl.multiple_of(half * group, group), group), :]
        grid = lax.dot_general(
            hat[mine], visitors, (((1,), (1,)), ((), ())), preferred_element_type=jnp.float32
        )
        logit = scale * grid + shift
        column = own_ids[mine, :, :]
        parts = []
        for at in range(0, group, 128):
            s = half * SPAN + at // piece
            line = ids[stream, s, c]
            for other in range(1, 128 // piece):
                line = jnp.where(turn == other, ids[stream, s + other, c], line)
            match = column == jnp.broadcast_to(line, (rows, 128))
            here = logit[:, at : at + 128]
            signed = jnp.where(match, here, -here)
            parts.append(jnp.where(match, weight, -weight) * (1.0 / (1.0 + jnp.exp(signed))))
        coef = jnp.concatenate(parts, axis=1).astype(jnp.bfloat16)
        total[mine] += jnp.dot(coef, visitors, preferred_element_type=jnp.float32)

    words = []
    line = lax.rem(g, LINE)
    turn_at = 2 * j + lax.div(k, RUN)
    for i in range(len(ORDER[0])):
        word = jnp.int32(0)
        for row in reversed(range(LINE)):
            entries = [ORDER[row * 2 * RUN + place][i] for place in range(2 * RUN)]
            entry = jnp.int32(entries[0])
            for place in range(1, 2 * RUN):
                if entries[place] != entries[place - 1]:
                    entry = jnp.where(turn_at >= place, entries[place], entry)
            word = entry if row == LINE - 1 else jnp.where(line == row, entry, word)
        words.append(word)

    def step(i, carry):
        word = words[0]
        for other in range(1, len(words)):
            word = jnp.where(i == other, words[other], word)

        @pl.when(lax.rem(word, 64) == 1)
        def _():
            cross()

        for _ in range(4):
            entry = lax.rem(word, 64)
            word = lax.div(word, 64)
            stream = lax.div(entry, 32)
            s = lax.rem(lax.div(entry, 4), 8)
            c = lax.rem(entry, 4)

            @pl.when(entry > 1)
            def _():
                receive(stream, s, c)
                forward(stream, s, c)
                wrap_late(stream, s, c)
                detour(stream, s, c)

        @pl.when(word > 0)
        def _():
            product = word - 1
            compute(lax.div(product, 8), lax.div(lax.rem(product, 8), 2), lax.rem(product, 2))

        return carry

    lax.fori_loop(0, len(words), step, 0)

    for stream, out in ((1, grad_image), (0, grad_text)):
        for c in range(WAVES):
            part = pl.ds(c * piece, piece)
            inv = inverse[stream, part, :][:, :1]
            unit = raw[stream, part, :].astype(jnp.float32) * inv
            grad = total[stream, part, :]
            along = jnp.sum(unit * grad, axis=-1, keepdims=True)
            out[part, :] = inv * (grad - unit * along)

    for stream in range(2):
        for s in range(SLOTS - 1):
            for reach in (2, 1):
                target, goes = route(stream, s, reach)

                @pl.when(goes)
                def _():
                    id_copy(stream, s, reach, target).wait_send()
                    remote(
                        hat.at[stream],
                        hat.at[stream],
                        send_sem.at[reach - 1, stream, s],
                        recv_sem.at[stream, s + 1, 0],
                        target,
                    ).wait_send()

        far, slot, target = wrap_route(stream)

        @pl.when(far)
        def _():
            wrap_id_copy(stream).wait_send()

        for distance in range(2, SLOTS - 1):
            away = [len(d[4]) for d in DETOURS if d[0] == stream and d[1] == distance]
            amount = rows - piece * sum(away)
            if amount:

                @pl.when(wrap_distance(stream)[0] == distance)
                def _():
                    part = hat.at[stream, pl.ds(0, amount)]
                    remote(
                        part, part, wrap_sem.at[stream], recv_sem.at[stream, slot, 0], target
                    ).wait_send()

    for n, (stream, _, sender, _, waves) in enumerate(DETOURS):

        @pl.when(j == (RUN - sender if stream == 0 else sender - 1))
        def _():
            part = hat.at[stream, pl.ds(0, piece * len(waves))]
            target = device(0, 1 - 2 * stream)
            remote(
                part, part, detour_sem.at[n], recv_sem.at[stream, 1, 0], target
            ).wait_send()


def body(n_grp, n_blk, image_emb, text_emb, image_pair_index, text_ids, sharpness, offset, adjoint):
    rows, width = image_emb.shape
    vmem = pl.BlockSpec(memory_space=pltpu.VMEM)
    smem = pl.BlockSpec(memory_space=pltpu.SMEM)
    hbm = pl.BlockSpec(memory_space=pltpu.HBM)
    flops = 4 * SLOTS * 2 * rows * rows * width
    return pl.pallas_call(
        functools.partial(kernel, n_grp, n_blk),
        out_shape=(
            jax.ShapeDtypeStruct((rows, width), jnp.float32),
            jax.ShapeDtypeStruct((rows, width), jnp.float32),
        ),
        in_specs=[hbm, hbm, vmem, vmem, smem, smem, smem],
        out_specs=(vmem, vmem),
        scratch_shapes=[
            pltpu.VMEM((2, rows, width), jnp.bfloat16),
            pltpu.VMEM((2, rows, width), jnp.bfloat16),
            pltpu.VMEM((2, WAVES, SLOTS * rows // WAVES, width), jnp.bfloat16),
            pltpu.VMEM((2, SLOTS, WAVES, 1, 128), jnp.float32),
            pltpu.VMEM((2, rows, 128), jnp.float32),
            pltpu.VMEM((2, rows, 128), jnp.float32),
            pltpu.VMEM((2, rows, width), jnp.float32),
            pltpu.SemaphoreType.DMA((2,)),
            pltpu.SemaphoreType.DMA((2, 2, SLOTS)),
            pltpu.SemaphoreType.DMA((2, 2, SLOTS)),
            pltpu.SemaphoreType.DMA((2,)),
            pltpu.SemaphoreType.DMA((2,)),
            pltpu.SemaphoreType.DMA((max(1, len(DETOURS)),)),
            pltpu.SemaphoreType.REGULAR,
            pltpu.SemaphoreType.DMA((2, SLOTS, WAVES)),
            pltpu.SemaphoreType.DMA((2, SLOTS)),
        ],
        compiler_params=pltpu.CompilerParams(
            collective_id=0, has_side_effects=True, vmem_limit_bytes=60 * 1024 * 1024
        ),
        cost_estimate=pl.CostEstimate(
            flops=flops, bytes_accessed=12 * rows * width, transcendentals=2 * SLOTS * rows * rows
        ),
    )(
        image_emb,
        text_emb,
        image_pair_index.reshape(rows // 128, 128),
        text_ids.reshape(rows // 128, 128),
        sharpness,
        offset,
        adjoint,
    )


def solution(mesh):
    both = ("grp", "blk")
    return jax.shard_map(
        functools.partial(body, mesh.shape["grp"], mesh.shape["blk"]),
        mesh=mesh,
        in_specs=(P(both, None), P(both, None), P(both), P(both), P(), P(), P()),
        out_specs=(P(both, None), P(both, None)),
        check_vma=False,
    )
```

```python
import functools

import jax
import jax.numpy as jnp
from jax import lax
from jax.experimental import pallas as pl
from jax.experimental.pallas import tpu as pltpu
from jax.sharding import PartitionSpec as P

MESH = pl.DeviceIdType.MESH
EPSILON = 1e-06

SPAN = 4
SLOTS = 8
LINE = 4
PATIENT = (7, 2)
RUN = 16
WAVES = 4
DETOURS = (
)


ORDER = (
    (
        10639617, 10394406, 150994989, 184549422, 218299032, 251658283, 2115340, 16777241, 1543181, 3791945,
        50331700, 4259418, 83927474, 173088570, 33554483, 2078645, 117552459, 67112381, 201328598, 234881086,
        268697047, 100663314, 134217747, 0, 0, 0, 0, 0,
    ),
    (
        10115329, 10910504, 150994989, 184549376, 218277422, 251837404, 7684889, 7017840, 6153656, 8240313,
        13583245, 15684602, 16777732, 167772540, 50331657, 204017478, 33554432, 83886087, 117440523, 67363958,
        234881024, 100663314, 134444287, 268435456, 0, 0, 0, 0,
    ),
    (
        1859908, 9865473, 11430569, 151177692, 184549421, 221368878, 16777216, 251661300, 13947504, 50331708,
        182537630, 83946570, 16090487, 201326649, 6619890, 33685391, 117440570, 234881050, 71679987,
        268435515, 100664722, 134218967, 0, 0, 0, 0, 0, 0,
    ),
    (
        1859908, 9865473, 11430569, 151177692, 196560413, 14002073, 218103854, 12710939, 251661302, 2346481,
        167776120, 16777228, 204969033, 50331648, 46720266, 99155851, 117440512, 234881042, 67354581,
        100666582, 268435456, 134219219, 0, 0, 0, 0, 0, 0,
    ),
    (
        2380292, 6, 162695425, 10005349, 184719815, 218276590, 251837487, 3354161, 16989812, 64544437,
        168021499, 83944472, 201326653, 235136793, 268436479, 117441821, 33554432, 72742801, 106509970,
        134219227, 0, 0, 0, 0, 0, 0, 0, 0,
    ),
    (
        2380292, 162695425, 11952549, 2003623, 184746734, 218299498, 251661483, 7720184, 14020212, 8351376,
        183729876, 201330513, 16854924, 234881024, 50331661, 272184703, 83886080, 33554456, 117440527,
        67110486, 100663322, 134219227, 0, 0, 0, 0, 0, 0,
    ),
    (
        1859908, 9476616, 41, 9741057, 16779917, 50331648, 84042635, 117503019, 151176295, 184737042,
        232197011, 251661423, 14626614, 182709501, 201326649, 235119900, 268558079, 33554456, 67110485,
        107575190, 134219487, 0, 0, 0, 0, 0, 0, 0,
    ),
    (
        1859908, 2568, 16925441, 50387529, 11076261, 83886094, 11336075, 117440529, 150997799, 196427026,
        218103854, 264183152, 5491894, 6504311, 167772216, 201330617, 234884757, 268678591, 33670617,
        67110746, 100663326, 134219487, 0, 0, 0, 0, 0, 0,
    ),
    (
        1206628, 11555367, 150997513, 6, 1878849, 184552489, 27839371, 218103808, 63353711, 251658260,
        89599502, 117441935, 13436409, 13967028, 168021750, 201577655, 234885011, 268435519, 33556248,
        67110745, 100787930, 134217759, 0, 0, 0, 0, 0, 0,
    ),
    (
        10381668, 516, 11571521, 162834950, 187632199, 3230634, 218103857, 16970603, 50331648, 251659157,
        83889336, 117507471, 13844055, 14228858, 183602898, 201579987, 33558428, 234881024, 268435519,
        74823321, 100663326, 134217759, 0, 0, 0, 0, 0, 0,
    ),
    (
        1859908, 9476616, 41, 16777985, 50483853, 93893546, 117508815, 151176295, 196445364, 230268243,
        264437146, 13092564, 14888789, 167772215, 201584243, 235122646, 268439255, 33554460, 67108893,
        100663326, 134217759, 0, 0, 0, 0, 0, 0, 0,
    ),
    (
        1859908, 8, 16941825, 61135113, 3737930, 83886122, 121443046, 4819687, 150998316, 184653037,
        218107246, 12430356, 267589366, 14507890, 167772216, 16487859, 201326620, 33558167, 234881024,
        268439295, 67108893, 100663326, 134217759, 0, 0, 0, 0, 0,
    ),
    (
        1206628, 11555367, 162955657, 10779658, 184552331, 11066444, 16777263, 50331648, 218311374, 83886100,
        251658240, 117444111, 13485077, 7816633, 13964794, 6516446, 33632031, 172859255, 201326654, 67108864,
        234885082, 100663323, 268435456, 134217728, 0, 0, 0, 0,
    ),
    (
        9980260, 11555367, 2648585, 150994989, 12227056, 184549387, 218103850, 29816076, 251658283, 50420877,
        83979790, 117440527, 13868240, 14013916, 14257978, 167774097, 33554432, 14495455, 67112793, 201582227,
        100663296, 234881051, 134217791, 268435456, 0, 0, 0, 0,
    ),
    (
        1859908, 16828936, 61135113, 11077962, 83886798, 128869455, 150997799, 196447506, 6745427, 218105136,
        264612854, 7310834, 7576789, 33558166, 67352029, 100663326, 134217759, 167772220, 201326653,
        234881086, 268435519, 0, 0, 0, 0, 0, 0, 0,
    ),
    (
        1859908, 16828936, 53908068, 2794533, 83886094, 4518630, 117440555, 155895335, 189635444, 218322606,
        251661296, 7282068, 7568568, 33789299, 67229114, 100906903, 134217759, 167772220, 201326653,
        234881086, 268435519, 0, 0, 0, 0, 0, 0, 0,
    ),
    (
        10381668, 1491460, 163764745, 12227206, 11058247, 184549423, 229428372, 5976917, 7404814, 16874832,
        256337437, 6780062, 50439391, 83886107, 117440512, 33554432, 67108864, 100663296, 134217728,
        167775804, 201584253, 235126778, 268435456, 0, 0, 0, 0, 0,
    ),
    (
        10381668, 10521348, 163762757, 2810281, 12890602, 3230447, 184604018, 13583254, 218166736, 7675228,
        6367158, 258291703, 16778970, 50331648, 83886080, 117440512, 33554432, 67108924, 100663352, 134217728,
        167776121, 201326650, 234881086, 268439547, 0, 0, 0, 0,
    ),
    (
        1859908, 9486888, 9753193, 4252330, 3980006, 16780071, 12159825, 50525778, 96840723, 117440512,
        151108756, 184549376, 218103808, 251747548, 33556310, 67110807, 100663327, 134217728, 15965496,
        167772213, 217046458, 235143095, 268435456, 0, 0, 0, 0, 0,
    ),
    (
        1859908, 3180840, 16777257, 3447461, 11314214, 4504014, 4903916, 50334616, 88972335, 7162970,
        150996338, 117556659, 184551255, 218234654, 251911480, 47967861, 67108922, 100663359, 134221559,
        167772160, 201326592, 234881024, 268435456, 0, 0, 0, 0, 0,
    ),
    (
        10381668, 1346308, 151034728, 184552006, 3072647, 218106858, 3492556, 16777230, 251659599, 50333462,
        83886080, 117442391, 6682142, 33621722, 4705332, 81990837, 14364499, 16481529, 100663354, 167772160,
        134221819, 201326592, 234881024, 268435456, 0, 0, 0, 0,
    ),
    (
        10381668, 1491460, 1612648, 2024105, 3340939, 151049515, 184549376, 218105166, 16778639, 251658268,
        50456029, 83886080, 117440536, 7063135, 12836379, 16457332, 167775925, 217017535, 234881024,
        268439027, 33554448, 67108881, 100663314, 134217747, 0, 0, 0, 0,
    ),
    (
        1859908, 3293736, 16777257, 61397321, 3062154, 4355022, 83886124, 12422061, 117440529, 150994969,
        184549402, 218103835, 251658240, 8251228, 15926482, 33558036, 5981553, 14102141, 14396631, 67354110,
        167772160, 100663359, 201326592, 134217728, 234881024, 268435456, 0, 0,
    ),
    (
        1859908, 3293736, 16777257, 3582281, 3848586, 62026699, 96308141, 117440537, 150994944, 184549402,
        218103808, 251658240, 7833371, 12709492, 13086047, 4402934, 4928631, 167772220, 33555731, 67202901,
        201330583, 100663359, 134217728, 234881024, 268435456, 0, 0, 0,
    ),
    (
        10381668, 151161604, 1479213, 184549422, 12497514, 218103814, 251658698, 16827659, 50332501, 83886094,
        117561103, 15796190, 5981304, 6229842, 13080083, 14364597, 167775897, 33664499, 201326592, 67112923,
        234881024, 100663355, 134217728, 268435456, 0, 0, 0, 0,
    ),
    (
        10381668, 150997548, 195330349, 11467438, 218104389, 251658240, 2912902, 16777228, 13829005, 14096143,
        13330333, 50331679, 83886080, 117440512, 5492211, 167772216, 5837845, 5055997, 201328185, 33556094,
        15726266, 67108891, 234881024, 100663296, 268435456, 134217728, 0, 0,
    ),
    (
        1859908, 10783016, 10013349, 16955849, 15772429, 62174222, 157537262, 83886127, 184549401, 218103808,
        117440512, 251658240, 14757777, 5702964, 5877331, 6143093, 13367098, 167772214, 201328499, 33554432,
        234884830, 67108864, 100666847, 134217728, 268435456, 0, 0, 0,
    ),
    (
        1859908, 9869608, 10011178, 16779755, 50385532, 84136842, 151057132, 117443629, 184549376, 218106990,
        251915439, 4686899, 167772212, 6812824, 6905428, 215312083, 33670650, 14661494, 234881054, 67108895,
        268435456, 100663296, 134217728, 0, 0, 0, 0, 0,
    ),
    (
        10381668, 10506756, 11049592, 2801222, 3124999, 171133972, 16777216, 13950805, 56159312, 14339215,
        201442427, 6366685, 5086078, 13479390, 91095022, 117440559, 150994944, 33554432, 234881024, 184549376,
        67108864, 100663296, 218103808, 268435456, 134217728, 251658240, 0, 0,
    ),
    (
        10381668, 10915448, 11043132, 15381061, 16171654, 150995655, 3883852, 16778224, 5311358, 13980795,
        50333503, 7693489, 5204888, 13493874, 8224239, 83887834, 167772160, 117440512, 184549376, 201326592,
        33554432, 218103808, 234881024, 67108864, 251658240, 268435456, 100663296, 134217728,
    ),
    (
        1859908, 13682952, 16932617, 50388326, 87808458, 14222072, 16450513, 117442066, 167772160, 208082169,
        14625300, 11624410, 11909754, 7812886, 15657623, 159300574, 234881024, 184549376, 33554432, 67108864,
        218103808, 268435456, 100663296, 251658240, 134217728, 0, 0, 0,
    ),
    (
        1859908, 9658164, 10214949, 31093512, 2786121, 50589262, 83887051, 117440512, 167775248, 16753772,
        5469353, 5082865, 151100245, 201326592, 5974702, 6147034, 184671467, 218232731, 234881024, 33554432,
        251658240, 268435456, 67108864, 100663296, 134217728, 0, 0, 0,
    ),
    (
        10115329, 151177767, 184552297, 218106794, 2146607, 16777259, 251658245, 50385289, 2035210, 6493451,
        83945268, 13462677, 117503609, 6911861, 7302814, 168021727, 33805367, 201326592, 67112849, 234881024,
        100663314, 268435519, 134217747, 0, 0, 0, 0, 0,
    ),
    (
        10115329, 151177767, 184552045, 218106542, 5435908, 251658283, 1412208, 14718741, 7704982, 20017842,
        48712912, 50455386, 67108881, 83887246, 100663296, 121418951, 15580853, 134217759, 167775676,
        201326653, 234881086, 268439543, 0, 0, 0, 0, 0, 0,
    ),
    (
        1859908, 9865473, 11446697, 154323400, 16777225, 184550253, 50334986, 83886094, 6353648, 117442350,
        218103824, 7019865, 251661277, 13233563, 182681361, 216520691, 33555604, 234884798, 67112917,
        268435515, 100664534, 134217751, 0, 0, 0, 0, 0, 0,
    ),
    (
        1859908, 10914049, 11430565, 16826919, 150997784, 2463540, 50331661, 184551085, 7276362, 83887029,
        5855124, 222130926, 117444017, 33554448, 251658287, 13180727, 67108920, 167772191, 201404029,
        100663358, 235142394, 134221523, 268435456, 0, 0, 0, 0, 0,
    ),
    (
        2380292, 6, 11700481, 10934602, 150997383, 184549415, 218278795, 254983152, 16777265, 50388530,
        87792947, 131661493, 5471964, 167898909, 201330512, 234885023, 268436863, 33653905, 67212502,
        100663322, 134219479, 0, 0, 0, 0, 0, 0, 0,
    ),
    (
        20996, 11682369, 150997541, 11823590, 184552010, 12255943, 218103850, 264944625, 16777228, 13843996,
        50332509, 15423417, 83886094, 6516447, 167772220, 215996057, 121749391, 234881024, 268436799,
        33554432, 67110225, 100742546, 134217751, 0, 0, 0, 0, 0,
    ),
    (
        1859908, 2509320, 152233, 16777985, 50331661, 86829482, 117440527, 151177707, 184552749, 218323888,
        266007601, 14664818, 5233874, 168005528, 201326649, 234884756, 268439547, 40985945, 67229146,
        100663326, 134219739, 0, 0, 0, 0, 0, 0, 0,
    ),
    (
        1859908, 150024, 27562753, 50334029, 4367242, 83886118, 117617611, 150997799, 184621940, 218323888,
        251861970, 14664950, 168005490, 13606812, 201326621, 235141050, 268435515, 33654047, 67110485,
        100771286, 134217755, 0, 0, 0, 0, 0, 0, 0,
    ),
    (
        10381668, 2380292, 27180, 150994945, 10779466, 184549387, 27986828, 218103821, 50332591, 84087787,
        251658240, 117443768, 13872377, 15691092, 167776055, 201330517, 234881086, 268439510, 39912924,
        67213137, 7185618, 100663326, 134217759, 0, 0, 0, 0, 0,
    ),
    (
        10381668, 2380292, 161508097, 10779466, 184550128, 218155946, 16777216, 11465556, 50332593, 251658240,
        83886095, 117440512, 5741752, 14134516, 183745942, 201577975, 234881086, 268435519, 40993872,
        74814674, 100787930, 134217759, 0, 0, 0, 0, 0, 0,
    ),
    (
        1859908, 9476616, 3576577, 16779594, 50331648, 83888782, 117502694, 164809195, 184549421, 218106805,
        267586991, 6500209, 168004855, 201561150, 234882682, 268439295, 4830298, 33556244, 67229011,
        100787670, 134217759, 0, 0, 0, 0, 0, 0, 0,
    ),
    (
        1859908, 2568, 19284737, 50331661, 87708329, 3979690, 117440528, 162630123, 184552308, 230878545,
        251763702, 14626609, 167776120, 217816282, 251510418, 268435515, 40981779, 67229142, 100663326,
        134217759, 0, 0, 0, 0, 0, 0, 0, 0,
    ),
    (
        9980260, 11555367, 150997513, 2019974, 197323339, 16779916, 218103857, 50334669, 251659179, 83886095,
        117444146, 13442640, 4939444, 167776054, 5232443, 201326647, 234881086, 268695380, 5895518, 33554456,
        67110487, 100663322, 134217755, 0, 0, 0, 0, 0,
    ),
    (
        9980260, 11555367, 150997513, 12767878, 196655687, 16779916, 218297201, 50331691, 251716914, 83886080,
        117444111, 15152156, 14134549, 182175569, 14668987, 201328531, 234881086, 268563903, 33555991,
        67108889, 100663322, 134217755, 0, 0, 0, 0, 0, 0,
    ),
    (
        1859908, 16828936, 61133412, 2689701, 83886094, 3978342, 117440555, 150997799, 184737042, 218295635,
        264203284, 14888021, 13463159, 6534650, 167772220, 49661593, 201326592, 67110747, 234881086,
        100663326, 268435519, 134217759, 0, 0, 0, 0, 0, 0,
    ),
    (
        1859908, 16828936, 61133412, 2794533, 83886094, 3978342, 117440555, 151176359, 189631348, 218103854,
        5442549, 251661430, 14650521, 6003925, 183746199, 201330522, 234999707, 33554432, 268435519, 67108893,
        100663326, 134217759, 0, 0, 0, 0, 0, 0,
    ),
    (
        10381668, 161516292, 12767813, 2812486, 184549418, 12368967, 223552299, 251659093, 4404622, 16872436,
        6772241, 50332854, 83886080, 117550547, 14798619, 33554493, 167772160, 201328505, 67348414, 100667359,
        234881083, 134217728, 268435456, 0, 0, 0, 0, 0,
    ),
    (
        10381668, 161516292, 12767813, 184738217, 12876426, 5422027, 218104626, 251659093, 13692118, 13956560,
        16778332, 7679384, 5207676, 57661112, 83886137, 117680062, 33798143, 67108864, 167772160, 201326592,
        100663296, 234881024, 134217728, 268435456, 0, 0, 0, 0,
    ),
    (
        1859908, 3180840, 16777257, 3447461, 3712038, 2955755, 4903916, 50525742, 7013971, 83999828, 7720085,
        150996403, 8357783, 117440564, 184549376, 218103865, 251658240, 33554432, 67108864, 100663296,
        134217781, 14663098, 167772220, 201326653, 234885118, 268435456, 0, 0,
    ),
    (
        1859908, 3180840, 16777257, 3447461, 50332710, 3046090, 11868942, 4819855, 83886127, 6895216,
        13219121, 13487637, 150996404, 15826525, 15334750, 184552893, 134213115, 218103808, 251658240,
        33554432, 67108864, 167772160, 100663296, 134217728, 201326592, 234881024, 268435456, 0,
    ),
    (
        10381668, 1491460, 150994984, 2648905, 184552361, 218276551, 5422028, 5825869, 6145039, 16778333,
        251658270, 50333202, 6635295, 91162292, 117440512, 33557885, 67108913, 100663296, 134217790, 14630070,
        167776248, 201326649, 234884858, 268435456, 0, 0, 0, 0,
    ),
    (
        10381668, 1491460, 150994984, 2648905, 184552361, 218276551, 5422028, 16777229, 3999054, 251658262,
        13829980, 50332796, 83888023, 14095890, 5111672, 15165081, 13483954, 117702327, 33554491, 167772160,
        67108864, 100663296, 201326592, 134217728, 234881024, 268435456, 0, 0,
    ),
    (
        1859908, 3293736, 16777257, 3582281, 3737994, 3979755, 50334481, 83889069, 117515823, 156345561,
        184550747, 230778680, 251660119, 46634974, 67108864, 100663296, 134217728, 13843642, 168021371,
        201580022, 234881086, 268435519, 0, 0, 0, 0, 0, 0,
    ),
    (
        1859908, 3293736, 16777257, 3582281, 3737994, 3979755, 12244076, 50525714, 12666451, 83889690,
        117440512, 7294037, 151111097, 15424663, 14366621, 184553183, 218103863, 251658240, 33554432,
        67108864, 100663296, 134217728, 167772220, 201326653, 234881086, 268435519, 0, 0,
    ),
    (
        10381668, 1491460, 150994984, 11964809, 2026122, 184549387, 223398639, 251659597, 16777230, 50331648,
        84100054, 117442012, 8082461, 6516497, 33554450, 67212511, 100861658, 13311485, 134217784, 167772211,
        201330302, 234885114, 268435515, 0, 0, 0, 0, 0,
    ),
    (
        10381668, 10666500, 10787653, 150994990, 12364422, 184549419, 218104519, 251658240, 12796692,
        16777237, 56302925, 97059766, 14480471, 6367027, 117520285, 33554432, 15837145, 67108891, 100663296,
        134217728, 167775805, 201330302, 234884799, 268435515, 0, 0, 0, 0,
    ),
    (
        1859908, 20072968, 3578185, 50375082, 3046094, 83888911, 12159868, 117634685, 151105456, 184549376,
        218103808, 251658256, 16587867, 5713428, 33646354, 67228887, 8339038, 100663348, 134217728, 167772160,
        201330042, 234884854, 268435511, 0, 0, 0, 0, 0,
    ),
    (
        1859908, 3293736, 16777257, 3582281, 50331686, 11577835, 3071758, 12651407, 155647832, 90694833,
        184549426, 117441754, 218103808, 251658260, 7167987, 33556246, 67340119, 100663326, 134217759,
        167775545, 201330042, 234884539, 268435511, 0, 0, 0, 0, 0,
    ),
    (
        10381668, 2380292, 14723590, 11055593, 16778041, 50332523, 150997818, 13874108, 83890029, 184549376,
        218107822, 117441492, 5622837, 167772176, 4715933, 12920727, 5110774, 14624344, 201440474, 251658240,
        33554432, 67108864, 234881024, 100663296, 268435456, 134217728, 0, 0,
    ),
    (
        10381668, 1475076, 11178616, 2798009, 153078586, 196599499, 5694228, 13827981, 4515216, 4191698,
        12703507, 16995870, 14358489, 218310362, 50335219, 251658240, 83886080, 117440512, 167772160,
        33554432, 67108864, 201326592, 100663296, 134217728, 234881024, 268435456, 0, 0,
    ),
    (
        1859908, 16777992, 13779785, 50332348, 83887013, 16210315, 117440527, 16476711, 150998572, 12770815,
        167775849, 184789930, 218103808, 201428048, 5349073, 12408466, 7158955, 251658262, 242601175,
        268437470, 33554432, 67108864, 100663296, 134217728, 0, 0, 0, 0,
    ),
    (
        1859908, 16925448, 15880820, 60774797, 87777981, 151177784, 14603006, 12293135, 117634153, 195658943,
        218103808, 12688122, 251658259, 168015508, 6141333, 201326641, 33676444, 235011294, 67108864,
        100663296, 268435456, 134217728, 0, 0, 0, 0, 0, 0,
    ),
    (
        10115329, 151177767, 184552297, 218106542, 2289932, 16777229, 251658283, 52749573, 1674352, 46777359,
        2838037, 83886105, 5977927, 6913401, 117441246, 14284538, 67110011, 167775740, 201326653, 100663314,
        234881086, 268436735, 134217728, 0, 0, 0, 0, 0,
    ),
    (
        10115329, 150997800, 184720231, 229163310, 16970253, 251658283, 52752718, 83930630, 117486855,
        13720688, 5885080, 48715344, 67109981, 7959706, 100663354, 8337147, 167773436, 134217728, 201330550,
        234881086, 268439039, 0, 0, 0, 0, 0, 0, 0,
    ),
    (
        1859908, 9865473, 11430569, 28363208, 150994944, 50386441, 5456540, 184549421, 91548697, 13034229,
        218103834, 33554448, 13301659, 251659254, 117440512, 14907388, 167772211, 67182165, 201326653,
        4812730, 234881083, 100663296, 268436735, 134217751, 0, 0, 0, 0,
    ),
    (
        1859908, 10914049, 11430565, 16828872, 150997769, 50334989, 83886986, 117503499, 7443504, 184549421,
        7033969, 38463316, 218103808, 67110262, 14542255, 251658267, 100663356, 167774200, 15195283,
        201326615, 134217728, 234884798, 268648191, 0, 0, 0, 0, 0,
    ),
    (
        2380292, 10633601, 150994988, 10005349, 184552039, 229302983, 13024240, 251658252, 16777216, 53972210,
        15060240, 6349941, 83886134, 15693690, 117687250, 167772190, 33556436, 201326653, 234882302,
        268435519, 67110233, 100664730, 134219479, 0, 0, 0, 0, 0,
    ),
    (
        2380292, 162695425, 10250661, 184720202, 12772039, 218103850, 16970545, 251661042, 50388531, 97840756,
        117441488, 5465914, 4701661, 167772220, 207742333, 33554432, 234885010, 67368534, 268435482,
        100663327, 134329811, 0, 0, 0, 0, 0, 0, 0,
    ),
    (
        1859908, 2509320, 41, 16777985, 50334029, 84059018, 121696998, 151177707, 184552273, 218295348,
        13063316, 251661298, 13485430, 5848572, 167776120, 201330302, 33558168, 234881024, 268439295,
        67213143, 100664990, 134219739, 0, 0, 0, 0, 0, 0,
    ),
    (
        1859908, 150024, 16777985, 50500425, 94954149, 121418790, 162601451, 184736820, 230366546, 12529044,
        251661811, 168003132, 201561469, 15308030, 234881052, 33813947, 268437338, 67108894, 100663296,
        134346455, 0, 0, 0, 0, 0, 0, 0, 0,
    ),
    (
        10381668, 2380292, 44, 151159169, 2915146, 184549417, 29551244, 218103821, 50331648, 251661291,
        83944753, 117673103, 13866320, 6503802, 15801750, 167772219, 201578103, 234881086, 268435519, 5076626,
        33554460, 67110747, 100663326, 134217759, 0, 0, 0, 0,
    ),
    (
        10381668, 516, 11571521, 151159430, 11965127, 184549424, 16968332, 218106957, 50331648, 255523540,
        83886130, 117440527, 13700629, 15424761, 168021398, 217560631, 234885009, 268437311, 33554432,
        73258578, 100665242, 134346451, 0, 0, 0, 0, 0, 0,
    ),
    (
        1859908, 9476616, 16777985, 50331661, 3035817, 84060558, 117441551, 151177959, 184735284, 12774737,
        218105428, 251661302, 16199473, 174706168, 33554432, 5582771, 201326649, 67348351, 234881024,
        268435515, 100787603, 134346203, 0, 0, 0, 0, 0, 0,
    ),
    (
        1859908, 8, 16777985, 59822696, 87726410, 11166416, 117440527, 151177707, 198366296, 224877614,
        266017748, 7068860, 167773368, 15199731, 201326620, 33554432, 234884799, 268436859, 67229075,
        100665243, 134219735, 0, 0, 0, 0, 0, 0, 0,
    ),
    (
        9980260, 11555367, 150997513, 195482246, 12104176, 218103850, 16777228, 50535373, 89336526, 259067407,
        117440512, 13844049, 33556026, 14013589, 167997243, 217544595, 234972798, 67108864, 268435519,
        100664983, 134219487, 0, 0, 0, 0, 0, 0, 0,
    ),
    (
        9980260, 11555367, 150997513, 2019974, 197180329, 218103850, 16777228, 5422191, 251658253, 50331648,
        83889294, 117441528, 4429148, 15415156, 49092149, 167849782, 5234142, 201326614, 234881086, 268435519,
        67108889, 100664983, 134219487, 0, 0, 0, 0, 0,
    ),
    (
        1859908, 16828936, 61133412, 3713360, 83886122, 3978342, 117440555, 164809170, 184628781, 218189166,
        265903088, 14536497, 39530009, 167772160, 201563389, 251379351, 67110557, 100665243, 134217759,
        268435519, 0, 0, 0, 0, 0, 0, 0, 0,
    ),
    (
        1859908, 16828936, 61133412, 2795856, 83886094, 4518630, 117440555, 150997799, 196560402, 230767541,
        5348783, 251658289, 7572663, 33554453, 15297785, 74954391, 100665243, 167772220, 201326653, 134221727,
        234881024, 268435519, 0, 0, 0, 0, 0, 0,
    ),
    (
        10381668, 161516292, 10932805, 2810288, 184549418, 12893127, 231261483, 14889813, 4408214, 251723351,
        6510353, 16880822, 15324378, 50331703, 83886107, 117440512, 33554432, 67108864, 100663326, 134467295,
        167772221, 201326654, 234881087, 268435456, 0, 0, 0, 0,
    ),
    (
        10381668, 161516292, 10932805, 2810288, 12521962, 184549387, 3353300, 5976917, 4259086, 4675036,
        4941341, 225000921, 251658240, 16779163, 50331648, 83886080, 117440512, 33554432, 67108864, 100663296,
        134219768, 183746233, 201326653, 234881086, 268435519, 0, 0, 0,
    ),
    (
        1859908, 3180840, 16777257, 3447461, 50332710, 10400650, 4113105, 96044205, 12688372, 15947411,
        151106865, 16108693, 125253046, 184551319, 218103808, 251658271, 33554432, 67108864, 100663296,
        134217728, 182681598, 201326649, 234881082, 268435515, 0, 0, 0, 0,
    ),
    (
        1859908, 3180840, 16777257, 3447461, 50331686, 3847178, 4113127, 83888977, 12397464, 5090329,
        13219121, 5977877, 150994973, 117442455, 184549407, 218103808, 251658240, 33554432, 67108864,
        100663296, 134217728, 14146876, 14679486, 167772216, 201326649, 234881082, 268435515, 0,
    ),
    (
        10381668, 1491460, 150994984, 2648905, 184552361, 12755655, 229458735, 3759181, 4025872, 7808785,
        7962194, 23459347, 251658266, 50331675, 83886080, 117440570, 33554432, 67112700, 100663296, 134217728,
        167989107, 201326645, 249560510, 268435456, 0, 0, 0, 0,
    ),
    (
        10381668, 1491460, 150994984, 2648905, 184552361, 218276551, 16780236, 54086349, 251724757, 4576668,
        90252766, 117544915, 33554458, 67108891, 100663296, 134217728, 15146544, 15679154, 167775548,
        201330549, 251625398, 268435456, 0, 0, 0, 0, 0, 0,
    ),
    (
        1859908, 3293736, 16777257, 3582281, 3737994, 2955755, 11873039, 50334616, 90653935, 123164308,
        150994966, 184549403, 218105623, 251658269, 33554462, 67112351, 100666872, 134217728, 167972476,
        15675057, 201330547, 234881086, 268435519, 0, 0, 0, 0, 0,
    ),
    (
        1859908, 3293736, 16777257, 3582281, 50334090, 84063246, 11695051, 4909905, 117443544, 157889817,
        184549376, 218103808, 251658261, 33670555, 67110743, 100663326, 134217759, 14642548, 13093944,
        167772217, 16203442, 201326651, 234881086, 268435519, 0, 0, 0, 0,
    ),
    (
        10381668, 1491460, 150994984, 10775369, 184722094, 11471815, 218103819, 251658260, 16866380, 50331661,
        83886998, 4519376, 117517468, 7818451, 33554456, 13999646, 7206588, 67338102, 167772160, 100663358,
        134217728, 201330303, 234881082, 268435515, 0, 0, 0, 0,
    ),
    (
        10381668, 161516292, 10932805, 184593286, 11317738, 218103855, 251658252, 16778509, 50333006,
        84002191, 117442064, 33674327, 6679570, 67112019, 100791986, 134219507, 168005428, 15167349,
        201326647, 250609342, 268435456, 0, 0, 0, 0, 0, 0, 0,
    ),
    (
        1859908, 3293736, 16777257, 3582281, 50373670, 94286926, 4180747, 150994962, 12311384, 117440537,
        191622099, 218103871, 251658240, 5854932, 7554544, 33558065, 167772189, 8363166, 67108915, 100663354,
        134217728, 201330043, 234881078, 268435511, 0, 0, 0, 0,
    ),
    (
        1859908, 10783016, 16777228, 3447461, 50331686, 95318922, 133350347, 150994989, 16059288, 4912217,
        16594622, 184551188, 218105179, 251658240, 33554432, 67204950, 100663326, 134220831, 167775544,
        14102129, 201330355, 235110134, 268435456, 0, 0, 0, 0, 0,
    ),
    (
        10381668, 2380292, 1743416, 11315897, 15532538, 16237265, 12660628, 13815756, 11887445, 6110542,
        14273423, 6485917, 17004529, 150996633, 167775387, 50331648, 184549376, 83886131, 117440512,
        218103808, 251658240, 33554432, 201326592, 67108864, 100663296, 134217728, 234881024, 268435456,
    ),
    (
        10381668, 14844420, 1741381, 2069162, 32033483, 55821179, 11796413, 150996302, 83886080, 123278288,
        6215472, 7941405, 184549422, 6682131, 167975925, 218103808, 46775706, 67112435, 251658240, 201326592,
        100663296, 134217728, 234881024, 268435456, 0, 0, 0, 0,
    ),
    (
        1859908, 16777992, 9503348, 4704589, 50375093, 10282173, 83967926, 16597751, 4113784, 117440569,
        15654552, 151193000, 167772160, 13036121, 12528282, 184551127, 201329899, 218103836, 235009949,
        251658240, 268435456, 33554432, 67108864, 100663296, 134217728, 0, 0, 0,
    ),
    (
        1859908, 20138248, 10002213, 2874701, 50334158, 100201206, 134024759, 6526060, 12041874, 150997523,
        10831470, 12777109, 11364074, 7718385, 198047666, 167772160, 218103808, 251658240, 201326592,
        33554432, 67108864, 234881024, 100663296, 134217728, 268435456, 0, 0, 0,
    ),
    (
        10115329, 10910504, 150994989, 184549422, 218106520, 3475212, 38868591, 251661021, 67108885, 1142042,
        7175518, 16777759, 1543222, 50334793, 100666962, 2847154, 83887034, 134217747, 3980487, 117440571,
        167772220, 201326653, 234881086, 268435519, 0, 0, 0, 0,
    ),
    (
        10115329, 162954024, 184552361, 224414348, 16811823, 258388877, 7816197, 33752335, 50331657, 6843509,
        84009650, 1908147, 67108885, 117551864, 5895351, 100663353, 134456535, 167775996, 201326653,
        234881086, 268435519, 0, 0, 0, 0, 0, 0, 0,
    ),
    (
        1859908, 9865473, 7498409, 10343723, 12764693, 150994969, 33554448, 2299802, 184552283, 16982815,
        218106804, 62709065, 251658240, 15953110, 83956618, 67108919, 182702807, 117441679, 100663296,
        201326649, 134221715, 234881082, 268439547, 0, 0, 0, 0, 0,
    ),
    (
        1859908, 10914049, 11430565, 27051784, 150994988, 5282845, 184552557, 50332504, 33620638, 218107054,
        83889422, 2989269, 251661301, 123279311, 67110582, 14532156, 167772183, 100663314, 134456569,
        201326653, 234885051, 268435519, 0, 0, 0, 0, 0, 0,
    ),
    (
        2380292, 6, 11700481, 11966794, 150997383, 184738535, 218103850, 251661039, 12698648, 8095577,
        38061361, 16777216, 13446303, 50568461, 87774426, 74409338, 117440527, 100666838, 134221591,
        167772219, 201326653, 234881086, 268435519, 0, 0, 0, 0, 0,
    ),
    (
        2380292, 10668289, 151151013, 2653031, 184738537, 218103850, 16954159, 251658240, 3609648, 50331672,
        3742876, 83889715, 33557780, 4035765, 117562809, 72693431, 8220318, 100665084, 167772160, 134221655,
        201326592, 234885051, 268435519, 0, 0, 0, 0, 0,
    ),
    (
        1859908, 2509320, 16828993, 50334029, 88140426, 117504395, 11696849, 150994962, 184549421, 218106780,
        13751508, 251658287, 39935868, 12677118, 6155381, 67214518, 115453151, 167772215, 134221403,
        201326592, 234881082, 268435515, 0, 0, 0, 0, 0, 0,
    ),
    (
        1859908, 2568, 26252033, 50332521, 11076261, 93918091, 117440527, 162605547, 184549421, 218103854,
        251658287, 7587028, 12797309, 40050686, 13462898, 6679965, 67108887, 167772216, 100793946, 201326592,
        134217755, 234884791, 268435515, 0, 0, 0, 0, 0,
    ),
    (
        10381668, 2380292, 161508097, 10793418, 184549421, 218106794, 16777228, 50525453, 251658283, 83886094,
        12645397, 117440568, 6532694, 16088849, 46515835, 5242770, 13483162, 167774068, 67108864, 201326645,
        100666782, 234881024, 134221279, 268435456, 0, 0, 0, 0,
    ),
    (
        10381668, 20996, 10525441, 150994950, 186553005, 218278795, 16971020, 50509133, 251658240, 83886094,
        4023352, 117440560, 6268473, 4961404, 16358525, 41100543, 167775514, 201447157, 67108915, 234881078,
        100663326, 268435511, 134217759, 0, 0, 0, 0, 0,
    ),
    (
        1859908, 2568, 26264129, 50331661, 3840330, 83888784, 117502694, 6363627, 150994988, 184552749,
        232187161, 251852434, 14933814, 33556245, 15197403, 7843831, 67108923, 100787670, 134217759,
        167772208, 201326641, 234881074, 268435507, 0, 0, 0, 0, 0,
    ),
    (
        1859908, 8, 16828929, 10801764, 50483856, 2955918, 83886118, 117443279, 157467815, 184764013,
        218103854, 258559343, 7565075, 33554488, 14507867, 15298489, 67352447, 167775255, 100663326,
        201326641, 234883058, 134217728, 268435507, 0, 0, 0, 0, 0,
    ),
    (
        9980260, 11555367, 150997513, 195482246, 12772039, 218104618, 16777216, 11326767, 50331697, 251658240,
        83889294, 123175951, 7837457, 33557784, 6005918, 14400883, 67356243, 167772160, 217413623, 234881086,
        268435519, 100663322, 134217755, 0, 0, 0, 0, 0,
    ),
    (
        9980260, 11555367, 11960713, 150994954, 3082823, 184549422, 218106516, 5708748, 16777259, 251661453,
        4425102, 50331663, 83886080, 117440540, 13753971, 47687185, 14231447, 173000699, 67110519, 201326653,
        100663322, 234881086, 268435519, 134217755, 0, 0, 0, 0,
    ),
    (
        1859908, 16828936, 61133412, 3713360, 83886122, 3978342, 117440555, 151176359, 184737048, 218106771,
        12424501, 251659632, 46518070, 6909815, 167775794, 7812606, 67112953, 201326650, 234881051, 268435515,
        100663326, 134217759, 0, 0, 0, 0, 0, 0,
    ),
    (
        1859908, 16828936, 10803465, 50331664, 3844426, 84042827, 117443279, 162690578, 184737049, 218106771,
        5442906, 251658287, 5753974, 33782940, 173790968, 216366334, 67108893, 234885114, 100667102,
        268435456, 134217759, 0, 0, 0, 0, 0, 0, 0,
    ),
    (
        10381668, 161516292, 10932805, 2820998, 184549418, 13038279, 218106580, 257395852, 5979725, 13726734,
        7410682, 4961845, 15951453, 8091283, 17032957, 50335711, 83886080, 117440512, 33554432, 67108864,
        167772160, 100663296, 201326592, 234881024, 134217728, 268435456, 0, 0,
    ),
    (
        10381668, 1346308, 151179880, 12626502, 11055598, 11357295, 184549388, 14736533, 15002838, 15269136,
        7673623, 7963829, 15689340, 218103827, 16121306, 251662235, 16777279, 50331648, 83886080, 117440512,
        33554432, 167772160, 67108864, 100663296, 201326592, 134217728, 234881024, 268435456,
    ),
    (
        1859908, 3180840, 16777257, 3447461, 50334096, 10400650, 4113105, 12011026, 84076149, 12690671,
        12956982, 14886263, 7812508, 8111609, 15597434, 150995006, 117440575, 184549376, 218103808, 251658240,
        33554432, 67108864, 167772160, 100663296, 201326592, 134217728, 234881024, 268435456,
    ),
    (
        1859908, 3293736, 16777257, 11065673, 10019472, 50331691, 3979729, 83886124, 131257496, 5200793,
        165260272, 12959508, 16199189, 16369079, 15062515, 184788927, 218105851, 251658240, 167772160,
        33554432, 67108864, 201326592, 100663296, 234881024, 268435456, 134217728, 0, 0,
    ),
    (
        10381668, 1491460, 150994984, 2648905, 184740905, 12890602, 5419823, 3759245, 222246288, 16779025,
        265385810, 14898398, 14286424, 50331673, 7306906, 83886139, 117440512, 33554432, 67108864, 100663356,
        134217728, 167772160, 201326653, 234881086, 268435519, 0, 0, 0,
    ),
    (
        10381668, 1346308, 151034728, 184552006, 12771975, 13040267, 218281228, 3756914, 16777232, 13434390,
        4673116, 4838906, 6418165, 6681846, 267499191, 50331648, 83886141, 117440574, 33554495, 67108864,
        100663296, 134217728, 167772160, 201326592, 234881024, 268435456, 0, 0,
    ),
    (
        1859908, 3293736, 16777257, 3582281, 3737994, 3044459, 11873039, 5176216, 50331673, 89589396,
        124720564, 158541301, 184671667, 218234334, 251658296, 33554432, 67108864, 100663296, 134217728,
        183746233, 201326653, 234881086, 268435519, 0, 0, 0, 0, 0,
    ),
    (
        1859908, 3293736, 16777257, 11065673, 61760144, 4518795, 83888935, 129600338, 150994944, 6767855,
        12692820, 184549430, 218330481, 251751579, 33764828, 8252957, 67108921, 100663296, 134217786,
        167776059, 201326653, 234881086, 268435519, 0, 0, 0, 0, 0,
    ),
    (
        10381668, 2263812, 12081773, 150997641, 187347375, 218103808, 251658240, 5440199, 5710641, 5977101,
        16778129, 7414743, 50451700, 83886104, 7034462, 131972511, 33554432, 67108864, 100663296, 134217728,
        167775804, 201330301, 235142846, 268435515, 0, 0, 0, 0,
    ),
    (
        10381668, 161513772, 2382445, 184552110, 2821062, 218103851, 264810993, 20005939, 55104849, 87770515,
        7558103, 8087069, 117442167, 33785818, 67108891, 100663296, 134217728, 167772220, 201330553,
        235122686, 268435515, 0, 0, 0, 0, 0, 0, 0,
    ),
    (
        1859908, 10783016, 4246181, 4633190, 11782605, 3920530, 16777261, 66912139, 151184915, 83886080,
        184549376, 117440512, 218187375, 251856218, 7435675, 33554481, 13495453, 67108895, 100663296,
        134217728, 167775544, 201330041, 235126202, 268435511, 0, 0, 0, 0,
    ),
    (
        1859908, 2267432, 16778021, 4233642, 15891149, 50391818, 11842685, 4910991, 150996500, 5586927,
        90113433, 184549402, 117440512, 218105585, 251658290, 33556275, 67110772, 100663326, 134217759,
        167772216, 201330293, 235106042, 268435511, 0, 0, 0, 0, 0,
    ),
    (
        10381668, 10715652, 15706745, 2607749, 2649963, 16547756, 150994955, 16778004, 50332501, 83944470,
        11859409, 117442322, 184648925, 12773273, 7292890, 33774577, 67108864, 218107314, 100666615,
        167772160, 134217728, 251658240, 201326592, 234881024, 268435456, 0, 0, 0,
    ),
    (
        10381668, 10522116, 1550969, 11516553, 16035590, 16544830, 3228369, 16780332, 150995797, 50390166,
        83949037, 5098776, 12180569, 184549402, 12447067, 14626207, 117440563, 167772160, 33554432, 67108864,
        218103808, 201326592, 100663296, 251658240, 134217728, 234881024, 268435456, 0,
    ),
    (
        1859908, 20073736, 16146229, 4423606, 2619793, 15105554, 2861581, 3067598, 50331663, 83886104,
        150996589, 117440512, 5352339, 191716329, 225617366, 33557533, 8305758, 67108914, 167772211,
        100663296, 201326592, 251658240, 134217728, 234881024, 268435456, 0, 0, 0,
    ),
    (
        1859908, 3293748, 16780668, 10186597, 16309705, 50331687, 14987256, 99421838, 4764945, 10550037,
        117442067, 150994944, 5876313, 184549421, 167775259, 11199964, 33554461, 230550257, 67112095,
        201326592, 100663347, 251658240, 134217728, 234881024, 268435456, 0, 0, 0,
    ),
)


def kernel(
    n_grp,
    n_blk,
    image_hbm,
    text_hbm,
    image_ids,
    text_ids,
    sharpness,
    offset,
    adjoint,
    grad_image,
    grad_text,
    raw,
    hat,
    buf,
    ids,
    own_ids,
    inverse,
    total,
    load_sem,
    send_sem,
    id_send_sem,
    wrap_sem,
    wrap_id_sem,
    detour_sem,
    ready_sem,
    recv_sem,
    id_recv_sem,
):
    rows = hat.shape[1]
    piece = rows // WAVES
    g = lax.axis_index("grp")
    k = lax.axis_index("blk")
    j = lax.rem(k, RUN)

    loads = [
        pltpu.make_async_copy(text_hbm, raw.at[0], load_sem.at[0]),
        pltpu.make_async_copy(image_hbm, raw.at[1], load_sem.at[1]),
    ]
    for load in loads:
        load.start()

    def device(dg, dk):
        return (lax.rem(g + dg + n_grp, n_grp), lax.rem(k + dk + n_blk, n_blk))

    next_grp = [device(step, 0)[0] for step in (1, -1)]
    next_blk = [device(0, step)[1] for step in (1, -1)]

    barrier = pltpu.get_barrier_semaphore()

    def greet(target):
        pl.semaphore_signal(barrier, inc=1, device_id=target, device_id_type=MESH)

    for target in (device(0, -1), device(1, 0), device(-1, 0)):
        greet(target)

    @pl.when(j != RUN - 1)
    def _():
        greet(device(0, 1))

    even = lax.rem(j, 2) == 0

    @pl.when(even & (j >= 2))
    def _():
        greet(device(0, -2))

    @pl.when(jnp.logical_not(even) & (j <= RUN - 3))
    def _():
        greet(device(0, 2))

    def wrap_target(stream, owner, sender):
        step = 1 - 2 * stream
        return (0 if owner < SPAN else step, step * sender)

    def wrap_links(stream):
        links = [(distance, distance) for distance in range(1, SLOTS - 1)]
        links += [(owner, sender) for which, owner, sender, _, _ in DETOURS if which == stream]
        return sorted({(wrap_target(stream, *link), link[1]) for link in links})

    def others(stream):
        return [link for link in wrap_links(stream) if link[0] != (0, 1 - 2 * stream)]

    @pl.when(j == 0)
    def _():
        for (dg, dk), _ in others(0):
            greet(device(-dg, -dk))

    far_sends = sum([(RUN - j == sender).astype(jnp.int32) for _, sender in others(0)])
    far_sends += jnp.where(j == RUN - 1, len(others(1)), 0) - jnp.where(j == 0, 1, 0)
    ready_count = sum([(j + 1 == sender).astype(jnp.int32) for _, sender in wrap_links(1)])
    for (dg, dk), sender in others(1):

        @pl.when(j + 1 == sender)
        def _():
            greet(device(dg, dk))

    def wrap_distance(stream):
        to_edge = RUN - j if stream == 0 else j + 1
        return to_edge, (to_edge >= 2) & (to_edge <= 6)

    skips = jnp.where(even, j != RUN - 2, j != 1).astype(jnp.int32)
    barrier_count = 4 + skips + far_sends

    @pl.when(j == RUN - 1)
    def _():
        pl.semaphore_wait(barrier, barrier_count)
        for (dg, dk), _ in wrap_links(1):
            pl.semaphore_signal(
                ready_sem, inc=1, device_id=device(-dg, -dk), device_id_type=MESH
            )

    for stream, own in ((0, text_ids), (1, image_ids)):
        loads[stream].wait()
        for c in range(WAVES):
            part = pl.ds(c * piece, piece)
            wide = raw[stream, part, :].astype(jnp.float32)
            inv = lax.rsqrt(jnp.sum(wide * wide, axis=-1, keepdims=True) + EPSILON)
            inverse[stream, part, :] = jnp.broadcast_to(inv, (piece, 128))
            unit = (wide * inv).astype(jnp.bfloat16)
            hat[stream, part, :] = unit
            buf[stream, c, pl.ds(0, piece), :] = unit
            at = c * piece
            line = own[at // 128 : at // 128 + 1, :].astype(jnp.float32)
            line = line[:, at % 128 : at % 128 + piece]
            ids[stream, 0, c] = jnp.concatenate([line] * (128 // piece), axis=1)

    @pl.when(j != RUN - 1)
    def _():
        pl.semaphore_wait(barrier, barrier_count)

    def pick(stream, pair):
        return pair[stream] if isinstance(stream, int) else jnp.where(stream == 0, pair[0], pair[1])

    def route(stream, s, reach):
        place = pick(stream, (j, RUN - 1 - j))
        entry = lax.rem(place, 2) == 0
        fresh = (s == 0) | (s == SPAN)
        if reach == 2:
            goes = entry & (place != RUN - 2) & (fresh | (s == 1) | (s == SPAN + 1))
            return (g, pick(stream, [device(0, step)[1] for step in (2, -2)])), goes
        hop = s == SPAN - 1
        target = (
            jnp.where(hop, pick(stream, next_grp), g),
            jnp.where(hop, k, pick(stream, next_blk)),
        )
        goes = jnp.where(place == RUN - 1, s == 0, entry | fresh)
        return target, (s < SLOTS - 1) & (hop | goes)

    def chunk(stream, s, c):
        at = s * piece
        if not isinstance(at, int):
            at = pl.multiple_of(at, piece)
        return buf.at[stream, c, pl.ds(at, piece)]

    def remote(src, dst, send, recv, target):
        return pltpu.make_async_remote_copy(
            src_ref=src,
            dst_ref=dst,
            send_sem=send,
            recv_sem=recv,
            device_id=target,
            device_id_type=MESH,
        )

    def block_copy(stream, s, c, reach, target):
        return remote(
            chunk(stream, s, c),
            chunk(stream, s + reach, c),
            send_sem.at[reach - 1, stream, s],
            recv_sem.at[stream, s + reach, c],
            target,
        )

    def id_copy(stream, s, reach, target):
        return remote(
            ids.at[stream, s],
            ids.at[stream, s + reach],
            id_send_sem.at[reach - 1, stream, s],
            id_recv_sem.at[stream, s + reach],
            target,
        )

    def forward(stream, s, c):
        for reach in (2, 1):
            target, goes = route(stream, s, reach)

            @pl.when(goes)
            def _():
                @pl.when(c == 0)
                def _():
                    id_copy(stream, s, reach, target).start()

                block_copy(stream, s, c, reach, target).start()

    def receive(stream, s, c):
        target = (g, pick(stream, next_blk))

        @pl.when(c == 0)
        def _():
            id_copy(stream, s - 1, 1, target).wait_recv()

        block_copy(stream, s - 1, c, 1, target).wait_recv()

    def wrap_route(stream):
        to_edge, far = wrap_distance(stream)
        same = to_edge < SPAN
        slot = jnp.where(same, to_edge, to_edge + 1)
        step = 1 - 2 * stream
        return far, slot, device(jnp.where(same, 0, step), step * to_edge)

    def wrap_id_copy(stream):
        _, slot, target = wrap_route(stream)
        return remote(
            ids.at[stream, 0],
            ids.at[stream, slot],
            wrap_id_sem.at[stream],
            id_recv_sem.at[stream, slot],
            target,
        )

    def wrap(stream, c, far):
        _, slot, target = wrap_route(stream)

        @pl.when(far)
        def _():
            remote(
                chunk(stream, 0, c),
                chunk(stream, slot, c),
                wrap_sem.at[stream],
                recv_sem.at[stream, slot, c],
                target,
            ).start()

    def wrap_early(stream):
        to_edge, far = wrap_distance(stream)

        @pl.when(far)
        def _():
            wrap_id_copy(stream).start()

        for c in range(WAVES):
            now = far & (to_edge < PATIENT[stream])
            for which, owner, _, _, waves in DETOURS:
                if which == stream and c in waves:
                    now = now & (to_edge != owner)
            wrap(stream, c, now)

    def wrap_late(other, s, c):
        for stream in range(2):
            to_edge, far = wrap_distance(stream)
            now = far & (to_edge >= PATIENT[stream]) & (other == 1 - stream) & (s == SPAN - 1)
            for which, owner, _, _, waves in DETOURS:
                if which == stream:
                    kept = functools.reduce(jnp.logical_and, [c != wave for wave in waves])
                    now = now & ((to_edge != owner) | kept)
            wrap(stream, c, now)

    def detour_copy(n, c):
        stream, owner, sender, s, _ = DETOURS[n]
        slot = owner if owner < SPAN else owner + 1
        return remote(
            chunk(stream, s, c),
            chunk(stream, slot, c),
            detour_sem.at[n],
            recv_sem.at[stream, slot, c],
            device(*wrap_target(stream, owner, sender)),
        )

    def detour(stream, s, c):
        for n, (which, _, sender, slot, waves) in enumerate(DETOURS):
            place = RUN - sender if which == 0 else sender - 1
            now = functools.reduce(jnp.logical_or, [c == wave for wave in waves])

            @pl.when((stream == which) & (s == slot) & (j == place) & now)
            def _():
                detour_copy(n, c).start()

    for c in range(WAVES):
        forward(0, 0, c)

        @pl.when(j != 0)
        def _():
            forward(1, 0, c)

    wrap_early(0)

    def cross():
        pl.semaphore_wait(ready_sem, ready_count)
        for c in range(WAVES):

            @pl.when(j == 0)
            def _():
                forward(1, 0, c)

        wrap_early(1)

    row = lax.broadcasted_iota(jnp.int32, (128, 128), 0)
    lane = lax.broadcasted_iota(jnp.int32, (128, 128), 1)
    for stream, own in ((0, text_ids), (1, image_ids)):
        for half in range(rows // 128):
            line = jnp.broadcast_to(own[half : half + 1, :].astype(jnp.float32), (128, 128))
            column = jnp.sum(jnp.where(row == lane, line, 0.0), axis=-1, keepdims=True)
            own_ids[stream, pl.ds(half * 128, 128), :] = jnp.broadcast_to(column, (128, 128))
        total[stream] = jnp.zeros(total.shape[1:], jnp.float32)

    scale = jnp.exp(jnp.full((1, 128), sharpness[0], jnp.float32))[:, :1]
    shift = offset[0]
    weight = -(adjoint[0] * scale / rows)
    group = SPAN * piece
    turn = lax.broadcasted_iota(jnp.int32, (1, 128), 1) // piece

    def compute(stream, c, half):
        mine = 1 - stream
        visitors = buf[stream, c, pl.ds(pl.multiple_of(half * group, group), group), :]
        grid = lax.dot_general(
            hat[mine], visitors, (((1,), (1,)), ((), ())), preferred_element_type=jnp.float32
        )
        logit = scale * grid + shift
        column = own_ids[mine, :, :]
        parts = []
        for at in range(0, group, 128):
            s = half * SPAN + at // piece
            line = ids[stream, s, c]
            for other in range(1, 128 // piece):
                line = jnp.where(turn == other, ids[stream, s + other, c], line)
            match = column == jnp.broadcast_to(line, (rows, 128))
            here = logit[:, at : at + 128]
            signed = jnp.where(match, here, -here)
            parts.append(jnp.where(match, weight, -weight) * (1.0 / (1.0 + jnp.exp(signed))))
        coef = jnp.concatenate(parts, axis=1).astype(jnp.bfloat16)
        total[mine] += jnp.dot(coef, visitors, preferred_element_type=jnp.float32)

    words = []
    line = lax.rem(g, LINE)
    turn_at = 2 * j + lax.div(k, RUN)
    for i in range(len(ORDER[0])):
        word = jnp.int32(0)
        for row in reversed(range(LINE)):
            entries = [ORDER[row * 2 * RUN + place][i] for place in range(2 * RUN)]
            entry = jnp.int32(entries[0])
            for place in range(1, 2 * RUN):
                if entries[place] != entries[place - 1]:
                    entry = jnp.where(turn_at >= place, entries[place], entry)
            word = entry if row == LINE - 1 else jnp.where(line == row, entry, word)
        words.append(word)

    def step(i, carry):
        word = words[0]
        for other in range(1, len(words)):
            word = jnp.where(i == other, words[other], word)

        @pl.when(lax.rem(word, 64) == 1)
        def _():
            cross()

        for _ in range(4):
            entry = lax.rem(word, 64)
            word = lax.div(word, 64)
            stream = lax.div(entry, 32)
            s = lax.rem(lax.div(entry, 4), 8)
            c = lax.rem(entry, 4)

            @pl.when(entry > 1)
            def _():
                receive(stream, s, c)
                forward(stream, s, c)
                wrap_late(stream, s, c)
                detour(stream, s, c)

        @pl.when(word > 0)
        def _():
            product = word - 1
            compute(lax.div(product, 8), lax.div(lax.rem(product, 8), 2), lax.rem(product, 2))

        return carry

    lax.fori_loop(0, len(words), step, 0)

    for stream, out in ((1, grad_image), (0, grad_text)):
        for c in range(WAVES):
            part = pl.ds(c * piece, piece)
            inv = inverse[stream, part, :][:, :1]
            unit = raw[stream, part, :].astype(jnp.float32) * inv
            grad = total[stream, part, :]
            along = jnp.sum(unit * grad, axis=-1, keepdims=True)
            out[part, :] = inv * (grad - unit * along)

    for stream in range(2):
        for s in range(SLOTS - 1):
            for reach in (2, 1):
                target, goes = route(stream, s, reach)

                @pl.when(goes)
                def _():
                    id_copy(stream, s, reach, target).wait_send()
                    remote(
                        hat.at[stream],
                        hat.at[stream],
                        send_sem.at[reach - 1, stream, s],
                        recv_sem.at[stream, s + 1, 0],
                        target,
                    ).wait_send()

        far, slot, target = wrap_route(stream)

        @pl.when(far)
        def _():
            wrap_id_copy(stream).wait_send()

        for distance in range(2, SLOTS - 1):
            away = [len(d[4]) for d in DETOURS if d[0] == stream and d[1] == distance]
            amount = rows - piece * sum(away)
            if amount:

                @pl.when(wrap_distance(stream)[0] == distance)
                def _():
                    part = hat.at[stream, pl.ds(0, amount)]
                    remote(
                        part, part, wrap_sem.at[stream], recv_sem.at[stream, slot, 0], target
                    ).wait_send()

    for n, (stream, _, sender, _, waves) in enumerate(DETOURS):

        @pl.when(j == (RUN - sender if stream == 0 else sender - 1))
        def _():
            part = hat.at[stream, pl.ds(0, piece * len(waves))]
            target = device(0, 1 - 2 * stream)
            remote(
                part, part, detour_sem.at[n], recv_sem.at[stream, 1, 0], target
            ).wait_send()


def body(n_grp, n_blk, image_emb, text_emb, image_pair_index, text_ids, sharpness, offset, adjoint):
    rows, width = image_emb.shape
    vmem = pl.BlockSpec(memory_space=pltpu.VMEM)
    smem = pl.BlockSpec(memory_space=pltpu.SMEM)
    hbm = pl.BlockSpec(memory_space=pltpu.HBM)
    flops = 4 * SLOTS * 2 * rows * rows * width
    return pl.pallas_call(
        functools.partial(kernel, n_grp, n_blk),
        out_shape=(
            jax.ShapeDtypeStruct((rows, width), jnp.float32),
            jax.ShapeDtypeStruct((rows, width), jnp.float32),
        ),
        in_specs=[hbm, hbm, vmem, vmem, smem, smem, smem],
        out_specs=(vmem, vmem),
        scratch_shapes=[
            pltpu.VMEM((2, rows, width), jnp.bfloat16),
            pltpu.VMEM((2, rows, width), jnp.bfloat16),
            pltpu.VMEM((2, WAVES, SLOTS * rows // WAVES, width), jnp.bfloat16),
            pltpu.VMEM((2, SLOTS, WAVES, 1, 128), jnp.float32),
            pltpu.VMEM((2, rows, 128), jnp.float32),
            pltpu.VMEM((2, rows, 128), jnp.float32),
            pltpu.VMEM((2, rows, width), jnp.float32),
            pltpu.SemaphoreType.DMA((2,)),
            pltpu.SemaphoreType.DMA((2, 2, SLOTS)),
            pltpu.SemaphoreType.DMA((2, 2, SLOTS)),
            pltpu.SemaphoreType.DMA((2,)),
            pltpu.SemaphoreType.DMA((2,)),
            pltpu.SemaphoreType.DMA((max(1, len(DETOURS)),)),
            pltpu.SemaphoreType.REGULAR,
            pltpu.SemaphoreType.DMA((2, SLOTS, WAVES)),
            pltpu.SemaphoreType.DMA((2, SLOTS)),
        ],
        compiler_params=pltpu.CompilerParams(
            collective_id=0, has_side_effects=True, vmem_limit_bytes=60 * 1024 * 1024
        ),
        cost_estimate=pl.CostEstimate(
            flops=flops, bytes_accessed=12 * rows * width, transcendentals=2 * SLOTS * rows * rows
        ),
    )(
        image_emb,
        text_emb,
        image_pair_index.reshape(rows // 128, 128),
        text_ids.reshape(rows // 128, 128),
        sharpness,
        offset,
        adjoint,
    )


def solution(mesh):
    both = ("grp", "blk")
    return jax.shard_map(
        functools.partial(body, mesh.shape["grp"], mesh.shape["blk"]),
        mesh=mesh,
        in_specs=(P(both, None), P(both, None), P(both), P(both), P(), P(), P()),
        out_specs=(P(both, None), P(both, None)),
        check_vma=False,
    )
```
